32 devices in a mesh: filter: 8 (over z, x), space: 4 (over y, core).
Axes of the slice: x: 2, y: 2, z: 4, core: 2. Of those that a mesh axis runs over, the one named last changes fastest.
Arguments:
- volume: bfloat16 [1024, 16, 1024], P('filter', 'space'), may hold values from -6 to 6
- mixing: bfloat16 [1024, 1024], P('filter'), may hold values from -0.1875 to 0.1875
- kernel_taps: float32 [1024, 27], P('filter'), may hold values from -1.25 to 1.25
- upstream: bfloat16 [1024, 16, 1024], P('filter', 'space'), may hold values from -6 to 6
Outputs:
- output: bfloat16 [1024, 16, 1024], P('filter', 'space')
- volume_grad: bfloat16 [1024, 16, 1024], P('filter', 'space')
- mixing_grad: float32 [1024, 1024], P('filter', 'space')
- taps_grad: float32 [1024, 27], P('filter')
The draws below stay inside these ranges and needn't reach their ends.
All inputs are finite; a program needn't handle non-finite values.
Results may differ from the reference program's by a relative error of at most 0.0055.
Values may be sent and summed in bfloat16 or wider, within the bound.
No kernel may reach another device: no remote copies, remote signals or barrier semaphores. Data moves between devices by JAX's collectives and lax.ppermute only.
A program may use at most 64 MiB of HBM per device.

```python
import math
import jax
import jax.numpy as jnp
from jax import lax

C = 1024
HH = 16
WW = 64
D = 16
HW = 1024


def with_spikes(values, key, source, target, parts, factor):
    def block_of(position):
        return (jnp.arange(values.shape[position]) // (values.shape[position] // parts)).reshape((-1,) + (1,) * (values.ndim - 1 - position))

    near = jax.random.permutation(key, parts)[block_of(target)]
    other_side = (block_of(target) + parts // 2) % parts
    return jnp.where((block_of(source) == near) | (block_of(source) == other_side), factor * values, values)


def block_scale(rng, shape, shards, low, top_value):
    def one(dim, shards_of):
        steps = jax.random.uniform(jax.random.fold_in(jax.random.fold_in(rng, 6), dim), (shards_of,), jnp.float32, low / len(shards), top_value / len(shards))
        return jnp.repeat(jnp.exp(steps), shape[dim] // shards_of).reshape((-1,) + (1,) * (len(shape) - dim - 1))

    loudness = one(*shards[0])
    for cut in shards[1:]:
        loudness = loudness * one(*cut)
    return loudness


def scatter_about(rng, dims, spread, bound, shards=(), kind=jnp.bfloat16):
    drawn = spread * jax.random.normal(rng, dims, jnp.float32)
    if shards:
        drawn = drawn * block_scale(rng, dims, shards, -0.22, 0.18)
    return jnp.clip(drawn, -bound, bound).astype(kind)


def heavy_noise(key, shape, deviation, bound, shards, heavy, held_as=jnp.bfloat16):
    values = deviation * jax.random.normal(key, shape, jnp.float32)
    if shards:
        values = values * block_scale(key, shape, shards, -0.22, 0.18)
    return jnp.clip(with_spikes(values, jax.random.fold_in(key, 3), *heavy), -bound, bound).astype(held_as)


def setup_inputs(seed: int = 0) -> dict:
    key_list = jax.random.split(jax.random.key(seed), 5)
    return {
        "volume": heavy_noise(key_list[0], (C, D, HW), 1.0, 6.0, ((0, 8), (1, 4)), (1, 0, 8, 2.0)),
        "mixing": scatter_about(key_list[1], (C, C), C ** -0.5, 0.1875, ((0, 8),)),
        "kernel_taps": scatter_about(key_list[2], (C, 27), 27 ** -0.5, 1.25, ((0, 8),), jnp.float32),
        "upstream": scatter_about(key_list[3], (C, D, HW), 1.0, 6.0, ((0, 8), (1, 4))),
    }


def pad_sides(field):
    return jnp.pad(field, ((0, 0), (1, 1), (1, 1), (1, 1)))

def depth_conv(padded, kernel_taps, flip):
    depth = padded.shape[1] - 2
    height = padded.shape[2] - 2
    breadth = padded.shape[3] - 2
    summed = jnp.zeros((padded.shape[0], depth, height, breadth), jnp.float32)
    for plane_off in range(3):
        for row_off in range(3):
            for col_off in range(3):
                index_tap = plane_off * 9 + row_off * 3 + col_off
                if flip:
                    plane_at, row_at, col_at = (2 - plane_off, 2 - row_off, 2 - col_off)
                else:
                    plane_at, row_at, col_at = (plane_off, row_off, col_off)
                window = padded[:, plane_at:plane_at + depth, row_at:row_at + height, col_at:col_at + breadth]
                summed = summed + kernel_taps[:, index_tap][:, None, None, None] * window.astype(jnp.float32)
    return summed

def tap_grads(grad_field, padded):
    depth = grad_field.shape[1]
    height = grad_field.shape[2]
    breadth = grad_field.shape[3]
    grad_wide = grad_field.astype(jnp.float32)
    columns_list = []
    for plane_off in range(3):
        for row_off in range(3):
            for col_off in range(3):
                window = padded[:, plane_off:plane_off + depth, row_off:row_off + height, col_off:col_off + breadth]
                columns_list.append(lax.optimization_barrier(jnp.sum(grad_wide * window.astype(jnp.float32), axis=(1, 2, 3))))
    return jnp.stack(columns_list, axis=1)

def silu_slope(values):
    sig_val = jax.nn.sigmoid(values)
    return sig_val * (1.0 + values * (1.0 - sig_val))

def reference(volume, mixing, kernel_taps, upstream):
    channels = volume.shape[0]
    flat_vol = volume.reshape(channels, D * HW)
    mixed = jnp.dot(mixing, flat_vol, preferred_element_type=jnp.float32).astype(jnp.bfloat16)
    mixed_pad = pad_sides(mixed.reshape(channels, D, HH, WW))
    spatial = depth_conv(mixed_pad, kernel_taps, False)
    vol_grid = volume.reshape(channels, D, HH, WW).astype(jnp.float32)
    output = (vol_grid + jax.nn.silu(spatial)).astype(jnp.bfloat16).reshape(channels, D, HW)
    up_grid = upstream.reshape(channels, D, HH, WW).astype(jnp.float32)
    spatial_grad = (up_grid * silu_slope(spatial)).astype(jnp.bfloat16)
    mixed_grad = depth_conv(pad_sides(spatial_grad), kernel_taps, True).astype(jnp.bfloat16).reshape(channels, D * HW)
    norm_factor = 1.0 / math.sqrt(D * HH * WW)
    back_sum = jnp.dot(mixing.T, mixed_grad, preferred_element_type=jnp.float32)
    volume_grad = (upstream.reshape(channels, D * HW).astype(jnp.float32) + back_sum).astype(jnp.bfloat16).reshape(channels, D, HW)
    mixing_grad = jnp.dot(mixed_grad, flat_vol.T, preferred_element_type=jnp.float32) * norm_factor
    taps_grad = tap_grads(spatial_grad, mixed_pad) * norm_factor
    return (output, volume_grad, mixing_grad, taps_grad)
```

```python
import math

import jax
import jax.numpy as jnp
from jax import lax
from jax.sharding import PartitionSpec as P

WW = 64


def swap(block, axis, step):
    size = lax.axis_size(axis)
    return lax.ppermute(block, axis, [(i, i ^ step) for i in range(size)])


def exchange(pieces, axis):
    return [pieces[0]] + [swap(pieces[s], axis, s) for s in range(1, len(pieces))]


def place(pieces, me):
    out = jnp.zeros((len(pieces),) + pieces[0].shape, pieces[0].dtype)
    for s, piece in enumerate(pieces):
        out = lax.dynamic_update_index_in_dim(out, piece, me ^ s, 0)
    return out


def gather_weights(mixing, me_space):
    rows, cols = mixing.shape
    nf, ns = lax.axis_size("filter"), lax.axis_size("space")
    share = cols // ns
    own = lax.dynamic_slice_in_dim(mixing, me_space * share, share, axis=1)
    even = jnp.stack([own] + [swap(own, "filter", s) for s in range(2, nf, 2)])
    odd = swap(even, "filter", 1)
    part = jnp.stack([even, odd], axis=1).reshape(nf, rows, share)
    if ns == 1:
        return part
    held = jnp.stack([part] + [swap(part, "space", s) for s in range(2, ns, 2)])
    other = swap(held, "space", 1)
    both = jnp.stack([held, other], axis=1).reshape(ns, nf * rows, share)
    full = place([both[s] for s in range(ns)], me_space)
    return full.transpose(1, 0, 2).reshape(nf * rows, cols)


def scatter_weight_sum(part, rows, me, me_space):
    nf, ns = lax.axis_size("filter"), lax.axis_size("space")
    cols = part.shape[1]
    share = cols // ns
    bit = me_space & 1
    split = part.reshape(nf * rows, ns // 2, 2, share)
    mine = lax.dynamic_index_in_dim(split, bit, 2, keepdims=False)
    theirs = lax.dynamic_index_in_dim(split, bit ^ 1, 2, keepdims=False)
    half = mine + swap(theirs, "space", 1)
    total = lax.dynamic_index_in_dim(half, me_space >> 1, 1, keepdims=False)
    for s in range(2, ns, 2):
        out = lax.dynamic_index_in_dim(half, (me_space ^ s) >> 1, 1, keepdims=False)
        total = total + swap(out.astype(jnp.bfloat16), "space", s).astype(jnp.float32)
    total = total.reshape(nf // 2, 2, rows, share)
    near = total[:, 0] + swap(total[:, 1].astype(jnp.bfloat16), "filter", 1).astype(jnp.float32)
    result = near[0]
    for s in range(2, nf, 2):
        result = result + swap(near[s // 2].astype(jnp.bfloat16), "filter", s).astype(jnp.float32)
    return result


def with_planes(field):
    size = lax.axis_size("space")
    up = [(i, i + 1) for i in range(size - 1)]
    down = [(i + 1, i) for i in range(size - 1)]
    before = lax.ppermute(field[-1:], "space", up)
    after = lax.ppermute(field[:1], "space", down)
    return jnp.concatenate([before, field, after], axis=0)


def pad_rows_cols(field):
    return jnp.pad(field, ((0, 0), (1, 1), (1, 1), (0, 0)))


def depth_conv(padded, taps, flip):
    depth, height, width = padded.shape[0] - 2, padded.shape[1] - 2, padded.shape[2] - 2
    summed = jnp.zeros((depth, height, width, padded.shape[3]), jnp.float32)
    for a in range(3):
        for b in range(3):
            for e in range(3):
                i, j, k = (2 - a, 2 - b, 2 - e) if flip else (a, b, e)
                window = padded[i : i + depth, j : j + height, k : k + width]
                summed = summed + taps[a * 9 + b * 3 + e] * window.astype(jnp.float32)
    return summed


def tap_grads(grad, padded):
    depth, height, width = grad.shape[:3]
    wide = grad.astype(jnp.float32)
    columns = []
    for a in range(3):
        for b in range(3):
            for e in range(3):
                window = padded[a : a + depth, b : b + height, e : e + width]
                columns.append(jnp.sum(wide * window.astype(jnp.float32), axis=(0, 1, 2)))
    return jnp.stack(columns, axis=1)


def body(volume, mixing, kernel_taps, upstream):
    ch, planes, flat = volume.shape
    rows = flat // WW
    cells = planes * flat
    nf, ns = lax.axis_size("filter"), lax.axis_size("space")
    me, me_space = lax.axis_index("filter"), lax.axis_index("space")
    blk = cells // nf
    norm = 1.0 / math.sqrt(planes * ns * flat)

    vol_blocks = volume.reshape(ch, nf, blk)
    send = [lax.dynamic_index_in_dim(vol_blocks, me ^ s, 1, keepdims=False) for s in range(nf)]
    vol_all = place(exchange(send, "filter"), me).reshape(nf * ch, blk)
    weights = gather_weights(mixing, me_space)

    mixed_t = lax.dot_general(
        vol_all, weights, (((0,), (1,)), ((), ())), preferred_element_type=jnp.float32
    ).astype(jnp.bfloat16)
    send = [mixed_t[:, s * ch : (s + 1) * ch] for s in range(nf)]
    mixed = place(exchange(send, "filter"), me).reshape(planes, rows, WW, ch)

    taps = kernel_taps.T
    mixed_pad = pad_rows_cols(with_planes(mixed))
    spatial = depth_conv(mixed_pad, taps, False)
    sig = jax.nn.sigmoid(spatial)
    up_t = upstream.reshape(ch, cells).T.reshape(planes, rows, WW, ch)
    grad = (up_t.astype(jnp.float32) * (sig * (1.0 + spatial * (1.0 - sig)))).astype(jnp.bfloat16)
    silu_t = spatial * sig
    grad_wide = with_planes(grad)
    mixed_grad = depth_conv(pad_rows_cols(grad_wide), taps, True).astype(jnp.bfloat16)
    mixed_grad = mixed_grad.reshape(nf, blk, ch)

    send = [lax.dynamic_index_in_dim(mixed_grad, me ^ s, 0, keepdims=False) for s in range(nf)]
    mg_all = jnp.stack(exchange(send, "filter"))
    back = lax.dot_general(
        weights.reshape(nf, ch, nf * ch),
        mg_all,
        (((0, 1), (0, 2)), ((), ())),
        preferred_element_type=jnp.float32,
    ).astype(jnp.bfloat16)
    back = back.reshape(nf, ch, blk)
    send = [lax.dynamic_index_in_dim(back, me ^ s, 0, keepdims=False) for s in range(nf)]
    back_own = place(exchange(send, "filter"), me).transpose(1, 0, 2).reshape(ch, planes, flat)
    volume_grad = (upstream.astype(jnp.float32) + back_own.astype(jnp.float32)).astype(jnp.bfloat16)

    weight_part = lax.dot_general(
        mg_all, vol_all, (((1,), (1,)), ((), ())), preferred_element_type=jnp.float32
    )
    weight_part = weight_part.reshape(nf * ch, nf * ch) * norm
    mixing_grad = scatter_weight_sum(weight_part, ch, me, me_space)

    output = volume.astype(jnp.float32) + silu_t.reshape(cells, ch).T.reshape(ch, planes, flat)
    output = output.astype(jnp.bfloat16)
    taps_sum = tap_grads(grad, mixed_pad) * norm
    step = 1
    while step < ns:
        taps_sum = taps_sum + swap(taps_sum, "space", step)
        step *= 2
    return (output, volume_grad, mixing_grad, taps_sum)


def solution(mesh):
    in_specs = (
        P("filter", "space", None),
        P("filter", None),
        P("filter", None),
        P("filter", "space", None),
    )
    out_specs = (
        P("filter", "space", None),
        P("filter", "space", None),
        P("filter", "space"),
        P("filter", None),
    )
    return jax.shard_map(body, mesh=mesh, in_specs=in_specs, out_specs=out_specs, check_vma=False)
```

```python
import functools
import math

import jax
import jax.numpy as jnp
from jax import lax
from jax.experimental import pallas as pl
from jax.experimental.pallas import tpu as pltpu
from jax.sharding import PartitionSpec as P

WW = 64
BF = jnp.bfloat16
F32 = jnp.float32


def swap(block, axis, step):
    size = lax.axis_size(axis)
    return lax.ppermute(block, axis, [(i, i ^ step) for i in range(size)])


def exchange(pieces, axis):
    size = len(pieces)
    order = list(range(size // 2, size)) + list(range(1, size // 2))
    got = {0: pieces[0]}
    for s in order:
        got[s] = swap(pieces[s], axis, s)
    return [got[s] for s in range(size)]


def place(pieces, shift):
    out = jnp.zeros((len(pieces),) + pieces[0].shape, pieces[0].dtype)
    for s, piece in enumerate(pieces):
        out = lax.dynamic_update_index_in_dim(out, piece, shift ^ s, 0)
    return out


def restrip(part, count, strips):
    n, cells, ch = part.shape[0], part.shape[1] // count, part.shape[2]
    if n == strips:
        return part
    part = part.reshape(n, count, cells, ch).transpose(1, 0, 2, 3)
    part = part.reshape(count, strips, n * cells // strips, ch).transpose(1, 0, 2, 3)
    return part.reshape(strips, count * n * cells // strips, ch)


def pick(blocks, index):
    return lax.dynamic_index_in_dim(blocks, index, 0, keepdims=False)


def gather_weights(mixing, me_space):
    rows, cols = mixing.shape
    nf, ns = lax.axis_size("filter"), lax.axis_size("space")
    share = cols // ns
    own = lax.dynamic_slice_in_dim(mixing, me_space * share, share, axis=1)
    even = jnp.stack([own] + [swap(own, "filter", s) for s in range(2, nf, 2)])
    odd = swap(even, "filter", 1)
    part = jnp.stack([even, odd], axis=1).reshape(nf * rows, share)
    held = jnp.stack([part] + [swap(part, "space", s) for s in range(2, ns, 2)])
    other = swap(held, "space", 1)
    return jnp.stack([held, other], axis=1).reshape(ns, nf * rows, share)


def scatter_weight_sum(part, rows):
    nf, ns = lax.axis_size("filter"), lax.axis_size("space")
    share = part.shape[1] // ns
    split = [part[:, v * share : (v + 1) * share] for v in range(ns)]
    theirs = jnp.concatenate(split[1::2], axis=1)
    got = swap(theirs, "space", 1)
    half = [split[2 * k] + got[:, k * share : (k + 1) * share] for k in range(ns // 2)]
    total = half[0]
    for k in range(1, ns // 2):
        total = total + swap(half[k].astype(BF), "space", 2 * k).astype(F32)
    total = total.reshape(nf // 2, 2, rows, share)
    near = total[:, 0] + swap(total[:, 1].astype(BF), "filter", 1).astype(F32)
    result = near[0]
    for k in range(1, nf // 2):
        result = result + swap(near[k].astype(BF), "filter", 2 * k).astype(F32)
    return result


def halo(first, last):
    size = lax.axis_size("space")
    before = lax.ppermute(last, "space", [(i, i + 1) for i in range(size - 1)])
    after = lax.ppermute(first, "space", [(i + 1, i) for i in range(size - 1)])
    return before, after


def fill(pad_ref, plane, source):
    rows, width, ch = pad_ref.shape[1] - 2, pad_ref.shape[2], pad_ref.shape[3]
    pad_ref[plane, 1 : rows + 1] = source.astype(F32).reshape(rows, width, ch)
    pad_ref[plane, 0] = jnp.zeros((width, ch), F32)
    pad_ref[plane, rows + 1] = jnp.zeros((width, ch), F32)


def shifted(value, up):
    width = value.shape[0]
    index = lax.broadcasted_iota(jnp.int32, value.shape, 0)
    if up:
        return jnp.where(index == width - 1, 0.0, pltpu.roll(value, width - 1, 0))
    return jnp.where(index == 0, 0.0, pltpu.roll(value, 1, 0))


def conv_row(pad_ref, taps_ref, plane, row, flip):
    sums = [None, None, None]
    for a in range(3):
        for b in range(3):
            da, db = (1 - a, 1 - b) if flip else (a - 1, b - 1)
            line = pad_ref[plane + da, row + db]
            for e in range(3):
                term = taps_ref[pl.ds(a * 9 + b * 3 + e, 1), :] * line
                sums[e] = term if sums[e] is None else sums[e] + term
    lo, hi = (sums[2], sums[0]) if flip else (sums[0], sums[2])
    return sums[1] + shifted(lo, False) + shifted(hi, True)


def load_planes(pad_ref, refs, where, before_ref, after_ref, wanted, planes):
    for p in sorted(wanted):
        if p < 0:
            fill(pad_ref, 0, before_ref[...])
        elif p >= planes:
            fill(pad_ref, planes + 1, after_ref[...])
        else:
            which, at = where[p]
            cells = refs[which].shape[1] // len([q for q in where if where[q][0] == which])
            fill(pad_ref, p + 1, refs[which][:, at * cells : (at + 1) * cells, :])


def forward_kernel(group, where, planes, m0, m1, before, after, taps, vol, up, grad, out, pad):
    wanted = {p + a for p in group for a in (-1, 0, 1)}
    load_planes(pad, (m0, m1), where, before, after, wanted, planes)
    strips = m0.shape[0]
    cells = vol.shape[2] // len(group)
    rows = cells // WW
    for k, p in enumerate(group):

        def strip(f, carry, k=k, p=p):
            lines = [conv_row(pad, taps, p + 1, f * rows + 1 + r, False) for r in range(rows)]
            spatial = jnp.concatenate(lines, axis=0)
            sig = 1.0 / (1.0 + jnp.exp(-spatial))
            lane = slice(k * cells, (k + 1) * cells)
            cot = jnp.transpose(up[f, :, lane].astype(F32))
            slope = sig * (1.0 + spatial * (1.0 - sig))
            grad[f, lane, :] = (cot * slope).astype(BF)
            silu = jnp.transpose(spatial * sig)
            out[f, :, lane] = (vol[f, :, lane].astype(F32) + silu).astype(BF)
            return carry

        lax.fori_loop(0, strips, strip, 0)


def backward_kernel(group, where, planes, g0, g1, before, after, taps, out, pad):
    wanted = {p + a for p in group for a in (-1, 0, 1)}
    load_planes(pad, (g0, g1), where, before, after, wanted, planes)
    strips = g0.shape[0]
    cells = out.shape[1] // len(group)
    rows = cells // WW
    for k, p in enumerate(group):

        def strip(f, carry, k=k, p=p):
            lines = [conv_row(pad, taps, p + 1, f * rows + 1 + r, True) for r in range(rows)]
            out[f, k * cells : (k + 1) * cells, :] = jnp.concatenate(lines, axis=0).astype(BF)
            return carry

        lax.fori_loop(0, strips, strip, 0)


def taps_kernel(where, planes, norm, m0, m1, before, after, g0, g1, out, pad, gpad):
    load_planes(pad, (m0, m1), where, before, after, set(range(-1, planes + 1)), planes)
    load_planes(gpad, (g0, g1), where, before, after, set(range(planes)), planes)
    rows, width, ch = pad.shape[1] - 2, pad.shape[2], pad.shape[3]
    sums = tuple(jnp.zeros((8, ch), F32) for _ in range(27))

    def line(at, sums):
        p, h = at // rows, at % rows
        sums = list(sums)
        own = gpad[p + 1, h + 1]
        turned = (shifted(own, True), own, shifted(own, False))
        for a in range(3):
            for b in range(3):
                field = pad[p + a, h + b]
                for e in range(3):
                    prod = (turned[e] * field).reshape(width // 8, 8, ch)
                    sums[a * 9 + b * 3 + e] = sums[a * 9 + b * 3 + e] + jnp.sum(prod, axis=0)
        return tuple(sums)

    sums = lax.fori_loop(0, planes * rows, line, sums)
    for k in range(27):
        out[k : k + 1, :] = jnp.sum(sums[k], axis=0, keepdims=True) * norm


def call(kernel, out_shape, scratch, *args, ops=0):
    return pl.pallas_call(
        kernel,
        out_shape=out_shape,
        in_specs=[pl.BlockSpec(memory_space=pltpu.VMEM)] * len(args),
        out_specs=jax.tree.map(lambda _: pl.BlockSpec(memory_space=pltpu.VMEM), out_shape),
        scratch_shapes=scratch,
        compiler_params=pltpu.CompilerParams(vmem_limit_bytes=40 * 1024 * 1024),
        cost_estimate=pl.CostEstimate(flops=ops, bytes_accessed=4 * 1024 * 1024, transcendentals=0),
    )(*args)


def body(volume, mixing, kernel_taps, upstream):
    ch, planes, flat = volume.shape
    height = flat // WW
    nf, ns = lax.axis_size("filter"), lax.axis_size("space")
    me, me_space = lax.axis_index("filter"), lax.axis_index("space")
    cells = flat // nf
    strips = flat // (2 * WW)
    lanes = 2 * WW
    norm = 1.0 / math.sqrt(planes * ns * flat)
    edges, middle = (0, planes - 1), tuple(range(1, planes - 1))
    groups = (edges, middle)
    where = {p: (i, k) for i, g in enumerate(groups) for k, p in enumerate(g)}
    turn = me ^ (me_space * (nf // ns))

    def strips_of(field, group, count):
        part = jnp.stack([field[:, p] for p in group], axis=1)
        part = part.reshape(ch, len(group), count, flat // count).transpose(2, 0, 1, 3)
        return part.reshape(count, ch, len(group) * (flat // count))

    vol_all = []
    for g in groups:
        part = strips_of(volume, g, nf)
        got = exchange([pick(part, me ^ s) for s in range(nf)], "filter")
        vol_all.append(place(got, turn).reshape(ns, nf * ch // ns, part.shape[2]))
    weights = gather_weights(mixing, me_space)
    vol_strips = [strips_of(volume, g, strips) for g in groups]
    up_strips = [strips_of(upstream, g, strips) for g in groups]
    vol_all[0], up_strips = lax.optimization_barrier((vol_all[0], up_strips))

    mixed = []
    for part in vol_all:
        prod = lax.dot_general(
            part, weights, (((0, 1), (0, 2)), ((), ())), preferred_element_type=F32
        ).astype(BF)
        got = exchange([prod[:, s * ch : (s + 1) * ch] for s in range(nf)], "filter")
        mixed.append(restrip(place(got, me), len(groups[len(mixed)]), strips))

    taps = kernel_taps.T
    before, after = halo(mixed[0][:, :lanes], mixed[0][:, lanes:])
    pad = pltpu.VMEM((planes + 2, height + 2, WW, ch), F32)
    conv_ops = 60 * flat * ch

    def forward(i):
        g = groups[i]
        shapes = (
            jax.ShapeDtypeStruct((strips, len(g) * lanes, ch), BF),
            jax.ShapeDtypeStruct((strips, ch, len(g) * lanes), BF),
        )
        kernel = functools.partial(forward_kernel, g, where, planes)
        return call(
            kernel, shapes, [pad], mixed[0], mixed[1], before, after, taps,
            vol_strips[i], up_strips[i], ops=conv_ops * len(g),
        )

    grad_edges, out_edges = forward(0)
    grad_before, grad_after = halo(grad_edges[:, :lanes], grad_edges[:, lanes:])
    grad_middle, out_middle = forward(1)
    grads = (grad_edges, grad_middle)

    def backward(i):
        g = groups[i]
        shape = jax.ShapeDtypeStruct((strips, len(g) * lanes, ch), BF)
        kernel = functools.partial(backward_kernel, g, where, planes)
        return call(
            kernel, shape, [pad], grad_edges, grad_middle, grad_before, grad_after, taps,
            ops=conv_ops * len(g),
        )

    mg_all, back_all = [None, None], [None, None]
    for i in (1, 0):
        part = restrip(backward(i), len(groups[i]), nf)
        mg_all[i] = jnp.stack(exchange([pick(part, me ^ s) for s in range(nf)], "filter"))

    taps_part = call(
        functools.partial(taps_kernel, where, planes, norm),
        jax.ShapeDtypeStruct((27, ch), F32), [pad, pad],
        mixed[0], mixed[1], before, after, grad_edges, grad_middle,
        ops=conv_ops * planes,
    )
    taps_grad = taps_part
    step = 1
    while step < ns:
        taps_grad = taps_grad + swap(taps_grad, "space", step)
        step *= 2

    whole = [None] * planes
    for g, part in zip(groups, (out_edges, out_middle)):
        part = part.reshape(strips, ch, len(g), lanes)
        for k, p in enumerate(g):
            whole[p] = part[:, :, k].transpose(1, 0, 2).reshape(ch, flat)
    output = jnp.stack(whole, axis=1)

    whole = [None] * planes
    weights_rows = weights.reshape(ns, nf, ch, weights.shape[2])
    for i in (1, 0):
        g = groups[i]
        back = lax.dot_general(
            weights_rows, mg_all[i], (((1, 2), (0, 2)), ((), ())), preferred_element_type=F32
        ).astype(BF)
        back = back.reshape(nf, ch, len(g) * cells)
        got = exchange([pick(back, turn ^ s) for s in range(nf)], "filter")
        back_own = place(got, me).reshape(nf, ch, len(g), cells)
        for k, p in enumerate(g):
            whole[p] = back_own[:, :, k].transpose(1, 0, 2).reshape(ch, flat)
    volume_grad = (upstream.astype(F32) + jnp.stack(whole, axis=1).astype(F32)).astype(BF)

    weight_part = lax.dot_general(
        jnp.concatenate(mg_all, axis=1),
        jnp.concatenate(vol_all, axis=2).reshape(nf * ch, -1),
        (((1,), (1,)), ((), ())),
        preferred_element_type=F32,
    )
    weight_part = weight_part.reshape(nf * ch, nf * ch) * norm
    mixing_grad = scatter_weight_sum(weight_part, ch)
    return (output, volume_grad, mixing_grad, taps_grad.T)


def solution(mesh):
    in_specs = (
        P("filter", "space", None),
        P("filter", None),
        P("filter", None),
        P("filter", "space", None),
    )
    out_specs = (
        P("filter", "space", None),
        P("filter", "space", None),
        P("filter", "space"),
        P("filter", None),
    )
    return jax.shard_map(body, mesh=mesh, in_specs=in_specs, out_specs=out_specs, check_vma=False)
```

```python
import functools
import math

import jax
import jax.numpy as jnp
from jax import lax
from jax.experimental import pallas as pl
from jax.experimental.pallas import tpu as pltpu
from jax.sharding import PartitionSpec as P

WW = 64
BF = jnp.bfloat16
F32 = jnp.float32


def swap(block, axis, step):
    size = lax.axis_size(axis)
    return lax.ppermute(block, axis, [(i, i ^ step) for i in range(size)])


def exchange(pieces, axis):
    size = len(pieces)
    order = list(range(size // 2, size)) + list(range(1, size // 2))
    got = {0: pieces[0]}
    for s in order:
        got[s] = swap(pieces[s], axis, s)
    return [got[s] for s in range(size)]


def place(pieces, shift):
    out = jnp.zeros((len(pieces),) + pieces[0].shape, pieces[0].dtype)
    for s, piece in enumerate(pieces):
        out = lax.dynamic_update_index_in_dim(out, piece, shift ^ s, 0)
    return out


def restrip(part, count, strips):
    n, cells, ch = part.shape[0], part.shape[1] // count, part.shape[2]
    if n == strips:
        return part
    part = part.reshape(n, count, cells, ch).transpose(1, 0, 2, 3)
    part = part.reshape(count, strips, n * cells // strips, ch).transpose(1, 0, 2, 3)
    return part.reshape(strips, count * n * cells // strips, ch)


def pick(blocks, index):
    return lax.dynamic_index_in_dim(blocks, index, 0, keepdims=False)


def gather_weights(mixing, me_space):
    rows, cols = mixing.shape
    nf, ns = lax.axis_size("filter"), lax.axis_size("space")
    share = cols // ns
    own = lax.dynamic_slice_in_dim(mixing, me_space * share, share, axis=1)
    even = jnp.stack([own] + [swap(own, "filter", s) for s in range(2, nf, 2)])
    odd = swap(even, "filter", 1)
    part = jnp.stack([even, odd], axis=1).reshape(nf * rows, share)
    held = jnp.stack([part] + [swap(part, "space", s) for s in range(2, ns, 2)])
    other = swap(held, "space", 1)
    return jnp.stack([held, other], axis=1).reshape(ns, nf * rows, share)


def scatter_weight_sum(part, rows):
    nf, ns = lax.axis_size("filter"), lax.axis_size("space")
    share = part.shape[1] // ns
    split = [part[:, v * share : (v + 1) * share] for v in range(ns)]
    theirs = jnp.concatenate(split[1::2], axis=1)
    got = swap(theirs, "space", 1)
    half = [split[2 * k] + got[:, k * share : (k + 1) * share] for k in range(ns // 2)]
    total = half[0]
    for k in range(1, ns // 2):
        total = total + swap(half[k].astype(BF), "space", 2 * k).astype(F32)
    total = total.reshape(nf // 2, 2, rows, share)
    near = total[:, 0] + swap(total[:, 1].astype(BF), "filter", 1).astype(F32)
    result = near[0]
    for k in range(1, nf // 2):
        result = result + swap(near[k].astype(BF), "filter", 2 * k).astype(F32)
    return result


def halo(first, last):
    size = lax.axis_size("space")
    before = lax.ppermute(last, "space", [(i, i + 1) for i in range(size - 1)])
    after = lax.ppermute(first, "space", [(i + 1, i) for i in range(size - 1)])
    return before, after


def fill(pad_ref, plane, source):
    rows, width, ch = pad_ref.shape[1] - 2, pad_ref.shape[2], pad_ref.shape[3]
    pad_ref[plane, 1 : rows + 1] = source.astype(F32).reshape(rows, width, ch)
    pad_ref[plane, 0] = jnp.zeros((width, ch), F32)
    pad_ref[plane, rows + 1] = jnp.zeros((width, ch), F32)


def shifted(value, up):
    width = value.shape[0]
    index = lax.broadcasted_iota(jnp.int32, value.shape, 0)
    if up:
        return jnp.where(index == width - 1, 0.0, pltpu.roll(value, width - 1, 0))
    return jnp.where(index == 0, 0.0, pltpu.roll(value, 1, 0))


def conv_row(pad_ref, taps_ref, plane, row, flip):
    sums = [None, None, None]
    for a in range(3):
        for b in range(3):
            da, db = (1 - a, 1 - b) if flip else (a - 1, b - 1)
            line = pad_ref[plane + da, row + db]
            for e in range(3):
                term = taps_ref[pl.ds(a * 9 + b * 3 + e, 1), :] * line
                sums[e] = term if sums[e] is None else sums[e] + term
    lo, hi = (sums[2], sums[0]) if flip else (sums[0], sums[2])
    return sums[1] + shifted(lo, False) + shifted(hi, True)


def load_planes(pad_ref, refs, where, sides, wanted, planes):
    lanes = 2 * WW
    for p in sorted(wanted):
        if p < 0:
            fill(pad_ref, 0, sides[0][...])
        elif p >= planes:
            fill(pad_ref, planes + 1, sides[1][...])
        else:
            which, at = where[p]
            fill(pad_ref, p + 1, refs[which][:, at * lanes : (at + 1) * lanes, :])


def forward_kernel(group, at, where, planes, m, before, after, taps, vol, up, grad, out, pad):
    wanted = {p + a for p in group for a in (-1, 0, 1)}
    load_planes(pad, (m,), where, (before, after), wanted, planes)
    lanes = 2 * WW
    for k, p in enumerate(group):

        def strip(f, carry, k=k, p=p):
            lines = [conv_row(pad, taps, p + 1, f * 2 + 1 + r, False) for r in range(2)]
            spatial = jnp.concatenate(lines, axis=0)
            sig = 1.0 / (1.0 + jnp.exp(-spatial))
            lane = slice(k * lanes, (k + 1) * lanes)
            source = slice(at[p] * lanes, (at[p] + 1) * lanes)
            cot = jnp.transpose(up[f, :, source].astype(F32))
            slope = sig * (1.0 + spatial * (1.0 - sig))
            grad[f, lane, :] = (cot * slope).astype(BF)
            silu = jnp.transpose(spatial * sig)
            out[f, :, lane] = (vol[f, :, source].astype(F32) + silu).astype(BF)
            return carry

        lax.fori_loop(0, m.shape[0], strip, 0)


def middle_forward_kernel(group, at, where, planes, m, taps, vol, up, grad, out, pad):
    forward_kernel(group, at, where, planes, m, None, None, taps, vol, up, grad, out, pad)


def backward_kernel(group, where, planes, g0, g1, before, after, taps, out, pad):
    wanted = {p + a for p in group for a in (-1, 0, 1)}
    load_planes(pad, (g0, g1), where, (before, after), wanted, planes)
    lanes = 2 * WW
    for k, p in enumerate(group):

        def strip(f, carry, k=k, p=p):
            lines = [conv_row(pad, taps, p + 1, f * 2 + 1 + r, True) for r in range(2)]
            out[f, k * lanes : (k + 1) * lanes, :] = jnp.concatenate(lines, axis=0).astype(BF)
            return carry

        lax.fori_loop(0, g0.shape[0], strip, 0)


def middle_backward_kernel(group, where, planes, g0, g1, taps, out, pad):
    backward_kernel(group, where, planes, g0, g1, None, None, taps, out, pad)


def taps_kernel(where, where_grad, planes, norm, m, before, after, g0, g1, out, pad, gpad):
    load_planes(pad, (m,), where, (before, after), range(-1, planes + 1), planes)
    load_planes(gpad, (g0, g1), where_grad, (), range(planes), planes)
    rows, width, ch = pad.shape[1] - 2, pad.shape[2], pad.shape[3]
    sums = tuple(jnp.zeros((8, ch), F32) for _ in range(27))

    def line(at, sums):
        p, h = at // rows, at % rows
        sums = list(sums)
        own = gpad[p + 1, h + 1]
        turned = (shifted(own, True), own, shifted(own, False))
        for a in range(3):
            for b in range(3):
                field = pad[p + a, h + b]
                for e in range(3):
                    prod = (turned[e] * field).reshape(width // 8, 8, ch)
                    sums[a * 9 + b * 3 + e] = sums[a * 9 + b * 3 + e] + jnp.sum(prod, axis=0)
        return tuple(sums)

    sums = lax.fori_loop(0, planes * rows, line, sums)
    for k in range(27):
        out[k : k + 1, :] = jnp.sum(sums[k], axis=0, keepdims=True) * norm


def call(kernel, out_shape, scratch, *args, ops=0):
    return pl.pallas_call(
        kernel,
        out_shape=out_shape,
        in_specs=[pl.BlockSpec(memory_space=pltpu.VMEM)] * len(args),
        out_specs=jax.tree.map(lambda _: pl.BlockSpec(memory_space=pltpu.VMEM), out_shape),
        scratch_shapes=scratch,
        compiler_params=pltpu.CompilerParams(vmem_limit_bytes=40 * 1024 * 1024),
        cost_estimate=pl.CostEstimate(flops=ops, bytes_accessed=4 * 1024 * 1024, transcendentals=0),
    )(*args)


def body(volume, mixing, kernel_taps, upstream):
    ch, planes, flat = volume.shape
    height = flat // WW
    nf, ns = lax.axis_size("filter"), lax.axis_size("space")
    me, me_space = lax.axis_index("filter"), lax.axis_index("space")
    cells = flat // nf
    strips = flat // (2 * WW)
    lanes = 2 * WW
    norm = 1.0 / math.sqrt(planes * ns * flat)
    edges, middle = (0, planes - 1), tuple(range(1, planes - 1))
    groups = (edges, middle)
    order = edges + middle
    turn = me ^ (me_space * (nf // ns))

    def strips_of(field, count):
        part = jnp.stack([field[:, p] for p in order], axis=1)
        part = part.reshape(ch, planes, count, flat // count).transpose(2, 0, 1, 3)
        return part.reshape(count, ch, planes * (flat // count))

    def planes_of(part, count):
        part = part.reshape(count, ch, planes, flat // count)
        whole = [part[:, :, order.index(p)].transpose(1, 0, 2).reshape(ch, flat) for p in range(planes)]
        return jnp.stack(whole, axis=1)

    part = strips_of(volume, nf)
    got = exchange([pick(part, me ^ s) for s in range(nf)], "filter")
    vol_all = place(got, turn).reshape(ns, nf * ch // ns, planes * cells)
    weights = gather_weights(mixing, me_space)
    vol_strips = strips_of(volume, strips)
    up_strips = strips_of(upstream, strips)
    vol_all, up_strips = lax.optimization_barrier((vol_all, up_strips))

    prod = lax.dot_general(
        vol_all, weights, (((0, 1), (0, 2)), ((), ())), preferred_element_type=F32
    ).astype(BF)
    got = exchange([prod[:, s * ch : (s + 1) * ch] for s in range(nf)], "filter")
    mixed = restrip(place(got, me), planes, strips)

    taps = kernel_taps.T
    at = {p: k for k, p in enumerate(order)}
    where = {p: (0, at[p]) for p in order}
    where_grad = {p: (i, k) for i, g in enumerate(groups) for k, p in enumerate(g)}

    def plane(field, p):
        return field[:, at[p] * lanes : (at[p] + 1) * lanes]

    before, after = halo(plane(mixed, 0), plane(mixed, planes - 1))
    pad = pltpu.VMEM((planes + 2, height + 2, WW, ch), F32)
    conv_ops = 60 * flat * ch

    def forward(i):
        g = groups[i]
        shapes = (
            jax.ShapeDtypeStruct((strips, len(g) * lanes, ch), BF),
            jax.ShapeDtypeStruct((strips, ch, len(g) * lanes), BF),
        )
        if i == 0:
            kernel = functools.partial(forward_kernel, g, at, where, planes)
            sides = (before, after)
        else:
            kernel = functools.partial(middle_forward_kernel, g, at, where, planes)
            sides = ()
        return call(
            kernel, shapes, [pad], mixed, *sides, taps, vol_strips, up_strips,
            ops=conv_ops * len(g),
        )

    grad_middle, out_middle = forward(1)
    grad_edges, out_edges = forward(0)
    grad_before, grad_after = halo(grad_edges[:, :lanes], grad_edges[:, lanes:])

    def backward(i):
        g = groups[i]
        shape = jax.ShapeDtypeStruct((strips, len(g) * lanes, ch), BF)
        if i == 0:
            kernel = functools.partial(backward_kernel, g, where_grad, planes)
            sides = (grad_before, grad_after)
        else:
            kernel = functools.partial(middle_backward_kernel, g, where_grad, planes)
            sides = ()
        return call(
            kernel, shape, [pad], grad_edges, grad_middle, *sides, taps, ops=conv_ops * len(g)
        )

    mg_middle = backward(1)
    mg_edges = backward(0)
    part = restrip(jnp.concatenate([mg_edges, mg_middle], axis=1), planes, nf)
    mg_all = jnp.stack(exchange([pick(part, me ^ s) for s in range(nf)], "filter"))

    taps_part = call(
        functools.partial(taps_kernel, where, where_grad, planes, norm),
        jax.ShapeDtypeStruct((27, ch), F32), [pad, pad],
        mixed, before, after, grad_edges, grad_middle,
        ops=conv_ops * planes,
    )
    taps_grad = taps_part
    step = 1
    while step < ns:
        taps_grad = taps_grad + swap(taps_grad, "space", step)
        step *= 2
    output = planes_of(jnp.concatenate([out_edges, out_middle], axis=2), strips)
    mg_all, taps_grad, output = lax.optimization_barrier((mg_all, taps_grad, output))

    back = lax.dot_general(
        weights.reshape(ns, nf, ch, nf * ch // ns),
        mg_all,
        (((1, 2), (0, 2)), ((), ())),
        preferred_element_type=F32,
    ).astype(BF)
    back = back.reshape(nf, ch, planes * cells)
    got = exchange([pick(back, turn ^ s) for s in range(nf)], "filter")
    back_own = planes_of(place(got, me), nf)
    volume_grad = (upstream.astype(F32) + back_own.astype(F32)).astype(BF)

    weight_part = lax.dot_general(
        mg_all,
        vol_all.reshape(nf * ch, planes * cells),
        (((1,), (1,)), ((), ())),
        preferred_element_type=F32,
    )
    weight_part = weight_part.reshape(nf * ch, nf * ch) * norm
    mixing_grad = scatter_weight_sum(weight_part, ch)
    return (output, volume_grad, mixing_grad, taps_grad.T)


def solution(mesh):
    in_specs = (
        P("filter", "space", None),
        P("filter", None),
        P("filter", None),
        P("filter", "space", None),
    )
    out_specs = (
        P("filter", "space", None),
        P("filter", "space", None),
        P("filter", "space"),
        P("filter", None),
    )
    return jax.shard_map(body, mesh=mesh, in_specs=in_specs, out_specs=out_specs, check_vma=False)
```

```python
import functools
import math

import jax
import jax.numpy as jnp
from jax import lax
from jax.experimental import pallas as pl
from jax.experimental.pallas import tpu as pltpu
from jax.sharding import PartitionSpec as P

WW = 64
BF = jnp.bfloat16
F32 = jnp.float32


def swap(block, axis, step):
    size = lax.axis_size(axis)
    return lax.ppermute(block, axis, [(i, i ^ step) for i in range(size)])


def exchange(pieces, axis):
    size = len(pieces)
    order = list(range(size // 2, size)) + list(range(1, size // 2))
    got = {0: pieces[0]}
    for s in order:
        got[s] = swap(pieces[s], axis, s)
    return [got[s] for s in range(size)]


def place(pieces, shift):
    out = jnp.zeros((len(pieces),) + pieces[0].shape, pieces[0].dtype)
    for s, piece in enumerate(pieces):
        out = lax.dynamic_update_index_in_dim(out, piece, shift ^ s, 0)
    return out


def pick(blocks, index):
    return lax.dynamic_index_in_dim(blocks, index, 0, keepdims=False)


def gather_weights(mixing, me_space, after):
    rows, cols = mixing.shape
    nf, ns = lax.axis_size("filter"), lax.axis_size("space")
    share = cols // ns
    own = lax.dynamic_slice_in_dim(mixing, me_space * share, share, axis=1)
    even = jnp.stack([own] + [swap(own, "filter", s) for s in range(2, nf, 2)])
    even, _ = lax.optimization_barrier((even, after))
    odd = swap(even, "filter", 1)
    part = jnp.stack([even, odd], axis=1).reshape(nf * rows, share)
    held = jnp.stack([part] + [swap(part, "space", s) for s in range(2, ns, 2)])
    return held, swap(held, "space", 1)


def scatter_rest(half, rows):
    nf, ns = lax.axis_size("filter"), lax.axis_size("space")
    share = 2 * half.shape[1] // ns
    half = [half[:, k * share : (k + 1) * share] for k in range(ns // 2)]
    total = half[0]
    for k in range(1, ns // 2):
        total = total + swap(half[k].astype(BF), "space", 2 * k).astype(F32)
    total = total.reshape(nf // 2, 2, rows, share)
    near = total[:, 0] + swap(total[:, 1].astype(BF), "filter", 1).astype(F32)
    result = near[0]
    for k in range(1, nf // 2):
        result = result + swap(near[k].astype(BF), "filter", 2 * k).astype(F32)
    return result


def halo(first, last):
    size = lax.axis_size("space")
    before = lax.ppermute(last, "space", [(i, i + 1) for i in range(size - 1)])
    after = lax.ppermute(first, "space", [(i + 1, i) for i in range(size - 1)])
    return before, after


def fill(pad_ref, plane, source):
    rows, width, ch = pad_ref.shape[1] - 2, pad_ref.shape[2], pad_ref.shape[3]
    pad_ref[plane, 1 : rows + 1] = source.astype(F32).reshape(rows, width, ch)
    pad_ref[plane, 0] = jnp.zeros((width, ch), F32)
    pad_ref[plane, rows + 1] = jnp.zeros((width, ch), F32)


def shifted(value, up):
    width = value.shape[0]
    index = lax.broadcasted_iota(jnp.int32, value.shape, 0)
    if up:
        return jnp.where(index == width - 1, 0.0, pltpu.roll(value, width - 1, 0))
    return jnp.where(index == 0, 0.0, pltpu.roll(value, 1, 0))


def conv_row(pad_ref, taps_ref, plane, row, flip):
    sums = [None, None, None]
    for a in range(3):
        for b in range(3):
            da, db = (1 - a, 1 - b) if flip else (a - 1, b - 1)
            line = pad_ref[plane + da, row + db]
            for e in range(3):
                term = taps_ref[pl.ds(a * 9 + b * 3 + e, 1), :] * line
                sums[e] = term if sums[e] is None else sums[e] + term
    lo, hi = (sums[2], sums[0]) if flip else (sums[0], sums[2])
    return sums[1] + shifted(lo, False) + shifted(hi, True)


def load_planes(pad_ref, refs, where, sides, wanted, planes):
    for p in sorted(wanted):
        if p < 0:
            fill(pad_ref, 0, sides[0][...])
        elif p >= planes:
            fill(pad_ref, planes + 1, sides[1][...])
        else:
            which, at = where[p]
            fill(pad_ref, p + 1, refs[which][at])


def forward_kernel(group, planes, m, before, after, taps, vol, up, grad, out, pad):
    wanted = {p + a for p in group for a in (-1, 0, 1)}
    where = {p: (0, p) for p in range(planes)}
    load_planes(pad, (m,), where, (before, after), wanted, planes)
    lanes, flat = 2 * WW, m.shape[1]
    for k, p in enumerate(group):

        def strip(f, carry, k=k, p=p):
            lines = [conv_row(pad, taps, p + 1, f * 2 + 1 + r, False) for r in range(2)]
            spatial = jnp.concatenate(lines, axis=0)
            sig = 1.0 / (1.0 + jnp.exp(-spatial))
            cells = pl.ds(pl.multiple_of(f * lanes, lanes), lanes)
            source = pl.ds(pl.multiple_of(p * flat + f * lanes, lanes), lanes)
            target = pl.ds(pl.multiple_of(k * flat + f * lanes, lanes), lanes)
            cot = jnp.transpose(up[:, source].astype(F32))
            slope = sig * (1.0 + spatial * (1.0 - sig))
            grad[k, cells, :] = (cot * slope).astype(BF)
            silu = jnp.transpose(spatial * sig)
            out[:, target] = (vol[:, source].astype(F32) + silu).astype(BF)
            return carry

        lax.fori_loop(0, flat // lanes, strip, 0)


def middle_forward_kernel(group, planes, m, taps, vol, up, grad, out, pad):
    forward_kernel(group, planes, m, None, None, taps, vol, up, grad, out, pad)


def backward_kernel(group, where, planes, g0, g1, before, after, taps, out, pad):
    wanted = {p + a for p in group for a in (-1, 0, 1)}
    load_planes(pad, (g0, g1), where, (before, after), wanted, planes)
    lanes, flat = 2 * WW, g0.shape[1]
    for k, p in enumerate(group):

        def strip(f, carry, k=k, p=p):
            lines = [conv_row(pad, taps, p + 1, f * 2 + 1 + r, True) for r in range(2)]
            cells = pl.ds(pl.multiple_of(f * lanes, lanes), lanes)
            out[k, cells, :] = jnp.concatenate(lines, axis=0).astype(BF)
            return carry

        lax.fori_loop(0, flat // lanes, strip, 0)


def middle_backward_kernel(group, where, planes, g0, g1, taps, out, pad):
    backward_kernel(group, where, planes, g0, g1, None, None, taps, out, pad)


def taps_kernel(where_grad, planes, norm, m, before, after, g0, g1, out, pad, gpad):
    where = {p: (0, p) for p in range(planes)}
    load_planes(pad, (m,), where, (before, after), range(-1, planes + 1), planes)
    load_planes(gpad, (g0, g1), where_grad, (), range(planes), planes)
    rows, width, ch = pad.shape[1] - 2, pad.shape[2], pad.shape[3]
    sums = tuple(jnp.zeros((8, ch), F32) for _ in range(27))

    def line(at, sums):
        p, h = at // rows, at % rows
        sums = list(sums)
        own = gpad[p + 1, h + 1]
        turned = (shifted(own, True), own, shifted(own, False))
        for a in range(3):
            for b in range(3):
                field = pad[p + a, h + b]
                for e in range(3):
                    prod = (turned[e] * field).reshape(width // 8, 8, ch)
                    sums[a * 9 + b * 3 + e] = sums[a * 9 + b * 3 + e] + jnp.sum(prod, axis=0)
        return tuple(sums)

    sums = lax.fori_loop(0, planes * rows, line, sums)
    for k in range(27):
        out[k : k + 1, :] = jnp.sum(sums[k], axis=0, keepdims=True) * norm


def call(kernel, out_shape, scratch, *args, ops=0):
    def place_of(arg):
        return pltpu.SMEM if arg.dtype == jnp.int32 else pltpu.VMEM

    return pl.pallas_call(
        kernel,
        out_shape=out_shape,
        in_specs=[pl.BlockSpec(memory_space=place_of(arg)) for arg in args],
        out_specs=jax.tree.map(lambda _: pl.BlockSpec(memory_space=pltpu.VMEM), out_shape),
        scratch_shapes=scratch,
        compiler_params=pltpu.CompilerParams(vmem_limit_bytes=40 * 1024 * 1024),
        cost_estimate=pl.CostEstimate(flops=ops, bytes_accessed=4 * 1024 * 1024, transcendentals=0),
    )(*args)


def mix_kernel(turn, *refs):
    nf = len(refs) - 4
    pieces, (held, other, vol_t, out) = refs[:nf], refs[nf:]
    ch = pieces[0].shape[0]
    share = held.shape[2]
    for t, piece in enumerate(pieces):
        lane = pl.ds(pl.multiple_of((turn[0] ^ t) * ch, 128), ch)
        vol_t[:, lane] = jnp.transpose(piece[...])
    for s in range(0, nf, 2):
        total = None
        for v in range(2 * held.shape[0]):
            block = (other if v % 2 else held)[v // 2, s * ch : (s + 2) * ch, :]
            term = lax.dot_general(
                vol_t[:, v * share : (v + 1) * share], block, (((1,), (1,)), ((), ())),
                preferred_element_type=F32,
            )
            total = term if total is None else total + term
        out[s] = total[:, :ch].astype(BF)
        out[s + 1] = total[:, ch:].astype(BF)


def mix(turn, pieces, held, other):
    nf, (ch, blk) = len(pieces), pieces[0].shape
    pairs, rows, share = held.shape
    if ch % 128:
        vol_t = place(pieces, turn[0]).reshape(nf * ch, blk).T
        weights = jnp.stack([held, other], axis=1).reshape(2 * pairs, rows, share)
        out = jnp.einsum(
            "cvi,voi->co", vol_t.reshape(blk, 2 * pairs, share), weights, preferred_element_type=F32
        )
        return vol_t, out.astype(BF).reshape(blk, nf, ch).transpose(1, 0, 2)
    shapes = (
        jax.ShapeDtypeStruct((blk, nf * ch), BF),
        jax.ShapeDtypeStruct((nf, blk, ch), BF),
    )
    return call(mix_kernel, shapes, [], turn, *pieces, held, other, ops=2 * blk * rows * rows)


def unmix_kernel(turn, mg, held, other, out):
    ch = out.shape[1]
    share = held.shape[2]
    for v in range(2 * held.shape[0]):
        block = (other if v % 2 else held)[v // 2]
        total = lax.dot_general(
            mg[...], block, (((1,), (0,)), ((), ())), preferred_element_type=F32
        )
        turned = jnp.transpose(total).astype(BF)
        for k in range(share // ch):
            out[(v * (share // ch) + k) ^ turn[0]] = turned[k * ch : (k + 1) * ch, :]


def unmix(turn, mg, held, other, ch):
    blk = mg.shape[0]
    pairs, rows, share = held.shape
    nf = rows // ch
    if ch % 128:
        weights = jnp.stack([held, other], axis=1).reshape(2 * pairs, rows, share)
        out = jnp.einsum("co,voi->vic", mg, weights, preferred_element_type=F32)
        out = out.astype(BF).reshape(nf, ch, blk)
        return jnp.stack([pick(out, turn[0] ^ s) for s in range(nf)])
    shape = jax.ShapeDtypeStruct((nf, ch, blk), BF)
    return call(unmix_kernel, shape, [], turn, mg, held, other, ops=2 * blk * rows * rows)


def weight_kernel(norm, mg, vol_t, mine, theirs):
    pairs = mine.shape[0]
    share = mine.shape[2]
    for v in range(2 * pairs):
        total = lax.dot_general(
            mg[...], vol_t[:, v * share : (v + 1) * share], (((0,), (0,)), ((), ())),
            preferred_element_type=F32,
        )
        if v % 2:
            theirs[v // 2] = (total * norm).astype(BF)
        else:
            mine[v // 2] = total * norm


def weight_products(mg, vol_t, norm, ns):
    rows = mg.shape[1]
    share = vol_t.shape[1] // ns
    shapes = (
        jax.ShapeDtypeStruct((ns // 2, rows, share), F32),
        jax.ShapeDtypeStruct((ns // 2, rows, share), BF),
    )
    if share % 128:
        part = lax.dot_general(mg, vol_t, (((0,), (0,)), ((), ())), preferred_element_type=F32)
        part = (part * norm).reshape(rows, ns // 2, 2, share).transpose(2, 1, 0, 3)
        return part[0], part[1].astype(BF)
    kernel = functools.partial(weight_kernel, norm)
    return call(kernel, shapes, [], mg, vol_t, ops=2 * mg.shape[0] * rows * rows)


def body(volume, mixing, kernel_taps, upstream):
    ch, planes, flat = volume.shape
    height = flat // WW
    nf, ns = lax.axis_size("filter"), lax.axis_size("space")
    me, me_space = lax.axis_index("filter"), lax.axis_index("space")
    total = planes * flat
    blk = total // nf
    norm = 1.0 / math.sqrt(ns * total)
    edges, middle = (0, planes - 1), tuple(range(1, planes - 1))
    groups = (edges, middle)
    turn = jnp.reshape(me ^ (me_space * (nf // ns)), (1,)).astype(jnp.int32)

    vol = volume.reshape(ch, total)
    send = [lax.dynamic_slice_in_dim(vol, (me ^ s) * blk, blk, axis=1) for s in range(nf)]
    pieces = exchange(send, "filter")
    held, other = gather_weights(mixing, me_space, send)
    up = upstream.reshape(ch, total)
    pieces, up, held, other = lax.optimization_barrier((pieces, up, held, other))
    vol_t, prod = mix(turn, pieces, held, other)

    got = exchange([prod[s] for s in range(nf)], "filter")
    mixed = place(got, me).reshape(planes, flat, ch)

    taps = kernel_taps.T
    before, after = halo(mixed[0], mixed[planes - 1])
    pad = pltpu.VMEM((planes + 2, height + 2, WW, ch), F32)
    conv_ops = 60 * flat * ch

    def forward(i):
        g = groups[i]
        shapes = (
            jax.ShapeDtypeStruct((len(g), flat, ch), BF),
            jax.ShapeDtypeStruct((ch, len(g) * flat), BF),
        )
        kernel = middle_forward_kernel if i else forward_kernel
        sides = () if i else (before, after)
        return call(
            functools.partial(kernel, g, planes), shapes, [pad], mixed, *sides, taps, vol, up,
            ops=conv_ops * len(g),
        )

    grad_middle, out_middle = forward(1)
    grad_edges, out_edges = forward(0)
    grad_before, grad_after = halo(grad_edges[0], grad_edges[1])
    where_grad = {p: (i, k) for i, g in enumerate(groups) for k, p in enumerate(g)}

    def backward(i):
        g = groups[i]
        shape = jax.ShapeDtypeStruct((len(g), flat, ch), BF)
        kernel = middle_backward_kernel if i else backward_kernel
        sides = () if i else (grad_before, grad_after)
        return call(
            functools.partial(kernel, g, where_grad, planes), shape, [pad],
            grad_edges, grad_middle, *sides, taps, ops=conv_ops * len(g),
        )

    mg_middle = backward(1)
    mg_edges = backward(0)
    mixed_grad = jnp.concatenate([mg_edges[:1], mg_middle, mg_edges[1:]], axis=0)
    mixed_grad = mixed_grad.reshape(nf, blk, ch)
    got = exchange([pick(mixed_grad, me ^ s) for s in range(nf)], "filter")

    late = lax.optimization_barrier((got[nf // 2], mixed, grad_edges, out_edges, out_middle))
    _, mixed, grad_edges, out_edges, out_middle = late
    taps_grad = call(
        functools.partial(taps_kernel, where_grad, planes, norm),
        jax.ShapeDtypeStruct((27, ch), F32), [pad, pad],
        mixed, before, after, grad_edges, grad_middle,
        ops=conv_ops * planes,
    )
    output = jnp.concatenate([out_edges[:, :flat], out_middle, out_edges[:, flat:]], axis=1)
    output = output.reshape(ch, planes, flat)
    got, taps_grad, output = lax.optimization_barrier((got, taps_grad, output))

    mg_all = jnp.concatenate(got, axis=1)
    mine, theirs = weight_products(mg_all, vol_t, norm, ns)
    mg_all, theirs = lax.optimization_barrier((mg_all, theirs))
    half = mine + swap(theirs, "space", 1).astype(F32)
    back = unmix(turn, mg_all, held, other, ch)
    back, half = lax.optimization_barrier((back, half))
    got = exchange([back[s] for s in range(nf)], "filter")
    back_own = jnp.zeros((ch, total), BF)
    for s, piece in enumerate(got):
        back_own = lax.dynamic_update_slice_in_dim(back_own, piece, (me ^ s) * blk, axis=1)
    back_own = back_own.reshape(ch, planes, flat)
    volume_grad = (upstream.astype(F32) + back_own.astype(F32)).astype(BF)

    half = half.transpose(1, 0, 2).reshape(nf * ch, -1)
    mixing_grad = scatter_rest(half, ch)
    step = 1
    while step < ns:
        taps_grad = taps_grad + swap(taps_grad, "space", step)
        step *= 2
    return (output, volume_grad, mixing_grad, taps_grad.T)


def solution(mesh):
    in_specs = (
        P("filter", "space", None),
        P("filter", None),
        P("filter", None),
        P("filter", "space", None),
    )
    out_specs = (
        P("filter", "space", None),
        P("filter", "space", None),
        P("filter", "space"),
        P("filter", None),
    )
    return jax.shard_map(body, mesh=mesh, in_specs=in_specs, out_specs=out_specs, check_vma=False)
```

```python
import functools
import math

import jax
import jax.numpy as jnp
from jax import lax
from jax.experimental import pallas as pl
from jax.experimental.pallas import tpu as pltpu
from jax.sharding import PartitionSpec as P

WW = 64
BF = jnp.bfloat16
F32 = jnp.float32


def swap(block, axis, step):
    size = lax.axis_size(axis)
    return lax.ppermute(block, axis, [(i, i ^ step) for i in range(size)])


def exchange(pieces, axis):
    size = len(pieces)
    order = list(range(size // 2, size)) + list(range(1, size // 2))
    got = {0: pieces[0]}
    for s in order:
        got[s] = swap(pieces[s], axis, s)
    return [got[s] for s in range(size)]


def place(pieces, shift):
    out = jnp.zeros((len(pieces),) + pieces[0].shape, pieces[0].dtype)
    for s, piece in enumerate(pieces):
        out = lax.dynamic_update_index_in_dim(out, piece, shift ^ s, 0)
    return out


def pick(blocks, index):
    return lax.dynamic_index_in_dim(blocks, index, 0, keepdims=False)


def gather_weights(mixing, me_space, send, pieces):
    rows, cols = mixing.shape
    nf, ns = lax.axis_size("filter"), lax.axis_size("space")
    share = cols // ns
    own = lax.dynamic_slice_in_dim(mixing, me_space * share, share, axis=1)
    even = jnp.stack([own] + [swap(own, "filter", s) for s in range(2, nf, 2)])
    even, _ = lax.optimization_barrier((even, send))
    odd = swap(even, "filter", 1)
    part = jnp.stack([even, odd], axis=1).reshape(nf * rows, share)
    part, _ = lax.optimization_barrier((part, pieces[nf // 2]))
    held = jnp.stack([part] + [swap(part, "space", s) for s in range(2, ns, 2)])
    held, _ = lax.optimization_barrier((held, pieces[nf // 2 :]))
    return held, swap(held, "space", 1)


def scatter_rest(half, rows):
    nf = lax.axis_size("filter")
    total = half[0]
    for k in range(1, len(half)):
        total = total + swap(half[k].astype(BF), "space", 2 * k).astype(F32)
    total = total.reshape(nf // 2, 2, rows, total.shape[1])
    near = total[:, 0] + swap(total[:, 1].astype(BF), "filter", 1).astype(F32)
    result = near[0]
    for k in range(1, nf // 2):
        result = result + swap(near[k].astype(BF), "filter", 2 * k).astype(F32)
    return result


def halo(field):
    size = lax.axis_size("space")
    odd = lax.axis_index("space") & 1
    planes = field.shape[0]
    inner = [(i, i ^ 1) for i in range(size)]
    outer = [(i, ((i + 1) ^ 1) - 1) for i in range(1, size - 1)]
    near = lax.ppermute(pick(field, (1 - odd) * (planes - 1)), "space", inner)
    far = lax.ppermute(pick(field, odd * (planes - 1)), "space", outer)
    return jnp.where(odd == 1, near, far), jnp.where(odd == 1, far, near)


def fill(pad_ref, plane, source):
    rows, width, ch = pad_ref.shape[1] - 2, pad_ref.shape[2], pad_ref.shape[3]
    pad_ref[plane, 1 : rows + 1] = source.astype(F32).reshape(rows, width, ch)
    pad_ref[plane, 0] = jnp.zeros((width, ch), F32)
    pad_ref[plane, rows + 1] = jnp.zeros((width, ch), F32)


def shifted(value, up):
    width = value.shape[0]
    index = lax.broadcasted_iota(jnp.int32, value.shape, 0)
    if up:
        return jnp.where(index == width - 1, 0.0, pltpu.roll(value, width - 1, 0))
    return jnp.where(index == 0, 0.0, pltpu.roll(value, 1, 0))


def conv_row(pad_ref, taps_ref, plane, row, flip):
    sums = [None, None, None]
    for a in range(3):
        for b in range(3):
            da, db = (1 - a, 1 - b) if flip else (a - 1, b - 1)
            line = pad_ref[plane + da, row + db]
            for e in range(3):
                term = taps_ref[pl.ds(a * 9 + b * 3 + e, 1), :] * line
                sums[e] = term if sums[e] is None else sums[e] + term
    lo, hi = (sums[2], sums[0]) if flip else (sums[0], sums[2])
    return sums[1] + shifted(lo, False) + shifted(hi, True)


def load_planes(pad_ref, refs, where, sides, wanted, planes):
    for p in sorted(wanted):
        if p < 0:
            fill(pad_ref, 0, sides[0][...])
        elif p >= planes:
            fill(pad_ref, planes + 1, sides[1][...])
        else:
            which, at = where[p]
            fill(pad_ref, p + 1, refs[which][at])


def forward_kernel(group, planes, m, before, after, taps, vol, up, grad, out, pad):
    wanted = {p + a for p in group for a in (-1, 0, 1)}
    where = {p: (0, p) for p in range(planes)}
    load_planes(pad, (m,), where, (before, after), wanted, planes)
    lanes, flat = 2 * WW, m.shape[1]
    for k, p in enumerate(group):

        def strip(f, carry, k=k, p=p):
            lines = [conv_row(pad, taps, p + 1, f * 2 + 1 + r, False) for r in range(2)]
            spatial = jnp.concatenate(lines, axis=0)
            sig = 1.0 / (1.0 + jnp.exp(-spatial))
            cells = pl.ds(pl.multiple_of(f * lanes, lanes), lanes)
            source = pl.ds(pl.multiple_of(p * flat + f * lanes, lanes), lanes)
            target = pl.ds(pl.multiple_of(k * flat + f * lanes, lanes), lanes)
            cot = jnp.transpose(up[:, source].astype(F32))
            slope = sig * (1.0 + spatial * (1.0 - sig))
            grad[k, cells, :] = (cot * slope).astype(BF)
            silu = jnp.transpose(spatial * sig)
            out[:, target] = (vol[:, source].astype(F32) + silu).astype(BF)
            return carry

        lax.fori_loop(0, flat // lanes, strip, 0)


def middle_forward_kernel(group, planes, m, taps, vol, up, grad, out, pad):
    forward_kernel(group, planes, m, None, None, taps, vol, up, grad, out, pad)


def backward_kernel(group, where, planes, g0, g1, before, after, taps, out, pad):
    wanted = {p + a for p in group for a in (-1, 0, 1)}
    load_planes(pad, (g0, g1), where, (before, after), wanted, planes)
    lanes, flat = 2 * WW, g0.shape[1]
    for k, p in enumerate(group):

        def strip(f, carry, k=k, p=p):
            lines = [conv_row(pad, taps, p + 1, f * 2 + 1 + r, True) for r in range(2)]
            cells = pl.ds(pl.multiple_of(f * lanes, lanes), lanes)
            out[k, cells, :] = jnp.concatenate(lines, axis=0).astype(BF)
            return carry

        lax.fori_loop(0, flat // lanes, strip, 0)


def middle_backward_kernel(group, where, planes, g0, g1, taps, out, pad):
    backward_kernel(group, where, planes, g0, g1, None, None, taps, out, pad)


def taps_kernel(where_grad, planes, norm, m, before, after, g0, g1, out, pad, gpad):
    where = {p: (0, p) for p in range(planes)}
    load_planes(pad, (m,), where, (before, after), range(-1, planes + 1), planes)
    load_planes(gpad, (g0, g1), where_grad, (), range(planes), planes)
    rows, width, ch = pad.shape[1] - 2, pad.shape[2], pad.shape[3]
    sums = tuple(jnp.zeros((8, ch), F32) for _ in range(27))

    def line(at, sums):
        p, h = at // rows, at % rows
        sums = list(sums)
        own = gpad[p + 1, h + 1]
        turned = (shifted(own, True), own, shifted(own, False))
        for a in range(3):
            for b in range(3):
                field = pad[p + a, h + b]
                for e in range(3):
                    prod = (turned[e] * field).reshape(width // 8, 8, ch)
                    sums[a * 9 + b * 3 + e] = sums[a * 9 + b * 3 + e] + jnp.sum(prod, axis=0)
        return tuple(sums)

    sums = lax.fori_loop(0, planes * rows, line, sums)
    for k in range(27):
        out[k : k + 1, :] = jnp.sum(sums[k], axis=0, keepdims=True) * norm


def call(kernel, out_shape, scratch, *args, ops=0):
    def place_of(arg):
        return pltpu.SMEM if arg.dtype == jnp.int32 else pltpu.VMEM

    return pl.pallas_call(
        kernel,
        out_shape=out_shape,
        in_specs=[pl.BlockSpec(memory_space=place_of(arg)) for arg in args],
        out_specs=jax.tree.map(lambda _: pl.BlockSpec(memory_space=pltpu.VMEM), out_shape),
        scratch_shapes=scratch,
        compiler_params=pltpu.CompilerParams(vmem_limit_bytes=20 * 1024 * 1024),
        cost_estimate=pl.CostEstimate(flops=ops, bytes_accessed=4 * 1024 * 1024, transcendentals=0),
    )(*args)


def mix_kernel(turn, *refs):
    nf = (len(refs) - 3) // 2
    pieces, (held, other, vol_t), out = refs[:nf], refs[nf : nf + 3], refs[nf + 3 :]
    ch = pieces[0].shape[0]
    share = held.shape[2]
    for t, piece in enumerate(pieces):
        lane = pl.ds(pl.multiple_of((turn[0] ^ t) * ch, 128), ch)
        vol_t[:, lane] = jnp.transpose(piece[...])
    for s in range(0, nf, 2):
        total = None
        for v in range(2 * held.shape[0]):
            block = (other if v % 2 else held)[v // 2, s * ch : (s + 2) * ch, :]
            term = lax.dot_general(
                vol_t[:, v * share : (v + 1) * share], block, (((1,), (1,)), ((), ())),
                preferred_element_type=F32,
            )
            total = term if total is None else total + term
        out[s][...] = total[:, :ch].astype(BF)
        out[s + 1][...] = total[:, ch:].astype(BF)


def mix(turn, pieces, held, other):
    nf, (ch, blk) = len(pieces), pieces[0].shape
    pairs, rows, share = held.shape
    if ch % 128:
        vol_t = place(pieces, turn[0]).reshape(nf * ch, blk).T
        weights = jnp.stack([held, other], axis=1).reshape(2 * pairs, rows, share)
        out = jnp.einsum(
            "cvi,voi->co", vol_t.reshape(blk, 2 * pairs, share), weights, preferred_element_type=F32
        ).astype(BF)
        return vol_t, [out[:, s * ch : (s + 1) * ch] for s in range(nf)]
    shapes = [jax.ShapeDtypeStruct((blk, nf * ch), BF)] + [jax.ShapeDtypeStruct((blk, ch), BF)] * nf
    got = call(mix_kernel, shapes, [], turn, *pieces, held, other, ops=2 * blk * rows * rows)
    return got[0], got[1:]


def unmix_kernel(turn, *refs):
    nf = (len(refs) - 4) // 2
    pieces, (held, other), out = refs[:nf], refs[nf : nf + 2], refs[nf + 2 : 2 * nf + 2]
    mg, back = refs[2 * nf + 2 :]
    ch = out[0].shape[0]
    share = held.shape[2]
    for r, piece in enumerate(pieces):
        mg[:, r * ch : (r + 1) * ch] = piece[...]
    for v in range(2 * held.shape[0]):
        block = (other if v % 2 else held)[v // 2]
        total = lax.dot_general(
            mg[...], block, (((1,), (0,)), ((), ())), preferred_element_type=F32
        )
        turned = jnp.transpose(total).astype(BF)
        for k in range(share // ch):
            back[v * (share // ch) + k] = turned[k * ch : (k + 1) * ch, :]
    for s in range(nf):
        out[s][...] = back[turn[0] ^ s]


def unmix(turn, pieces, held, other):
    nf, (blk, ch) = len(pieces), pieces[0].shape
    pairs, rows, share = held.shape
    if ch % 128:
        weights = jnp.stack([held, other], axis=1).reshape(2 * pairs, rows, share)
        mg = jnp.concatenate(pieces, axis=1)
        out = jnp.einsum("co,voi->vic", mg, weights, preferred_element_type=F32)
        out = out.astype(BF).reshape(nf, ch, blk)
        return [pick(out, turn[0] ^ s) for s in range(nf)]
    shapes = [jax.ShapeDtypeStruct((ch, blk), BF)] * nf
    scratch = [pltpu.VMEM((blk, nf * ch), BF), pltpu.VMEM((nf, ch, blk), BF)]
    return call(unmix_kernel, shapes, scratch, turn, *pieces, held, other, ops=2 * blk * rows * rows)


def weight_products(pieces, vol_t, norm, ns):
    nf, (blk, ch) = len(pieces), pieces[0].shape
    share = vol_t.shape[1] // ns
    pairs = ns // 2
    if ch % 128 or share % 128:
        mg = jnp.concatenate(pieces, axis=1)
        part = lax.dot_general(mg, vol_t, (((0,), (0,)), ((), ())), preferred_element_type=F32)
        part = (part * norm).reshape(nf * ch, pairs, 2, share)
        return [part[:, k, 0] for k in range(pairs)], part[:, :, 1].transpose(1, 0, 2).astype(BF)

    def kernel(*refs):
        parts, vol, mine, theirs = refs[:nf], refs[nf], refs[nf + 1 : nf + 1 + pairs], refs[-1]
        for r, piece in enumerate(parts):
            turned = jnp.transpose(piece[...])
            for v in range(ns):
                total = norm * lax.dot_general(
                    turned, vol[:, v * share : (v + 1) * share], (((1,), (0,)), ((), ())),
                    preferred_element_type=F32,
                )
                row = slice(r * ch, (r + 1) * ch)
                if v % 2:
                    theirs[v // 2, row, :] = total.astype(BF)
                else:
                    mine[v // 2][row, :] = total

    shapes = [jax.ShapeDtypeStruct((nf * ch, share), F32)] * pairs
    shapes.append(jax.ShapeDtypeStruct((pairs, nf * ch, share), BF))
    got = call(kernel, shapes, [], *pieces, vol_t, ops=2 * blk * (nf * ch) ** 2)
    return got[:-1], got[-1]


def finish_kernel(me, *refs):
    pieces, (up, out) = refs[:-2], refs[-2:]
    blk = pieces[0].shape[1]
    for s, piece in enumerate(pieces):
        lane = pl.ds(pl.multiple_of((me[0] ^ s) * blk, 128), blk)
        out[:, lane] = (up[:, lane].astype(F32) + piece[...].astype(F32)).astype(BF)


def body(volume, mixing, kernel_taps, upstream):
    ch, planes, flat = volume.shape
    height = flat // WW
    nf, ns = lax.axis_size("filter"), lax.axis_size("space")
    me, me_space = lax.axis_index("filter"), lax.axis_index("space")
    total = planes * flat
    blk = total // nf
    norm = 1.0 / math.sqrt(ns * total)
    edges, middle = (0, planes - 1), tuple(range(1, planes - 1))
    groups = (edges, middle)
    turn = jnp.reshape(me ^ (me_space * (nf // ns)), (1,)).astype(jnp.int32)

    vol = volume.reshape(ch, total)
    send = [lax.dynamic_slice_in_dim(vol, (me ^ s) * blk, blk, axis=1) for s in range(nf)]
    pieces = exchange(send, "filter")
    held, other = gather_weights(mixing, me_space, send, pieces)
    up = upstream.reshape(ch, total)
    pieces, up, held, other = lax.optimization_barrier((pieces, up, held, other))
    vol_t, prod = mix(turn, pieces, held, other)

    got = exchange(prod, "filter")
    mixed = place(got, me).reshape(planes, flat, ch)

    taps = kernel_taps.T
    before, after = halo(mixed)
    pad = pltpu.VMEM((planes + 2, height + 2, WW, ch), F32)
    conv_ops = 60 * flat * ch

    def forward(i):
        g = groups[i]
        shapes = (
            jax.ShapeDtypeStruct((len(g), flat, ch), BF),
            jax.ShapeDtypeStruct((ch, len(g) * flat), BF),
        )
        kernel = middle_forward_kernel if i else forward_kernel
        sides = () if i else (before, after)
        return call(
            functools.partial(kernel, g, planes), shapes, [pad], mixed, *sides, taps, vol, up,
            ops=conv_ops * len(g),
        )

    grad_middle, out_middle = forward(1)
    grad_edges, out_edges = forward(0)
    grad_before, grad_after = halo(grad_edges)
    where_grad = {p: (i, k) for i, g in enumerate(groups) for k, p in enumerate(g)}

    def backward(i):
        g = groups[i]
        shape = jax.ShapeDtypeStruct((len(g), flat, ch), BF)
        kernel = middle_backward_kernel if i else backward_kernel
        sides = () if i else (grad_before, grad_after)
        return call(
            functools.partial(kernel, g, where_grad, planes), shape, [pad],
            grad_edges, grad_middle, *sides, taps, ops=conv_ops * len(g),
        )

    mg_middle = backward(1)
    mg_edges = backward(0)
    mixed_grad = jnp.concatenate([mg_edges[:1], mg_middle, mg_edges[1:]], axis=0)
    mixed_grad = mixed_grad.reshape(nf, blk, ch)
    got = exchange([pick(mixed_grad, me ^ s) for s in range(nf)], "filter")

    late = lax.optimization_barrier((got[nf // 2], mixed, grad_edges, out_edges, out_middle))
    _, mixed, grad_edges, out_edges, out_middle = late
    taps_grad = call(
        functools.partial(taps_kernel, where_grad, planes, norm),
        jax.ShapeDtypeStruct((27, ch), F32), [pad, pad],
        mixed, before, after, grad_edges, grad_middle,
        ops=conv_ops * planes,
    )
    output = jnp.concatenate([out_edges[:, :flat], out_middle, out_edges[:, flat:]], axis=1)
    output = output.reshape(ch, planes, flat)
    step = 1
    while step < ns:
        taps_grad = taps_grad + swap(taps_grad, "space", step)
        step *= 2
    got, taps_grad, output = lax.optimization_barrier((got, taps_grad, output))

    mine, theirs = weight_products(got, vol_t, norm, ns)
    got, theirs = lax.optimization_barrier((got, theirs))
    theirs = swap(theirs, "space", 1)
    half = [mine[k] + theirs[k].astype(F32) for k in range(ns // 2)]
    mixing_grad = scatter_rest(half, ch)
    got = exchange(unmix(turn, got, held, other), "filter")
    got, mixing_grad = lax.optimization_barrier((got, mixing_grad))
    volume_grad = call(
        finish_kernel, jax.ShapeDtypeStruct((ch, total), BF), [],
        jnp.reshape(me, (1,)).astype(jnp.int32), *got, up, ops=total * ch,
    ).reshape(ch, planes, flat)
    return (output, volume_grad, mixing_grad, taps_grad.T)


def solution(mesh):
    in_specs = (
        P("filter", "space", None),
        P("filter", None),
        P("filter", None),
        P("filter", "space", None),
    )
    out_specs = (
        P("filter", "space", None),
        P("filter", "space", None),
        P("filter", "space"),
        P("filter", None),
    )
    return jax.shard_map(body, mesh=mesh, in_specs=in_specs, out_specs=out_specs, check_vma=False)
```

```python
import functools
import math

import jax
import jax.numpy as jnp
from jax import lax
from jax.experimental import pallas as pl
from jax.experimental.pallas import tpu as pltpu
from jax.sharding import PartitionSpec as P

WW = 64
BF = jnp.bfloat16
F32 = jnp.float32
VM = 16


def swap(block, axis, step):
    size = lax.axis_size(axis)
    return lax.ppermute(block, axis, [(i, i ^ step) for i in range(size)])


def exchange(pieces, axis):
    size = len(pieces)
    order = list(range(size // 2, size)) + list(range(1, size // 2))
    got = {0: pieces[0]}
    for s in order:
        got[s] = swap(pieces[s], axis, s)
    return [got[s] for s in range(size)]


def place(pieces, shift):
    out = jnp.zeros((len(pieces),) + pieces[0].shape, pieces[0].dtype)
    for s, piece in enumerate(pieces):
        out = lax.dynamic_update_index_in_dim(out, piece, shift ^ s, 0)
    return out


def pick(blocks, index):
    return lax.dynamic_index_in_dim(blocks, index, 0, keepdims=False)


def join(parts, after, us=0.4):
    def kernel(*refs):
        for k in range(len(parts)):
            refs[-1][k] = refs[k][...]

    shape = jax.ShapeDtypeStruct((len(parts),) + parts[0].shape, parts[0].dtype)
    return call(kernel, shape, [], *parts, us=us, after=after)


def gather_weights(mixing, me_space, send, pieces):
    rows, cols = mixing.shape
    nf, ns = lax.axis_size("filter"), lax.axis_size("space")
    share, pairs = cols // ns, ns // 2
    own = lax.dynamic_slice_in_dim(mixing, me_space * share, share, axis=1)
    even = join([own] + [swap(own, "filter", s) for s in range(2, nf, 2)], send[nf // 2 :])
    first = [even] + [swap(even, "space", s) for s in range(2, ns, 2)]
    odd = join([swap(even, "filter", 1)], pieces[nf // 2 : nf // 2 + 2])[0]
    second = [odd] + [swap(odd, "space", s) for s in range(2, ns, 2)]

    def kernel(*refs):
        for k in range(pairs):
            for r in range(nf):
                source = refs[pairs * (r % 2) + k]
                refs[-1][k, r * rows : (r + 1) * rows, :] = source[r // 2]

    shape = jax.ShapeDtypeStruct((pairs, nf * rows, share), BF)
    after = pieces[nf // 2 + 2 : nf // 2 + 3]
    held = call(kernel, shape, [], *first, *second, us=0.6, after=after)
    return held, swap(held, "space", 1)


def scatter_rest(mine, theirs, rows, back, pieces):
    nf, pairs, share = lax.axis_size("filter"), len(mine), theirs.shape[2]

    def near_half(*refs):
        kept, sent = refs[-pairs], refs[len(refs) - pairs + 1 :]
        got = refs[pairs]
        kept[...] = refs[0][...] + got[0].astype(F32)
        for k in range(1, pairs):
            sent[k - 1][...] = (refs[k][...] + got[k].astype(F32)).astype(BF)

    flat = jax.ShapeDtypeStruct((nf * rows, share), BF)
    shapes = [jax.ShapeDtypeStruct((nf * rows, share), F32)] + [flat] * (pairs - 1)
    half = call(near_half, shapes, [], *mine, theirs, us=0.8, after=(back,))
    got = [swap(half[k], "space", 2 * k) for k in range(1, pairs)]

    def rows_half(*refs):
        kept, sent = refs[-2:]
        for r in range(nf):
            row = slice(r * rows, (r + 1) * rows)
            total = refs[0][row, :]
            for k in range(1, pairs):
                total = total + refs[k][row, :].astype(F32)
            if r % 2:
                sent[r // 2] = total.astype(BF)
            else:
                kept[r // 2] = total

    shapes = (
        jax.ShapeDtypeStruct((nf // 2, rows, share), F32),
        jax.ShapeDtypeStruct((nf // 2, rows, share), BF),
    )
    after = pieces[nf // 2 : nf // 2 + 2]
    kept, sent = call(rows_half, shapes, [], half[0], *got, us=0.6, after=after)
    got = swap(sent, "filter", 1)

    def rows_rest(*refs):
        kept, sent = refs[-nf // 2], refs[len(refs) - nf // 2 + 1 :]
        kept[...] = refs[0][0] + refs[1][0].astype(F32)
        for k in range(1, nf // 2):
            sent[k - 1][...] = (refs[0][k] + refs[1][k].astype(F32)).astype(BF)

    one = jax.ShapeDtypeStruct((rows, share), BF)
    shapes = [jax.ShapeDtypeStruct((rows, share), F32)] + [one] * (nf // 2 - 1)
    after = pieces[nf // 2 + 2 : nf // 2 + 3]
    rest = call(rows_rest, shapes, [], kept, got, us=0.4, after=after)
    result = rest[0]
    for k in range(1, nf // 2):
        result = result + swap(rest[k], "filter", 2 * k).astype(F32)
    return result


def halo(near, far):
    size = lax.axis_size("space")
    inner = [(i, i ^ 1) for i in range(size)]
    outer = [(i, ((i + 1) ^ 1) - 1) for i in range(1, size - 1)]
    return lax.ppermute(near, "space", inner), lax.ppermute(far, "space", outer)


def fill(pad_ref, plane, source):
    rows, width, ch = pad_ref.shape[1] - 2, pad_ref.shape[2], pad_ref.shape[3]
    pad_ref[plane, 1 : rows + 1] = source.astype(F32).reshape(rows, width, ch)
    pad_ref[plane, 0] = jnp.zeros((width, ch), F32)
    pad_ref[plane, rows + 1] = jnp.zeros((width, ch), F32)


def shifted(value, up):
    width = value.shape[0]
    index = lax.broadcasted_iota(jnp.int32, value.shape, 0)
    if up:
        return jnp.where(index == width - 1, 0.0, pltpu.roll(value, width - 1, 0))
    return jnp.where(index == 0, 0.0, pltpu.roll(value, 1, 0))


def conv_row(pad_ref, taps_ref, plane, row, flip):
    sums = [None, None, None]
    for a in range(3):
        for b in range(3):
            da, db = (1 - a, 1 - b) if flip else (a - 1, b - 1)
            line = pad_ref[plane + da, row + db]
            for e in range(3):
                term = taps_ref[pl.ds(a * 9 + b * 3 + e, 1), :] * line
                sums[e] = term if sums[e] is None else sums[e] + term
    lo, hi = (sums[2], sums[0]) if flip else (sums[0], sums[2])
    return sums[1] + shifted(lo, False) + shifted(hi, True)


def load_planes(pad_ref, refs, where, sides, wanted, planes):
    for p in sorted(wanted):
        if p < 0:
            fill(pad_ref, 0, jnp.where(sides[0][0] == 1, sides[1][...], sides[2][...]))
        elif p >= planes:
            fill(pad_ref, planes + 1, jnp.where(sides[0][0] == 1, sides[2][...], sides[1][...]))
        else:
            which, at = where[p]
            fill(pad_ref, p + 1, refs[which][at])


def forward_planes(group, planes, sides, m, taps, vol, up, grad, out, pad):
    wanted = {p + a for p in group for a in (-1, 0, 1)}
    where = {p: (0, p) for p in range(planes)}
    load_planes(pad, (m,), where, sides, wanted, planes)
    lanes, flat = 2 * WW, m.shape[1]
    for k, p in enumerate(group):

        def strip(f, carry, k=k, p=p):
            lines = [conv_row(pad, taps, p + 1, f * 2 + 1 + r, False) for r in range(2)]
            spatial = jnp.concatenate(lines, axis=0)
            sig = 1.0 / (1.0 + jnp.exp(-spatial))
            cells = pl.ds(pl.multiple_of(f * lanes, lanes), lanes)
            source = pl.ds(pl.multiple_of(p * flat + f * lanes, lanes), lanes)
            target = pl.ds(pl.multiple_of(k * flat + f * lanes, lanes), lanes)
            cot = jnp.transpose(up[:, source].astype(F32))
            slope = sig * (1.0 + spatial * (1.0 - sig))
            grad[k, cells, :] = (cot * slope).astype(BF)
            silu = jnp.transpose(spatial * sig)
            out[:, target] = (vol[:, source].astype(F32) + silu).astype(BF)
            return carry

        lax.fori_loop(0, flat // lanes, strip, 0)


def forward_middle(group, planes, m, taps, vol, up, grad, out, pad):
    forward_planes(group, planes, (), m, taps, vol, up, grad, out, pad)


def forward_edges(planes, odd, m, near, far, taps, vol, up, grad, out, to_near, to_far, pad):
    sides = (odd, near, far)
    forward_planes((0, planes - 1), planes, sides, m, taps, vol, up, grad, out, pad)
    to_near[...] = jnp.where(odd[0] == 1, grad[0], grad[1])
    to_far[...] = jnp.where(odd[0] == 1, grad[1], grad[0])


def backward_planes(group, where, planes, sides, g0, g1, taps, put, pad):
    wanted = {p + a for p in group for a in (-1, 0, 1)}
    load_planes(pad, (g0, g1), where, sides, wanted, planes)
    lanes, flat = 2 * WW, g0.shape[1]
    for k, p in enumerate(group):

        def strip(f, carry, k=k, p=p):
            lines = [conv_row(pad, taps, p + 1, f * 2 + 1 + r, True) for r in range(2)]
            put(k, p, pl.multiple_of(f * lanes, lanes), jnp.concatenate(lines, axis=0).astype(BF))
            return carry

        lax.fori_loop(0, flat // lanes, strip, 0)


def backward_middle(group, where, planes, g0, g1, taps, out, pad):
    def put(k, p, cell, value):
        out[k, pl.ds(cell, value.shape[0]), :] = value

    backward_planes(group, where, planes, (), g0, g1, taps, put, pad)


def backward_edges(where, planes, me, odd, g0, g1, near, far, taps, inner, *refs):
    out, (whole, pad) = refs[:-2], refs[-2:]
    flat = g0.shape[1]

    def put(k, p, cell, value):
        whole[pl.ds(p * flat + cell, value.shape[0]), :] = value

    backward_planes((0, planes - 1), where, planes, (odd, near, far), g0, g1, taps, put, pad)
    for k in range(1, planes - 1):
        whole[k * flat : (k + 1) * flat, :] = inner[k - 1]
    blk = out[0].shape[0]
    for s in range(len(out)):
        out[s][...] = whole[pl.ds(pl.multiple_of((me[0] ^ s) * blk, blk), blk), :]


def taps_kernel(where_grad, planes, norm, odd, m, near, far, g0, g1, o0, o1, *refs):
    out, output, pad, gpad = refs[-4:]
    flat = m.shape[1]
    output[:, :flat] = o0[:, :flat]
    output[:, flat:-flat] = o1[...]
    output[:, -flat:] = o0[:, flat:]
    where = {p: (0, p) for p in range(planes)}
    load_planes(pad, (m,), where, (odd, near, far), range(-1, planes + 1), planes)
    load_planes(gpad, (g0, g1), where_grad, (), range(planes), planes)
    rows, width, ch = pad.shape[1] - 2, pad.shape[2], pad.shape[3]
    sums = tuple(jnp.zeros((8, ch), F32) for _ in range(27))

    def line(at, sums):
        p, h = at // rows, at % rows
        sums = list(sums)
        own = gpad[p + 1, h + 1]
        turned = (shifted(own, True), own, shifted(own, False))
        for a in range(3):
            for b in range(3):
                field = pad[p + a, h + b]
                for e in range(3):
                    prod = (turned[e] * field).reshape(width // 8, 8, ch)
                    sums[a * 9 + b * 3 + e] = sums[a * 9 + b * 3 + e] + jnp.sum(prod, axis=0)
        return tuple(sums)

    sums = lax.fori_loop(0, planes * rows, line, sums)
    for k in range(27):
        out[k : k + 1, :] = jnp.sum(sums[k], axis=0, keepdims=True) * norm


def call(kernel, out_shape, scratch, *args, us=1.0, vmem=VM, fetched=0, after=(), kept_out=()):
    def place_of(k, arg):
        if k >= len(args) - fetched:
            return pltpu.HBM
        return pltpu.SMEM if arg.dtype == jnp.int32 else pltpu.VMEM

    specs = [pl.BlockSpec(memory_space=place_of(k, arg)) for k, arg in enumerate(args)]
    many = isinstance(out_shape, (list, tuple))
    out_specs = [
        pl.BlockSpec(memory_space=pltpu.HBM if k in kept_out else pltpu.VMEM)
        for k in range(len(out_shape) if many else 1)
    ]

    def wrapped(*refs):
        kernel(*refs[: len(args)], *refs[len(args) + len(after) :])

    return pl.pallas_call(
        wrapped,
        out_shape=out_shape,
        in_specs=specs + [pl.BlockSpec(memory_space=pl.ANY)] * len(after),
        out_specs=type(out_shape)(out_specs) if many else out_specs[0],
        scratch_shapes=scratch,
        compiler_params=pltpu.CompilerParams(vmem_limit_bytes=vmem * 1024 * 1024),
        cost_estimate=pl.CostEstimate(
            flops=int(us * 1.15e9), bytes_accessed=1024 * 1024, transcendentals=0
        ),
    )(*args, *after)


def fetch(pieces, held, sems):
    copies = [pltpu.make_async_copy(p, held.at[t], sems.at[t]) for t, p in enumerate(pieces)]
    for copy in copies:
        copy.start()
    return copies


def fetched(pieces):
    nf = len(pieces)
    return [pltpu.VMEM((nf,) + pieces[0].shape, BF), pltpu.SemaphoreType.DMA((nf,))]


def mix_kernel(turn, held, other, *refs):
    nf = (len(refs) - 1) // 2
    pieces, vol_t, out = refs[:nf], refs[nf], refs[nf + 1 :]
    ch = pieces[0].shape[0]
    share = held.shape[2]
    for t, piece in enumerate(pieces):
        lane = pl.ds(pl.multiple_of((turn[0] ^ t) * ch, 128), ch)
        vol_t[:, lane] = jnp.transpose(piece[...])
    for s in range(0, nf, 2):
        total = None
        for v in range(2 * held.shape[0]):
            block = (other if v % 2 else held)[v // 2, s * ch : (s + 2) * ch, :]
            term = lax.dot_general(
                vol_t[:, v * share : (v + 1) * share], block, (((1,), (1,)), ((), ())),
                preferred_element_type=F32,
            )
            total = term if total is None else total + term
        out[s][...] = total[:, :ch].astype(BF)
        out[s + 1][...] = total[:, ch:].astype(BF)


def mix(turn, pieces, held, other, after):
    nf, (ch, blk) = len(pieces), pieces[0].shape
    pairs, rows, share = held.shape
    if ch % 128:
        vol_t = place(pieces, turn[0]).reshape(nf * ch, blk).T
        weights = jnp.stack([held, other], axis=1).reshape(2 * pairs, rows, share)
        out = jnp.einsum(
            "cvi,voi->co", vol_t.reshape(blk, 2 * pairs, share), weights, preferred_element_type=F32
        ).astype(BF)
        return vol_t, [out[:, s * ch : (s + 1) * ch] for s in range(nf)]
    shapes = [jax.ShapeDtypeStruct((blk, nf * ch), BF)] + [jax.ShapeDtypeStruct((blk, ch), BF)] * nf
    got = call(mix_kernel, shapes, [], turn, held, other, *pieces, us=3.0, after=after)
    return got[0], got[1:]


def unmix_kernel(turn, mg, held, other, *refs):
    out, back = refs[:-1], refs[-1]
    nf, ch = len(out), out[0].shape[0]
    share = held.shape[2]
    for v in range(2 * held.shape[0]):
        block = (other if v % 2 else held)[v // 2]
        total = lax.dot_general(
            mg[...], block, (((1,), (0,)), ((), ())), preferred_element_type=F32
        )
        turned = jnp.transpose(total).astype(BF)
        for k in range(share // ch):
            back[v * (share // ch) + k] = turned[k * ch : (k + 1) * ch, :]
    for s in range(nf):
        out[s][...] = back[turn[0] ^ s]


def unmix(turn, mg, held, other, ch):
    blk = mg.shape[0]
    pairs, rows, share = held.shape
    nf = rows // ch
    if ch % 128:
        weights = jnp.stack([held, other], axis=1).reshape(2 * pairs, rows, share)
        out = jnp.einsum("co,voi->vic", mg, weights, preferred_element_type=F32)
        out = out.astype(BF).reshape(nf, ch, blk)
        return [pick(out, turn[0] ^ s) for s in range(nf)]
    shapes = [jax.ShapeDtypeStruct((ch, blk), BF)] * nf
    scratch = [pltpu.VMEM((nf, ch, blk), BF)]
    return call(unmix_kernel, shapes, scratch, turn, mg, held, other, us=2.6)


def weight_products(pieces, vol_t, norm, ns, after):
    nf, (blk, ch) = len(pieces), pieces[0].shape
    share = vol_t.shape[1] // ns
    pairs = ns // 2
    if ch % 128 or share % 128:
        mg = jnp.concatenate(pieces, axis=1)
        part = lax.dot_general(mg, vol_t, (((0,), (0,)), ((), ())), preferred_element_type=F32)
        part = (part * norm).reshape(nf * ch, pairs, 2, share)
        return [part[:, k, 0] for k in range(pairs)], part[:, :, 1].transpose(1, 0, 2).astype(BF), mg

    def kernel(*refs):
        parts, vol, refs = refs[:nf], refs[nf], refs[nf + 1 :]
        mine, (theirs, mg) = refs[:pairs], refs[pairs:]
        for r, part in enumerate(parts):
            row = slice(r * ch, (r + 1) * ch)
            mg[:, row] = part[...]
            turned = jnp.transpose(part[...])
            for v in range(ns):
                total = norm * lax.dot_general(
                    turned, vol[:, v * share : (v + 1) * share], (((1,), (0,)), ((), ())),
                    preferred_element_type=F32,
                )
                if v % 2:
                    theirs[v // 2, row, :] = total.astype(BF)
                else:
                    mine[v // 2][row, :] = total

    shapes = [jax.ShapeDtypeStruct((nf * ch, share), F32)] * pairs
    shapes.append(jax.ShapeDtypeStruct((pairs, nf * ch, share), BF))
    shapes.append(jax.ShapeDtypeStruct((blk, nf * ch), BF))
    got = call(
        kernel, shapes, [], *pieces, vol_t, us=3.0, after=after,
    )
    return got[:-2], got[-2], got[-1]


def assemble_kernel(me, odd, *refs):
    pieces, (out, near, far, sems) = refs[:-4], refs[-4:]
    nf, flat = len(pieces), near.shape[0]
    copies = [
        pltpu.make_async_copy(p, out.at[me[0] ^ s], sems.at[s]) for s, p in enumerate(pieces)
    ]
    for copy in copies:
        copy.start()
    for copy in copies:
        copy.wait()
    blk = pieces[0].shape[0]
    for k in range(flat // blk):
        first = out[k]
        last = out[nf - flat // blk + k]
        near[k * blk : (k + 1) * blk, :] = jnp.where(odd[0] == 1, first, last)
        far[k * blk : (k + 1) * blk, :] = jnp.where(odd[0] == 1, last, first)


def assemble(me, odd, pieces, planes):
    nf, (blk, ch) = len(pieces), pieces[0].shape
    edge = jax.ShapeDtypeStruct((nf * blk // planes, ch), BF)
    shapes = (jax.ShapeDtypeStruct((nf, blk, ch), BF), edge, edge)
    got = call(
        assemble_kernel, shapes, [pltpu.SemaphoreType.DMA((nf,))], me, odd, *pieces,
        us=1.2, fetched=nf,
    )
    return got[0].reshape(planes, nf * blk // planes, ch), got[1], got[2]


def finish_kernel(me, up, *refs):
    pieces, out = refs[:-1], refs[-1]
    blk = pieces[0].shape[1]
    for s, piece in enumerate(pieces):
        lane = pl.ds(pl.multiple_of((me[0] ^ s) * blk, 128), blk)
        out[:, lane] = (up[:, lane].astype(F32) + piece[...].astype(F32)).astype(BF)


def body(volume, mixing, kernel_taps, upstream):
    ch, planes, flat = volume.shape
    height = flat // WW
    nf, ns = lax.axis_size("filter"), lax.axis_size("space")
    me, me_space = lax.axis_index("filter"), lax.axis_index("space")
    total = planes * flat
    blk = total // nf
    norm = 1.0 / math.sqrt(ns * total)
    edges, middle = (0, planes - 1), tuple(range(1, planes - 1))
    groups = (edges, middle)
    turn = jnp.reshape(me ^ (me_space * (nf // ns)), (1,)).astype(jnp.int32)

    odd = jnp.reshape(me_space & 1, (1,)).astype(jnp.int32)
    own = jnp.reshape(me, (1,)).astype(jnp.int32)

    vol = volume.reshape(ch, total)
    send = [lax.dynamic_slice_in_dim(vol, (me ^ s) * blk, blk, axis=1) for s in range(nf)]
    pieces = exchange(send, "filter")
    held, other = gather_weights(mixing, me_space, send, pieces)
    up = upstream.reshape(ch, total)
    vol_t, prod = mix(turn, pieces, held, other, (up,))

    got = exchange(prod, "filter")
    mixed, near, far = assemble(own, odd, got, planes)
    near, far = halo(near, far)

    taps = kernel_taps.T
    pad = pltpu.VMEM((planes + 2, height + 2, WW, ch), F32)

    def grad_shapes(g):
        return (
            jax.ShapeDtypeStruct((len(g), flat, ch), BF),
            jax.ShapeDtypeStruct((ch, len(g) * flat), BF),
        )

    edge = jax.ShapeDtypeStruct((flat, ch), BF)
    grad_middle, out_middle = call(
        functools.partial(forward_middle, middle, planes), grad_shapes(middle), [pad],
        mixed, taps, vol, up, us=4.0,
    )
    grad_edges, out_edges, to_near, to_far = call(
        functools.partial(forward_edges, planes), grad_shapes(edges) + (edge, edge), [pad],
        odd, mixed, near, far, taps, vol, up, us=4.0, after=(grad_middle,),
    )
    grad_near, grad_far = halo(to_near, to_far)
    where = {p: (i, k) for i, g in enumerate(groups) for k, p in enumerate(g)}
    mg_middle = call(
        functools.partial(backward_middle, middle, where, planes),
        jax.ShapeDtypeStruct((len(middle), flat, ch), BF), [pad],
        grad_edges, grad_middle, taps, us=2.3,
    )
    send = call(
        functools.partial(backward_edges, where, planes),
        [jax.ShapeDtypeStruct((blk, ch), BF)] * nf,
        [pltpu.VMEM((total, ch), BF), pad],
        own, odd, grad_edges, grad_middle, grad_near, grad_far, taps, mg_middle,
        us=2.8,
    )
    got = exchange(send, "filter")

    after = got[nf // 2 : nf // 2 + 2]
    taps_grad, output = call(
        functools.partial(taps_kernel, where, planes, norm),
        (jax.ShapeDtypeStruct((27, ch), F32), jax.ShapeDtypeStruct((ch, total), BF)), [pad, pad],
        odd, mixed, near, far, grad_edges, grad_middle, out_edges, out_middle,
        us=5.8, after=after,
    )
    output = output.reshape(ch, planes, flat)

    mine, theirs, mg_all = weight_products(got, vol_t, norm, ns, (taps_grad, output))
    theirs = swap(theirs, "space", 1)
    back = unmix(turn, mg_all, held, other, ch)
    got = exchange(back, "filter")
    mixing_grad = scatter_rest(mine, theirs, ch, back[1], got)
    volume_grad = call(
        finish_kernel, jax.ShapeDtypeStruct((ch, total), BF), [],
        own, up, *got, us=1.6,
    ).reshape(ch, planes, flat)
    step = 1
    while step < ns:
        taps_grad = taps_grad + swap(taps_grad, "space", step)
        step *= 2
    return (output, volume_grad, mixing_grad, taps_grad.T)


def solution(mesh):
    in_specs = (
        P("filter", "space", None),
        P("filter", None),
        P("filter", None),
        P("filter", "space", None),
    )
    out_specs = (
        P("filter", "space", None),
        P("filter", "space", None),
        P("filter", "space"),
        P("filter", None),
    )
    return jax.shard_map(body, mesh=mesh, in_specs=in_specs, out_specs=out_specs, check_vma=False)
```

```python
import functools
import math

import jax
import jax.numpy as jnp
from jax import lax
from jax.experimental import pallas as pl
from jax.experimental.pallas import tpu as pltpu
from jax.sharding import PartitionSpec as P

WW = 64
BF = jnp.bfloat16
F32 = jnp.float32


def swap(block, axis, step):
    size = lax.axis_size(axis)
    return lax.ppermute(block, axis, [(i, i ^ step) for i in range(size)])


def exchange(pieces, axis):
    size = len(pieces)
    order = list(range(size // 2, size)) + list(range(1, size // 2))
    got = {0: pieces[0]}
    for s in order:
        got[s] = swap(pieces[s], axis, s)
    return [got[s] for s in range(size)]


def place(pieces, shift):
    out = jnp.zeros((len(pieces),) + pieces[0].shape, pieces[0].dtype)
    for s, piece in enumerate(pieces):
        out = lax.dynamic_update_index_in_dim(out, piece, shift ^ s, 0)
    return out


def pick(blocks, index):
    return lax.dynamic_index_in_dim(blocks, index, 0, keepdims=False)


def join(parts, after, us=0.4):
    def kernel(*refs):
        for k in range(len(parts)):
            refs[-1][k] = refs[k][...]

    shape = jax.ShapeDtypeStruct((len(parts),) + parts[0].shape, parts[0].dtype)
    return call(kernel, shape, [], *parts, us=us, after=after)


def gather_weights(mixing, me_space, send, first_in, second_in):
    rows, cols = mixing.shape
    nf, ns = lax.axis_size("filter"), lax.axis_size("space")
    share, pairs = cols // ns, ns // 2
    own = lax.dynamic_slice_in_dim(mixing, me_space * share, share, axis=1)
    even = join([own] + [swap(own, "filter", s) for s in range(2, nf, 2)], send[nf // 2 :])
    first = [even] + [swap(even, "space", s) for s in range(2, ns, 2)]
    odd = join([swap(even, "filter", 1)], (first_in,))[0]
    second = [odd] + [swap(odd, "space", s) for s in range(2, ns, 2)]

    def kernel(*refs):
        for k in range(pairs):
            for r in range(nf):
                source = refs[pairs * (r % 2) + k]
                refs[-1][k, r * rows : (r + 1) * rows, :] = source[r // 2]

    shape = jax.ShapeDtypeStruct((pairs, nf * rows, share), BF)
    held = call(kernel, shape, [], *first, *second, us=0.6, after=(second_in,))
    return held, swap(held, "space", 1)


def halved(ch, share, ns):
    return ns == 4 and share == 2 * ch and ch % 128 == 0


def halves_first(rows, nf, mine0, mine1, got, taps, a_keep, a_send, b_keep, b_next, b_send, sums):
    h, count = a_keep.shape[1], taps.shape[0]
    total = joined(*split(taps[...])) + joined(got[0, nf * rows :, :h], got[1, nf * rows :, :h])
    high, low = split(total)
    a_send[nf * rows : nf * rows + count, :] = high
    a_send[nf * rows + count :, :] = low
    sums[...] = joined(high, low)
    for r in range(nf):
        row = slice(r * rows, (r + 1) * rows)
        own = mine0[row, :] + got[0, row, :].astype(F32)
        step = mine1[row, :] + got[1, row, :].astype(F32)
        a_keep[row, :] = own[:, :h]
        a_send[row, :] = step[:, :h].astype(BF)
        if r % 2:
            b_send[0, r // 2] = own[:, h:].astype(BF)
            b_send[1, r // 2] = step[:, h:].astype(BF)
        else:
            b_keep[r // 2] = own[:, h:]
            b_next[r // 2] = step[:, h:]


def halves_second(rows, nf, a_keep, a_got, b_keep, b_next, b_got, sums, near, a_send, far, b_send, taps):
    count = taps.shape[0]
    high, low = a_got[nf * rows : nf * rows + count, :], a_got[nf * rows + count :, :]
    taps[...] = sums[...] + joined(high, low)
    for r in range(nf):
        row = slice(r * rows, (r + 1) * rows)
        own = a_keep[row, :] + a_got[row, :].astype(F32)
        if r % 2:
            a_send[r // 2] = own.astype(BF)
        else:
            near[r // 2] = own
    far[...] = b_keep[...] + b_got[0].astype(F32)
    b_send[...] = (b_next[...] + b_got[1].astype(F32)).astype(BF)


def halves_third(near, a_got, far, b_got, keep, *send):
    h = near.shape[2]
    for k in range(near.shape[0]):
        left = near[k] + a_got[k].astype(F32)
        right = far[k] + b_got[k].astype(F32)
        if k:
            send[k - 1][:, :h] = left.astype(BF)
            send[k - 1][:, h:] = right.astype(BF)
        else:
            keep[:, :h] = left
            keep[:, h:] = right


def scatter_rest(mine, theirs, taps, rows, first_in, second_in):
    nf, ns = lax.axis_size("filter"), lax.axis_size("space")
    pairs, share = ns // 2, theirs.shape[2]
    theirs = swap(theirs, "space", 1)
    if halved(rows, share, ns):
        h, n, count = share // 2, nf // 2, taps.shape[0]
        shapes = (
            jax.ShapeDtypeStruct((nf * rows, h), F32),
            jax.ShapeDtypeStruct((nf * rows + 2 * count, h), BF),
            jax.ShapeDtypeStruct((n, rows, h), F32), jax.ShapeDtypeStruct((n, rows, h), F32),
            jax.ShapeDtypeStruct((2, n, rows, h), BF), jax.ShapeDtypeStruct((count, h), F32),
        )
        kernel = functools.partial(halves_first, rows, nf)
        a_keep, a_send, b_keep, b_next, b_send, sums = call(
            kernel, shapes, [], *mine, theirs, taps, us=0.8
        )
        a_got = swap(a_send, "space", 2)
        b_got = swap(b_send, "filter", 1)
        shapes = (
            jax.ShapeDtypeStruct((n, rows, h), F32), jax.ShapeDtypeStruct((n, rows, h), BF),
            jax.ShapeDtypeStruct((n, rows, h), F32), jax.ShapeDtypeStruct((n, rows, h), BF),
            jax.ShapeDtypeStruct((count, h), F32),
        )
        kernel = functools.partial(halves_second, rows, nf)
        near, a_send, far, b_send, taps = call(
            kernel, shapes, [], a_keep, a_got, b_keep, b_next, b_got, sums,
            us=0.6, after=(first_in,),
        )
        a_got = swap(a_send, "filter", 1)
        b_got = swap(b_send, "space", 2)
        shapes = [jax.ShapeDtypeStruct((rows, share), F32)]
        shapes += [jax.ShapeDtypeStruct((rows, share), BF)] * (n - 1)
        keep, *rest = call(
            halves_third, shapes, [], near, a_got, far, b_got, us=0.5, after=(second_in,)
        )
    else:
        step = 1
        while step < ns:
            taps = taps + swap(taps, "space", step)
            step *= 2
        total = mine[0] + theirs[0].astype(F32)
        for k in range(1, pairs):
            send = (mine[k] + theirs[k].astype(F32)).astype(BF)
            total = total + swap(send, "space", 2 * k).astype(F32)
        total = total.reshape(nf // 2, 2, rows, share)
        near = total[:, 0] + swap(total[:, 1].astype(BF), "filter", 1).astype(F32)
        keep, rest = near[0], [near[k].astype(BF) for k in range(1, nf // 2)]
    for k, part in enumerate(rest):
        keep = keep + swap(part, "filter", 2 * (k + 1)).astype(F32)
    return keep, taps


def halo(near, far):
    size = lax.axis_size("space")
    inner = [(i, i ^ 1) for i in range(size)]
    outer = [(i, ((i + 1) ^ 1) - 1) for i in range(1, size - 1)]
    return lax.ppermute(near, "space", inner), lax.ppermute(far, "space", outer)


def fill(pad_ref, plane, source):
    rows, width, ch = pad_ref.shape[1] - 2, pad_ref.shape[2], pad_ref.shape[3]
    pad_ref[plane, 1 : rows + 1] = source.astype(F32).reshape(rows, width, ch)
    pad_ref[plane, 0] = jnp.zeros((width, ch), F32)
    pad_ref[plane, rows + 1] = jnp.zeros((width, ch), F32)


def shifted(value, up):
    width = value.shape[0]
    index = lax.broadcasted_iota(jnp.int32, value.shape, 0)
    if up:
        return jnp.where(index == width - 1, 0.0, pltpu.roll(value, width - 1, 0))
    return jnp.where(index == 0, 0.0, pltpu.roll(value, 1, 0))


def conv_row(pad_ref, taps_ref, plane, row, flip):
    sums = [None, None, None]
    for a in range(3):
        for b in range(3):
            da, db = (1 - a, 1 - b) if flip else (a - 1, b - 1)
            line = pad_ref[plane + da, row + db]
            for e in range(3):
                term = taps_ref[pl.ds(a * 9 + b * 3 + e, 1), :] * line
                sums[e] = term if sums[e] is None else sums[e] + term
    lo, hi = (sums[2], sums[0]) if flip else (sums[0], sums[2])
    return sums[1] + shifted(lo, False) + shifted(hi, True)


def load_planes(pad_ref, refs, where, sides, wanted, planes):
    for p in sorted(wanted):
        if p < 0:
            fill(pad_ref, 0, jnp.where(sides[0][0] == 1, sides[1][...], sides[2][...]))
        elif p >= planes:
            fill(pad_ref, planes + 1, jnp.where(sides[0][0] == 1, sides[2][...], sides[1][...]))
        else:
            which, at = where[p]
            fill(pad_ref, p + 1, refs[which][at])


def forward_planes(group, planes, sides, m, taps, vol, up, grad, out, pad):
    wanted = {p + a for p in group for a in (-1, 0, 1)}
    where = {p: (0, p) for p in range(planes)}
    load_planes(pad, (m,), where, sides, wanted, planes)
    lanes, flat = 2 * WW, m.shape[1]
    for k, p in enumerate(group):

        def strip(f, carry, k=k, p=p):
            lines = [conv_row(pad, taps, p + 1, f * 2 + 1 + r, False) for r in range(2)]
            spatial = jnp.concatenate(lines, axis=0)
            sig = 1.0 / (1.0 + jnp.exp(-spatial))
            cells = pl.ds(pl.multiple_of(f * lanes, lanes), lanes)
            source = pl.ds(pl.multiple_of(p * flat + f * lanes, lanes), lanes)
            target = pl.ds(pl.multiple_of(k * flat + f * lanes, lanes), lanes)
            cot = jnp.transpose(up[:, source].astype(F32))
            slope = sig * (1.0 + spatial * (1.0 - sig))
            grad[k, cells, :] = (cot * slope).astype(BF)
            silu = jnp.transpose(spatial * sig)
            out[:, target] = (vol[:, source].astype(F32) + silu).astype(BF)
            return carry

        lax.fori_loop(0, flat // lanes, strip, 0)


def forward_middle(group, planes, m, taps, vol, up, grad, out, pad):
    forward_planes(group, planes, (), m, taps, vol, up, grad, out, pad)


def forward_edges(planes, odd, m, near, far, taps, vol, up, grad, out, to_near, to_far, pad):
    sides = (odd, near, far)
    forward_planes((0, planes - 1), planes, sides, m, taps, vol, up, grad, out, pad)
    to_near[...] = jnp.where(odd[0] == 1, grad[0], grad[1])
    to_far[...] = jnp.where(odd[0] == 1, grad[1], grad[0])


def backward_planes(group, where, planes, sides, g0, g1, taps, put, pad):
    wanted = {p + a for p in group for a in (-1, 0, 1)}
    load_planes(pad, (g0, g1), where, sides, wanted, planes)
    lanes, flat = 2 * WW, g0.shape[1]
    for k, p in enumerate(group):

        def strip(f, carry, k=k, p=p):
            lines = [conv_row(pad, taps, p + 1, f * 2 + 1 + r, True) for r in range(2)]
            put(k, p, pl.multiple_of(f * lanes, lanes), jnp.concatenate(lines, axis=0).astype(BF))
            return carry

        lax.fori_loop(0, flat // lanes, strip, 0)


def backward_middle(group, where, planes, g0, g1, taps, out, pad):
    def put(k, p, cell, value):
        out[k, pl.ds(cell, value.shape[0]), :] = value

    backward_planes(group, where, planes, (), g0, g1, taps, put, pad)


def backward_edges(where, planes, steps, me, odd, g0, g1, near, far, taps, inner, whole, *refs):
    out, pad = refs[:-1], refs[-1]
    flat = g0.shape[1]

    def put(k, p, cell, value):
        whole[pl.ds(p * flat + cell, value.shape[0]), :] = value

    backward_planes((0, planes - 1), where, planes, (odd, near, far), g0, g1, taps, put, pad)
    for k in range(1, planes - 1):
        whole[k * flat : (k + 1) * flat, :] = inner[k - 1]
    blk = out[0].shape[0]
    for s, block in zip(steps, out):
        block[...] = whole[pl.ds(pl.multiple_of((me[0] ^ s) * blk, blk), blk), :]


def blocks(me, whole, blk, steps, after):
    def kernel(me, whole, *out):
        for s, block in zip(steps, out):
            block[...] = whole[pl.ds(pl.multiple_of((me[0] ^ s) * blk, blk), blk), :]

    shapes = [jax.ShapeDtypeStruct((blk, whole.shape[1]), BF)] * len(steps)
    return call(kernel, shapes, [], me, whole, us=0.3, after=after)


def taps_kernel(where_grad, planes, norm, steps, odd, m, near, far, g0, g1, o0, o1, *refs):
    parts, refs = refs[: len(steps)], refs[len(steps) :]
    out, output, pad, gpad = refs[0], refs[1], refs[-2], refs[-1]
    for r, part in zip(steps, parts):
        refs[2][:, r * part.shape[1] : (r + 1) * part.shape[1]] = part[...]
    flat = m.shape[1]
    output[:, :flat] = o0[:, :flat]
    output[:, flat:-flat] = o1[...]
    output[:, -flat:] = o0[:, flat:]
    where = {p: (0, p) for p in range(planes)}
    load_planes(pad, (m,), where, (odd, near, far), range(-1, planes + 1), planes)
    load_planes(gpad, (g0, g1), where_grad, (), range(planes), planes)
    rows, width, ch = pad.shape[1] - 2, pad.shape[2], pad.shape[3]
    sums = tuple(jnp.zeros((8, ch), F32) for _ in range(27))

    def line(at, sums):
        p, h = at // rows, at % rows
        sums = list(sums)
        own = gpad[p + 1, h + 1]
        turned = (shifted(own, True), own, shifted(own, False))
        for a in range(3):
            for b in range(3):
                field = pad[p + a, h + b]
                for e in range(3):
                    prod = (turned[e] * field).reshape(width // 8, 8, ch)
                    sums[a * 9 + b * 3 + e] = sums[a * 9 + b * 3 + e] + jnp.sum(prod, axis=0)
        return tuple(sums)

    sums = lax.fori_loop(0, planes * rows, line, sums)
    for k in range(27):
        out[k : k + 1, :] = jnp.sum(sums[k], axis=0, keepdims=True) * norm
    out[27:, :] = jnp.zeros((5, ch), F32)


def call(kernel, out_shape, scratch, *args, us=1.0, after=(), alias=None):
    specs = [
        pl.BlockSpec(memory_space=pltpu.SMEM if arg.dtype == jnp.int32 else pltpu.VMEM)
        for arg in args
    ]

    def wrapped(*refs):
        kernel(*refs[: len(args)], *refs[len(args) + len(after) :])

    return pl.pallas_call(
        wrapped,
        out_shape=out_shape,
        in_specs=specs + [pl.BlockSpec(memory_space=pl.ANY)] * len(after),
        out_specs=jax.tree.map(lambda _: pl.BlockSpec(memory_space=pltpu.VMEM), out_shape),
        scratch_shapes=scratch,
        input_output_aliases={} if alias is None else {alias: 0},
        compiler_params=pltpu.CompilerParams(vmem_limit_bytes=32 * 1024 * 1024),
        cost_estimate=pl.CostEstimate(
            flops=int(us * 1.15e9), bytes_accessed=1024 * 1024, transcendentals=0
        ),
    )(*args, *after)


def in_place(kernel, shape, leading, base, pieces, us):
    if base is None:
        return call(kernel, shape, [], *leading, *pieces, us=us)

    def wrapped(*refs):
        kernel(*refs[: len(leading)], *refs[len(leading) + 1 :])

    return call(wrapped, shape, [], *leading, base, *pieces, us=us, alias=len(leading))


def fold_volume(turn, base, pieces, steps):
    nf, (ch, blk) = lax.axis_size("filter"), pieces[0].shape
    if ch % 128:
        out = jnp.zeros((nf, ch, blk), BF) if base is None else base
        for t, piece in zip(steps, pieces):
            out = lax.dynamic_update_index_in_dim(out, piece, turn[0] ^ t, 0)
        return out

    def kernel(turn, *refs):
        for t, piece in zip(steps, refs[:-1]):
            lane = pl.ds(pl.multiple_of((turn[0] ^ t) * ch, 128), ch)
            refs[-1][:, lane] = jnp.transpose(piece[...])

    shape = jax.ShapeDtypeStruct((blk, nf * ch), BF)
    return in_place(kernel, shape, (turn,), base, pieces, 0.3 * len(pieces))


def mix_kernel(held, other, vol_t, *out):
    nf, ch, share = len(out), out[0].shape[1], held.shape[2]
    for s in range(0, nf, 2):
        total = None
        for v in range(2 * held.shape[0]):
            block = (other if v % 2 else held)[v // 2, s * ch : (s + 2) * ch, :]
            term = lax.dot_general(
                vol_t[:, v * share : (v + 1) * share], block, (((1,), (1,)), ((), ())),
                preferred_element_type=F32,
            )
            total = term if total is None else total + term
        out[s][...] = total[:, :ch].astype(BF)
        out[s + 1][...] = total[:, ch:].astype(BF)


def mix(vol, held, other, ch, after):
    pairs, rows, share = held.shape
    nf = rows // ch
    if ch % 128:
        vol_t = vol.reshape(rows, vol.shape[2]).T
        weights = jnp.stack([held, other], axis=1).reshape(2 * pairs, rows, share)
        out = jnp.einsum(
            "cvi,voi->co", vol_t.reshape(-1, 2 * pairs, share), weights, preferred_element_type=F32
        ).astype(BF)
        return vol_t, [out[:, s * ch : (s + 1) * ch] for s in range(nf)]
    shapes = [jax.ShapeDtypeStruct((vol.shape[0], ch), BF)] * nf
    return vol, call(mix_kernel, shapes, [], held, other, vol, us=2.6, after=after)


def unmix(turn, base, pieces, steps, held, other, ch, after):
    blk = pieces[0].shape[0]
    pairs, rows, share = held.shape
    nf = rows // ch
    if ch % 128:
        weights = jnp.stack([held, other], axis=1).reshape(2 * pairs, rows, share)
        mg = jnp.concatenate([part for _, part in sorted(list(base.items()) + list(zip(steps, pieces)))], axis=1)
        out = jnp.einsum("co,voi->vic", mg, weights, preferred_element_type=F32)
        out = out.astype(BF).reshape(nf, ch, blk)
        return mg, [pick(out, turn[0] ^ s) for s in range(nf)]

    def kernel(turn, base, held, other, *refs):
        parts, mg, out, back = refs[: len(steps)], refs[len(steps)], refs[-nf - 1 : -1], refs[-1]
        mg[...] = base[...]
        for r, part in zip(steps, parts):
            mg[:, r * ch : (r + 1) * ch] = part[...]
        for v in range(2 * pairs):
            block = (other if v % 2 else held)[v // 2]
            total = lax.dot_general(
                mg[...], block, (((1,), (0,)), ((), ())), preferred_element_type=F32
            )
            turned = jnp.transpose(total).astype(BF)
            for k in range(share // ch):
                back[v * (share // ch) + k] = turned[k * ch : (k + 1) * ch, :]
        for s in range(nf):
            out[s][...] = back[turn[0] ^ s]

    shapes = [jax.ShapeDtypeStruct((blk, rows), BF)] + [jax.ShapeDtypeStruct((ch, blk), BF)] * nf
    got = call(
        kernel, shapes, [pltpu.VMEM((nf, ch, blk), BF)], turn, base, held, other, *pieces,
        us=3.0, after=after,
    )
    return got[0], got[1:]


def split(value):
    high = value.astype(BF)
    return high, (value - high.astype(F32)).astype(BF)


def joined(high, low):
    return high.astype(F32) + low.astype(F32)


def weight_products(mg, vol_t, taps, ch, norm, ns):
    rows, share, pairs = mg.shape[1], vol_t.shape[1] // ns, ns // 2
    if halved(ch, share, ns):
        count = taps.shape[0]

        def kernel(mg, vol, taps, *refs):
            mine, theirs = refs[:pairs], refs[-1]
            for r in range(rows // ch):
                row = slice(r * ch, (r + 1) * ch)
                turned = jnp.transpose(mg[:, row])
                for v in range(ns):
                    total = norm * lax.dot_general(
                        turned, vol[:, v * share : (v + 1) * share], (((1,), (0,)), ((), ())),
                        preferred_element_type=F32,
                    )
                    if v % 2:
                        theirs[v // 2, row, :] = total.astype(BF)
                    else:
                        mine[v // 2][row, :] = total
            high, low = split(taps[...])
            theirs[0, rows:, :ch] = high
            theirs[1, rows:, :ch] = low

        shapes = [jax.ShapeDtypeStruct((rows, share), F32)] * pairs
        shapes.append(jax.ShapeDtypeStruct((pairs, rows + count, share), BF))
        got = call(kernel, shapes, [], mg, vol_t, taps, us=2.5)
        return got[:-1], got[-1]
    part = lax.dot_general(mg, vol_t, (((0,), (0,)), ((), ())), preferred_element_type=F32)
    part = (part * norm).reshape(rows, pairs, 2, share)
    return [part[:, k, 0] for k in range(pairs)], part[:, :, 1].transpose(1, 0, 2).astype(BF)


def assemble(me, base, pieces, steps):
    blk, ch = pieces[0].shape

    def kernel(me, *refs):
        for s, piece in zip(steps, refs[:-1]):
            refs[-1][me[0] ^ s] = piece[...]

    shape = jax.ShapeDtypeStruct((lax.axis_size("filter"), blk, ch), BF)
    return in_place(kernel, shape, (me,), base, pieces, 0.5)


def assemble_last(me, odd, base, pieces, steps, planes):
    nf, blk, ch = base.shape
    flat = nf * blk // planes

    def kernel(me, odd, base, *refs):
        out, near, far = refs[-3:]
        for s, piece in zip(steps, refs[:-3]):
            out[me[0] ^ s] = piece[...]
        for k in range(flat // blk):
            first, last = out[k], out[nf - flat // blk + k]
            near[k * blk : (k + 1) * blk, :] = jnp.where(odd[0] == 1, first, last)
            far[k * blk : (k + 1) * blk, :] = jnp.where(odd[0] == 1, last, first)

    edge = jax.ShapeDtypeStruct((flat, ch), BF)
    shapes = (jax.ShapeDtypeStruct((nf, blk, ch), BF), edge, edge)
    out, near, far = call(kernel, shapes, [], me, odd, base, *pieces, us=0.8, alias=2)
    return out.reshape(planes, flat, ch), near, far


def finish(me, up, base, pieces, steps):
    blk = pieces[0].shape[1]

    def kernel(me, up, *refs):
        for s, piece in zip(steps, refs[:-1]):
            lane = pl.ds(pl.multiple_of((me[0] ^ s) * blk, 128), blk)
            refs[-1][:, lane] = (up[:, lane].astype(F32) + piece[...].astype(F32)).astype(BF)

    shape = jax.ShapeDtypeStruct(up.shape, BF)
    return in_place(kernel, shape, (me, up), base, pieces, 0.25 * len(pieces))


def body(volume, mixing, kernel_taps, upstream):
    ch, planes, flat = volume.shape
    height = flat // WW
    nf, ns = lax.axis_size("filter"), lax.axis_size("space")
    me, me_space = lax.axis_index("filter"), lax.axis_index("space")
    total = planes * flat
    blk = total // nf
    norm = 1.0 / math.sqrt(ns * total)
    edges, middle = (0, planes - 1), tuple(range(1, planes - 1))
    groups = (edges, middle)
    turn = jnp.reshape(me ^ (me_space * (nf // ns)), (1,)).astype(jnp.int32)

    odd = jnp.reshape(me_space & 1, (1,)).astype(jnp.int32)
    own = jnp.reshape(me, (1,)).astype(jnp.int32)

    vol = volume.reshape(ch, total)
    mid = nf // 2
    early = [0, mid]
    later = [s for s in range(mid + 1, nf)]
    last = list(range(1, mid))

    def some(parts, steps):
        return [parts[s] for s in steps]

    send = [lax.dynamic_slice_in_dim(vol, (me ^ s) * blk, blk, axis=1) for s in range(nf)]
    pieces = exchange(send, "filter")
    steps = early + [mid + 1]
    vol_1 = fold_volume(turn, None, some(pieces, steps), steps)
    vol_2 = fold_volume(turn, vol_1, some(pieces, [mid + 2, 1]), [mid + 2, 1])
    rest = later[2:] + last[1:]
    vol_3 = fold_volume(turn, vol_2, some(pieces, rest), rest)
    held, other = gather_weights(mixing, me_space, send, vol_1, vol_2)
    up = upstream.reshape(ch, total)
    vol_t, prod = mix(vol_3, held, other, ch, (up,))

    got = exchange(prod, "filter")
    near_steps, cross = list(range(2, mid)), list(range(mid, nf))
    mixed = assemble(own, None, some(got, [0, 1]), [0, 1])
    mixed = assemble(own, mixed, some(got, near_steps), near_steps)
    mixed, near, far = assemble_last(own, odd, mixed, some(got, cross), cross, planes)
    near, far = halo(near, far)

    taps = kernel_taps.T
    pad = pltpu.VMEM((planes + 2, height + 2, WW, ch), F32)

    def grad_shapes(g):
        return (
            jax.ShapeDtypeStruct((len(g), flat, ch), BF),
            jax.ShapeDtypeStruct((ch, len(g) * flat), BF),
        )

    edge = jax.ShapeDtypeStruct((flat, ch), BF)
    grad_middle, out_middle = call(
        functools.partial(forward_middle, middle, planes), grad_shapes(middle), [pad],
        mixed, taps, vol, up, us=4.0,
    )
    grad_edges, out_edges, to_near, to_far = call(
        functools.partial(forward_edges, planes), grad_shapes(edges) + (edge, edge), [pad],
        odd, mixed, near, far, taps, vol, up, us=4.0, after=(grad_middle,),
    )
    grad_near, grad_far = halo(to_near, to_far)
    where = {p: (i, k) for i, g in enumerate(groups) for k, p in enumerate(g)}
    mg_middle = call(
        functools.partial(backward_middle, middle, where, planes),
        jax.ShapeDtypeStruct((len(middle), flat, ch), BF), [pad],
        grad_edges, grad_middle, taps, us=2.3,
    )
    steps = [0, 1] + cross
    whole, *send = call(
        functools.partial(backward_edges, where, planes, steps),
        [jax.ShapeDtypeStruct((total, ch), BF)] + [jax.ShapeDtypeStruct((blk, ch), BF)] * len(steps),
        [pad], own, odd, grad_edges, grad_middle, grad_near, grad_far, taps, mg_middle, us=2.8,
    )
    got = {s: swap(block, "filter", s) if s else block for s, block in zip(steps, send)}

    wide = ch % 128 == 0
    side = some(got, [0, 1])
    shapes = (jax.ShapeDtypeStruct((32, ch), F32), jax.ShapeDtypeStruct((ch, total), BF))
    shapes += (jax.ShapeDtypeStruct((blk, nf * ch), BF),) if wide else ()
    kernel = functools.partial(taps_kernel, where, planes, norm, [0, 1] if wide else [])
    taps_grad, output, *mg = call(
        kernel, shapes, [pad, pad],
        odd, mixed, near, far, grad_edges, grad_middle, out_edges, out_middle,
        *(side if wide else []), us=5.8,
    )
    output = output.reshape(ch, planes, flat)
    send = blocks(own, whole, blk, near_steps, (taps_grad,))
    got.update((s, swap(block, "filter", s)) for s, block in zip(near_steps, send))
    base = mg[0] if wide else dict(zip([0, 1], side))
    rest = cross + near_steps
    mg_all, back = unmix(
        turn, base, some(got, rest), rest, held, other, ch, ()
    )
    got = exchange(back, "filter")
    mine, theirs = weight_products(mg_all, vol_t, taps_grad, ch, norm, ns)
    volume_grad_1 = finish(own, up, None, some(got, early), early)
    volume_grad_2 = finish(own, up, volume_grad_1, some(got, later), later)
    mixing_grad, taps_grad = scatter_rest(
        mine, theirs, taps_grad, ch, volume_grad_1, volume_grad_2
    )
    volume_grad = finish(own, up, volume_grad_2, some(got, last), last)
    volume_grad = volume_grad.reshape(ch, planes, flat)
    return (output, volume_grad, mixing_grad, taps_grad[:27].T)


def solution(mesh):
    in_specs = (
        P("filter", "space", None),
        P("filter", None),
        P("filter", None),
        P("filter", "space", None),
    )
    out_specs = (
        P("filter", "space", None),
        P("filter", "space", None),
        P("filter", "space"),
        P("filter", None),
    )
    return jax.shard_map(body, mesh=mesh, in_specs=in_specs, out_specs=out_specs, check_vma=False)
```

```python
import functools
import math

import jax
import jax.numpy as jnp
from jax import lax
from jax.experimental import pallas as pl
from jax.experimental.pallas import tpu as pltpu
from jax.sharding import PartitionSpec as P

WW = 64
BF = jnp.bfloat16
F32 = jnp.float32


def swap(block, axis, step):
    size = lax.axis_size(axis)
    return lax.ppermute(block, axis, [(i, i ^ step) for i in range(size)])


def exchange(pieces, axis):
    size = len(pieces)
    order = list(range(size // 2, size)) + list(range(1, size // 2))
    got = {0: pieces[0]}
    for s in order:
        got[s] = swap(pieces[s], axis, s)
    return [got[s] for s in range(size)]


def place(pieces, shift):
    out = jnp.zeros((len(pieces),) + pieces[0].shape, pieces[0].dtype)
    for s, piece in enumerate(pieces):
        out = lax.dynamic_update_index_in_dim(out, piece, shift ^ s, 0)
    return out


def pick(blocks, index):
    return lax.dynamic_index_in_dim(blocks, index, 0, keepdims=False)


def join(parts, after, us=0.4):
    def kernel(*refs):
        for k in range(len(parts)):
            refs[-1][k] = refs[k][...]

    shape = jax.ShapeDtypeStruct((len(parts),) + parts[0].shape, parts[0].dtype)
    return call(kernel, shape, [], *parts, us=us, after=after)


def gather_weights(mixing, me_space, send, first_in, second_in):
    rows, cols = mixing.shape
    nf, ns = lax.axis_size("filter"), lax.axis_size("space")
    share, pairs = cols // ns, ns // 2
    own = lax.dynamic_slice_in_dim(mixing, me_space * share, share, axis=1)
    even = join([own] + [swap(own, "filter", s) for s in range(2, nf, 2)], send[nf // 2 :])
    first = [even] + [swap(even, "space", s) for s in range(2, ns, 2)]
    odd = join([swap(even, "filter", 1)], (first_in,))[0]
    second = [odd] + [swap(odd, "space", s) for s in range(2, ns, 2)]

    def kernel(*refs):
        for k in range(pairs):
            for r in range(nf):
                source = refs[pairs * (r % 2) + k]
                refs[-1][k, r * rows : (r + 1) * rows, :] = source[r // 2]

    shape = jax.ShapeDtypeStruct((pairs, nf * rows, share), BF)
    held = call(kernel, shape, [], *first, *second, us=0.6, after=(second_in,))
    return held, swap(held, "space", 1)


def halved(ch, share, ns):
    return ns == 4 and share == 2 * ch and ch % 128 == 0


def halves_first(rows, nf, mine0, mine1, got, taps, a_keep, a_send, b_keep, b_next, b_send, sums):
    h, count = a_keep.shape[1], taps.shape[0]
    total = joined(*split(taps[...])) + joined(got[0, nf * rows :, :h], got[1, nf * rows :, :h])
    high, low = split(total)
    a_send[nf * rows : nf * rows + count, :] = high
    a_send[nf * rows + count :, :] = low
    sums[...] = joined(high, low)
    for r in range(nf):
        row = slice(r * rows, (r + 1) * rows)
        own = mine0[row, :] + got[0, row, :].astype(F32)
        step = mine1[row, :] + got[1, row, :].astype(F32)
        a_keep[row, :] = own[:, :h]
        a_send[row, :] = step[:, :h].astype(BF)
        if r % 2:
            b_send[0, r // 2] = own[:, h:].astype(BF)
            b_send[1, r // 2] = step[:, h:].astype(BF)
        else:
            b_keep[r // 2] = own[:, h:]
            b_next[r // 2] = step[:, h:]


def halves_second(rows, nf, a_keep, a_got, b_keep, b_next, b_got, sums, near, a_send, far, b_send, taps):
    count = taps.shape[0]
    high, low = a_got[nf * rows : nf * rows + count, :], a_got[nf * rows + count :, :]
    taps[...] = sums[...] + joined(high, low)
    for r in range(nf):
        row = slice(r * rows, (r + 1) * rows)
        own = a_keep[row, :] + a_got[row, :].astype(F32)
        if r % 2:
            a_send[r // 2] = own.astype(BF)
        else:
            near[r // 2] = own
    far[...] = b_keep[...] + b_got[0].astype(F32)
    b_send[...] = (b_next[...] + b_got[1].astype(F32)).astype(BF)


def halves_third(near, a_got, far, b_got, keep, *send):
    h = near.shape[2]
    for k in range(near.shape[0]):
        left = near[k] + a_got[k].astype(F32)
        right = far[k] + b_got[k].astype(F32)
        if k:
            send[k - 1][:, :h] = left.astype(BF)
            send[k - 1][:, h:] = right.astype(BF)
        else:
            keep[:, :h] = left
            keep[:, h:] = right


def scatter_rest(mine, theirs, taps, rows, first_in, second_in):
    nf, ns = lax.axis_size("filter"), lax.axis_size("space")
    pairs, share = ns // 2, theirs.shape[2]
    theirs = swap(theirs, "space", 1)
    if halved(rows, share, ns):
        h, n, count = share // 2, nf // 2, taps.shape[0]
        shapes = (
            jax.ShapeDtypeStruct((nf * rows, h), F32),
            jax.ShapeDtypeStruct((nf * rows + 2 * count, h), BF),
            jax.ShapeDtypeStruct((n, rows, h), F32), jax.ShapeDtypeStruct((n, rows, h), F32),
            jax.ShapeDtypeStruct((2, n, rows, h), BF), jax.ShapeDtypeStruct((count, h), F32),
        )
        kernel = functools.partial(halves_first, rows, nf)
        a_keep, a_send, b_keep, b_next, b_send, sums = call(
            kernel, shapes, [], *mine, theirs, taps, us=0.8
        )
        a_got = swap(a_send, "space", 2)
        b_got = swap(b_send, "filter", 1)
        shapes = (
            jax.ShapeDtypeStruct((n, rows, h), F32), jax.ShapeDtypeStruct((n, rows, h), BF),
            jax.ShapeDtypeStruct((n, rows, h), F32), jax.ShapeDtypeStruct((n, rows, h), BF),
            jax.ShapeDtypeStruct((count, h), F32),
        )
        kernel = functools.partial(halves_second, rows, nf)
        near, a_send, far, b_send, taps = call(
            kernel, shapes, [], a_keep, a_got, b_keep, b_next, b_got, sums,
            us=0.6, after=(first_in,),
        )
        a_got = swap(a_send, "filter", 1)
        b_got = swap(b_send, "space", 2)
        shapes = [jax.ShapeDtypeStruct((rows, share), F32)]
        shapes += [jax.ShapeDtypeStruct((rows, share), BF)] * (n - 1)
        keep, *rest = call(
            halves_third, shapes, [], near, a_got, far, b_got, us=0.5, after=(second_in,)
        )
    else:
        step = 1
        while step < ns:
            taps = taps + swap(taps, "space", step)
            step *= 2
        total = mine[0] + theirs[0].astype(F32)
        for k in range(1, pairs):
            send = (mine[k] + theirs[k].astype(F32)).astype(BF)
            total = total + swap(send, "space", 2 * k).astype(F32)
        total = total.reshape(nf // 2, 2, rows, share)
        near = total[:, 0] + swap(total[:, 1].astype(BF), "filter", 1).astype(F32)
        keep, rest = near[0], [near[k].astype(BF) for k in range(1, nf // 2)]
    for k, part in enumerate(rest):
        keep = keep + swap(part, "filter", 2 * (k + 1)).astype(F32)
    return keep, taps


def halo(near, far):
    size = lax.axis_size("space")
    inner = [(i, i ^ 1) for i in range(size)]
    outer = [(i, ((i + 1) ^ 1) - 1) for i in range(1, size - 1)]
    far = lax.ppermute(far, "space", outer)
    return lax.ppermute(near, "space", inner), far


def fill(pad_ref, plane, source):
    rows, width, ch = pad_ref.shape[1] - 2, pad_ref.shape[2], pad_ref.shape[3]
    pad_ref[plane, 1 : rows + 1] = source.astype(F32).reshape(rows, width, ch)
    pad_ref[plane, 0] = jnp.zeros((width, ch), F32)
    pad_ref[plane, rows + 1] = jnp.zeros((width, ch), F32)


def shifted(value, up):
    width = value.shape[0]
    index = lax.broadcasted_iota(jnp.int32, value.shape, 0)
    if up:
        return jnp.where(index == width - 1, 0.0, pltpu.roll(value, width - 1, 0))
    return jnp.where(index == 0, 0.0, pltpu.roll(value, 1, 0))


def conv_row(pad_ref, taps_ref, plane, row, flip):
    sums = [None, None, None]
    for a in range(3):
        for b in range(3):
            da, db = (1 - a, 1 - b) if flip else (a - 1, b - 1)
            line = pad_ref[plane + da, row + db]
            for e in range(3):
                term = taps_ref[pl.ds(a * 9 + b * 3 + e, 1), :] * line
                sums[e] = term if sums[e] is None else sums[e] + term
    lo, hi = (sums[2], sums[0]) if flip else (sums[0], sums[2])
    return sums[1] + shifted(lo, False) + shifted(hi, True)


def load_planes(pad_ref, refs, where, sides, wanted, planes):
    for p in sorted(wanted):
        if p < 0:
            fill(pad_ref, 0, jnp.where(sides[0][0] == 1, sides[1][...], sides[2][...]))
        elif p >= planes:
            fill(pad_ref, planes + 1, jnp.where(sides[0][0] == 1, sides[2][...], sides[1][...]))
        else:
            which, at = where[p]
            fill(pad_ref, p + 1, refs[which][at])


def forward_planes(group, planes, sides, m, taps, up, grad, silu, pad):
    wanted = {p + a for p in group for a in (-1, 0, 1)}
    where = {p: (0, p) for p in range(planes)}
    load_planes(pad, (m,), where, sides, wanted, planes)
    lanes, flat = 2 * WW, m.shape[1]
    for k, p in enumerate(group):

        def strip(f, carry, k=k, p=p):
            lines = [conv_row(pad, taps, p + 1, f * 2 + 1 + r, False) for r in range(2)]
            spatial = jnp.concatenate(lines, axis=0)
            sig = 1.0 / (1.0 + jnp.exp(-spatial))
            cells = pl.ds(pl.multiple_of(f * lanes, lanes), lanes)
            source = pl.ds(pl.multiple_of(p * flat + f * lanes, lanes), lanes)
            slope = sig * (1.0 + spatial * (1.0 - sig))
            grad[k, cells, :] = (up[source, :].astype(F32) * slope).astype(BF)
            silu[k, cells, :] = spatial * sig
            return carry

        lax.fori_loop(0, flat // lanes, strip, 0)


def forward_middle(group, planes, m, taps, up, grad, silu, pad):
    forward_planes(group, planes, (), m, taps, up, grad, silu, pad)


def forward_edges(planes, odd, m, near, far, taps, up, grad, silu, to_near, to_far, pad):
    sides = (odd, near, far)
    forward_planes((0, planes - 1), planes, sides, m, taps, up, grad, silu, pad)
    to_near[...] = jnp.where(odd[0] == 1, grad[0], grad[1])
    to_far[...] = jnp.where(odd[0] == 1, grad[1], grad[0])


def backward_planes(group, where, planes, sides, g0, g1, taps, put, pad):
    wanted = {p + a for p in group for a in (-1, 0, 1)}
    load_planes(pad, (g0, g1), where, sides, wanted, planes)
    lanes, flat = 2 * WW, g0.shape[1]
    for k, p in enumerate(group):

        def strip(f, carry, k=k, p=p):
            lines = [conv_row(pad, taps, p + 1, f * 2 + 1 + r, True) for r in range(2)]
            put(k, p, pl.multiple_of(f * lanes, lanes), jnp.concatenate(lines, axis=0).astype(BF))
            return carry

        lax.fori_loop(0, flat // lanes, strip, 0)


def backward_middle(group, where, planes, g0, g1, taps, out, pad):
    def put(k, p, cell, value):
        out[k, pl.ds(cell, value.shape[0]), :] = value

    backward_planes(group, where, planes, (), g0, g1, taps, put, pad)


def backward_edges(where, planes, steps, me, odd, g0, g1, near, far, taps, inner, whole, *refs):
    out, pad = refs[:-1], refs[-1]
    flat = g0.shape[1]

    def put(k, p, cell, value):
        whole[pl.ds(p * flat + cell, value.shape[0]), :] = value

    backward_planes((0, planes - 1), where, planes, (odd, near, far), g0, g1, taps, put, pad)
    for k in range(1, planes - 1):
        whole[k * flat : (k + 1) * flat, :] = inner[k - 1]
    blk = out[0].shape[0]
    for s, block in zip(steps, out):
        block[...] = whole[pl.ds(pl.multiple_of((me[0] ^ s) * blk, blk), blk), :]


def blocks(me, whole, blk, steps, after):
    def kernel(me, whole, *out):
        for s, block in zip(steps, out):
            block[...] = whole[pl.ds(pl.multiple_of((me[0] ^ s) * blk, blk), blk), :]

    shapes = [jax.ShapeDtypeStruct((blk, whole.shape[1]), BF)] * len(steps)
    return call(kernel, shapes, [], me, whole, us=0.3, after=after)


def taps_kernel(where_grad, planes, norm, steps, odd, m, near, far, g0, g1, s0, s1, vol, *refs):
    parts, refs = refs[: len(steps)], refs[len(steps) :]
    out, output, pad, gpad = refs[0], refs[1], refs[-2], refs[-1]
    for r, part in zip(steps, parts):
        refs[2][:, r * part.shape[1] : (r + 1) * part.shape[1]] = part[...]
    flat, lanes = m.shape[1], 2 * WW
    for p in range(planes):
        which, at = where_grad[p]
        silu = (s0, s1)[which]

        def strip(f, carry, p=p, at=at, silu=silu):
            cells = pl.ds(pl.multiple_of(f * lanes, lanes), lanes)
            lane = pl.ds(pl.multiple_of(p * flat + f * lanes, lanes), lanes)
            turned = jnp.transpose(silu[at, cells, :])
            output[:, lane] = (vol[:, lane].astype(F32) + turned).astype(BF)
            return carry

        lax.fori_loop(0, flat // lanes, strip, 0)
    where = {p: (0, p) for p in range(planes)}
    load_planes(pad, (m,), where, (odd, near, far), range(-1, planes + 1), planes)
    load_planes(gpad, (g0, g1), where_grad, (), range(planes), planes)
    rows, width, ch = pad.shape[1] - 2, pad.shape[2], pad.shape[3]
    sums = tuple(jnp.zeros((8, ch), F32) for _ in range(27))

    def line(at, sums):
        p, h = at // rows, at % rows
        sums = list(sums)
        own = gpad[p + 1, h + 1]
        turned = (shifted(own, True), own, shifted(own, False))
        for a in range(3):
            for b in range(3):
                field = pad[p + a, h + b]
                for e in range(3):
                    prod = (turned[e] * field).reshape(width // 8, 8, ch)
                    sums[a * 9 + b * 3 + e] = sums[a * 9 + b * 3 + e] + jnp.sum(prod, axis=0)
        return tuple(sums)

    sums = lax.fori_loop(0, planes * rows, line, sums)
    for k in range(27):
        out[k : k + 1, :] = jnp.sum(sums[k], axis=0, keepdims=True) * norm
    out[27:, :] = jnp.zeros((5, ch), F32)


def call(kernel, out_shape, scratch, *args, us=1.0, after=(), alias=None):
    specs = [
        pl.BlockSpec(memory_space=pltpu.SMEM if arg.dtype == jnp.int32 else pltpu.VMEM)
        for arg in args
    ]

    def wrapped(*refs):
        kernel(*refs[: len(args)], *refs[len(args) + len(after) :])

    return pl.pallas_call(
        wrapped,
        out_shape=out_shape,
        in_specs=specs + [pl.BlockSpec(memory_space=pl.ANY)] * len(after),
        out_specs=jax.tree.map(lambda _: pl.BlockSpec(memory_space=pltpu.VMEM), out_shape),
        scratch_shapes=scratch,
        input_output_aliases={} if alias is None else {alias: 0},
        compiler_params=pltpu.CompilerParams(vmem_limit_bytes=32 * 1024 * 1024),
        cost_estimate=pl.CostEstimate(
            flops=int(us * 1.15e9), bytes_accessed=1024 * 1024, transcendentals=0
        ),
    )(*args, *after)


def in_place(kernel, shape, leading, base, pieces, us):
    if base is None:
        return call(kernel, shape, [], *leading, *pieces, us=us)

    def wrapped(*refs):
        kernel(*refs[: len(leading)], *refs[len(leading) + 1 :])

    return call(wrapped, shape, [], *leading, base, *pieces, us=us, alias=len(leading))


def fold_volume(turn, base, pieces, steps):
    nf, (ch, blk) = lax.axis_size("filter"), pieces[0].shape
    if ch % 128:
        out = jnp.zeros((nf, ch, blk), BF) if base is None else base
        for t, piece in zip(steps, pieces):
            out = lax.dynamic_update_index_in_dim(out, piece, turn[0] ^ t, 0)
        return out

    def kernel(turn, *refs):
        for t, piece in zip(steps, refs[:-1]):
            lane = pl.ds(pl.multiple_of((turn[0] ^ t) * ch, 128), ch)
            refs[-1][:, lane] = jnp.transpose(piece[...])

    shape = jax.ShapeDtypeStruct((blk, nf * ch), BF)
    return in_place(kernel, shape, (turn,), base, pieces, 0.3 * len(pieces))


def mix_kernel(held, other, vol_t, *out):
    nf, ch, share = len(out), out[0].shape[1], held.shape[2]
    for s in range(0, nf, 2):
        total = None
        for v in range(2 * held.shape[0]):
            block = (other if v % 2 else held)[v // 2, s * ch : (s + 2) * ch, :]
            term = lax.dot_general(
                vol_t[:, v * share : (v + 1) * share], block, (((1,), (1,)), ((), ())),
                preferred_element_type=F32,
            )
            total = term if total is None else total + term
        out[s][...] = total[:, :ch].astype(BF)
        out[s + 1][...] = total[:, ch:].astype(BF)


def mix(vol, held, other, ch, after):
    pairs, rows, share = held.shape
    nf = rows // ch
    if ch % 128:
        vol_t = vol.reshape(rows, vol.shape[2]).T
        weights = jnp.stack([held, other], axis=1).reshape(2 * pairs, rows, share)
        out = jnp.einsum(
            "cvi,voi->co", vol_t.reshape(-1, 2 * pairs, share), weights, preferred_element_type=F32
        ).astype(BF)
        return vol_t, [out[:, s * ch : (s + 1) * ch] for s in range(nf)]
    shapes = [jax.ShapeDtypeStruct((vol.shape[0], ch), BF)] * nf
    return vol, call(mix_kernel, shapes, [], held, other, vol, us=2.6, after=after)


def turned(field):
    def kernel(field, out):
        step = 2 * WW

        def strip(f, carry):
            cells = pl.ds(pl.multiple_of(f * step, step), step)
            out[cells, :] = jnp.transpose(field[:, cells])
            return carry

        lax.fori_loop(0, field.shape[1] // step, strip, 0)

    return call(kernel, jax.ShapeDtypeStruct(field.shape[::-1], BF), [], field, us=1.2)


def unmix(turn, mg, held, other, ch):
    blk = mg.shape[0]
    pairs, rows, share = held.shape
    nf = rows // ch
    if ch % 128:
        weights = jnp.stack([held, other], axis=1).reshape(2 * pairs, rows, share)
        out = jnp.einsum("co,voi->vic", mg, weights, preferred_element_type=F32)
        out = out.astype(BF).reshape(nf, ch, blk)
        return [pick(out, turn[0] ^ s) for s in range(nf)]

    def kernel(turn, mg, held, other, *refs):
        out, back = refs[:-1], refs[-1]
        for v in range(2 * pairs):
            block = (other if v % 2 else held)[v // 2]
            total = lax.dot_general(
                mg[...], block, (((1,), (0,)), ((), ())), preferred_element_type=F32
            )
            turned = jnp.transpose(total).astype(BF)
            for k in range(share // ch):
                back[v * (share // ch) + k] = turned[k * ch : (k + 1) * ch, :]
        for s in range(nf):
            out[s][...] = back[turn[0] ^ s]

    shapes = [jax.ShapeDtypeStruct((ch, blk), BF)] * nf
    return call(
        kernel, shapes, [pltpu.VMEM((nf, ch, blk), BF)], turn, mg, held, other, us=2.2
    )


def split(value):
    high = value.astype(BF)
    return high, (value - high.astype(F32)).astype(BF)


def joined(high, low):
    return high.astype(F32) + low.astype(F32)


def weight_products(base, pieces, steps, vol_t, taps, ch, norm, ns):
    rows, pairs = vol_t.shape[1], ns // 2
    share = rows // ns
    if halved(ch, share, ns):
        count = taps.shape[0]

        def kernel(base, vol, taps, *refs):
            parts, mg, mine, theirs = refs[: len(steps)], refs[len(steps)], refs[-1 - pairs : -1], refs[-1]
            mg[...] = base[...]
            for r, part in zip(steps, parts):
                mg[:, r * ch : (r + 1) * ch] = part[...]
            for r in range(rows // ch):
                row = slice(r * ch, (r + 1) * ch)
                turned = jnp.transpose(mg[:, row])
                for v in range(ns):
                    total = norm * lax.dot_general(
                        turned, vol[:, v * share : (v + 1) * share], (((1,), (0,)), ((), ())),
                        preferred_element_type=F32,
                    )
                    if v % 2:
                        theirs[v // 2, row, :] = total.astype(BF)
                    else:
                        mine[v // 2][row, :] = total
            high, low = split(taps[...])
            theirs[0, rows:, :ch] = high
            theirs[1, rows:, :ch] = low

        shapes = [jax.ShapeDtypeStruct(vol_t.shape, BF)]
        shapes += [jax.ShapeDtypeStruct((rows, share), F32)] * pairs
        shapes.append(jax.ShapeDtypeStruct((pairs, rows + count, share), BF))
        got = call(kernel, shapes, [], base, vol_t, taps, *pieces, us=2.5)
        return got[0], got[1:-1], got[-1]
    if isinstance(base, dict):
        parts = {**base, **dict(zip(steps, pieces))}
        mg = jnp.concatenate([parts[r] for r in sorted(parts)], axis=1)
    else:
        mg = base
        for r, part in zip(steps, pieces):
            mg = lax.dynamic_update_slice_in_dim(mg, part, r * ch, axis=1)
    part = lax.dot_general(mg, vol_t, (((0,), (0,)), ((), ())), preferred_element_type=F32)
    part = (part * norm).reshape(rows, pairs, 2, share)
    theirs = part[:, :, 1].transpose(1, 0, 2).astype(BF)
    return mg, [part[:, k, 0] for k in range(pairs)], theirs


def assemble(me, base, pieces, steps):
    blk, ch = pieces[0].shape

    def kernel(me, *refs):
        for s, piece in zip(steps, refs[:-1]):
            refs[-1][me[0] ^ s] = piece[...]

    shape = jax.ShapeDtypeStruct((lax.axis_size("filter"), blk, ch), BF)
    return in_place(kernel, shape, (me,), base, pieces, 0.5)


def assemble_last(me, odd, base, pieces, steps, planes):
    nf, blk, ch = base.shape
    flat = nf * blk // planes

    def kernel(me, odd, base, *refs):
        out, near, far = refs[-3:]
        for s, piece in zip(steps, refs[:-3]):
            out[me[0] ^ s] = piece[...]
        for k in range(flat // blk):
            first, last = out[k], out[nf - flat // blk + k]
            near[k * blk : (k + 1) * blk, :] = jnp.where(odd[0] == 1, first, last)
            far[k * blk : (k + 1) * blk, :] = jnp.where(odd[0] == 1, last, first)

    edge = jax.ShapeDtypeStruct((flat, ch), BF)
    shapes = (jax.ShapeDtypeStruct((nf, blk, ch), BF), edge, edge)
    out, near, far = call(kernel, shapes, [], me, odd, base, *pieces, us=0.8, alias=2)
    return out.reshape(planes, flat, ch), near, far


def finish(me, up, base, pieces, steps):
    blk = pieces[0].shape[1]

    def kernel(me, up, *refs):
        for s, piece in zip(steps, refs[:-1]):
            lane = pl.ds(pl.multiple_of((me[0] ^ s) * blk, 128), blk)
            refs[-1][:, lane] = (up[:, lane].astype(F32) + piece[...].astype(F32)).astype(BF)

    shape = jax.ShapeDtypeStruct(up.shape, BF)
    return in_place(kernel, shape, (me, up), base, pieces, 0.25 * len(pieces))


def body(volume, mixing, kernel_taps, upstream):
    ch, planes, flat = volume.shape
    height = flat // WW
    nf, ns = lax.axis_size("filter"), lax.axis_size("space")
    me, me_space = lax.axis_index("filter"), lax.axis_index("space")
    total = planes * flat
    blk = total // nf
    norm = 1.0 / math.sqrt(ns * total)
    edges, middle = (0, planes - 1), tuple(range(1, planes - 1))
    groups = (edges, middle)
    turn = jnp.reshape(me ^ (me_space * (nf // ns)), (1,)).astype(jnp.int32)

    odd = jnp.reshape(me_space & 1, (1,)).astype(jnp.int32)
    own = jnp.reshape(me, (1,)).astype(jnp.int32)

    vol = volume.reshape(ch, total)
    mid = nf // 2
    early = [0, mid]
    later = [s for s in range(mid + 1, nf)]
    last = list(range(1, mid))

    def some(parts, steps):
        return [parts[s] for s in steps]

    send = [lax.dynamic_slice_in_dim(vol, (me ^ s) * blk, blk, axis=1) for s in range(nf)]
    pieces = exchange(send, "filter")
    steps = early + [mid + 1]
    vol_1 = fold_volume(turn, None, some(pieces, steps), steps)
    vol_2 = fold_volume(turn, vol_1, some(pieces, [mid + 2, 1]), [mid + 2, 1])
    rest = later[2:] + last[1:]
    vol_3 = fold_volume(turn, vol_2, some(pieces, rest), rest)
    held, other = gather_weights(mixing, me_space, send, vol_1, vol_2)
    up = upstream.reshape(ch, total)
    up_t = turned(up)
    vol_t, prod = mix(vol_3, held, other, ch, (up_t,))

    got = exchange(prod, "filter")
    near_steps, cross = list(range(2, mid)), list(range(mid, nf))
    mixed = assemble(own, None, some(got, [0, 1]), [0, 1])
    mixed = assemble(own, mixed, some(got, near_steps), near_steps)
    mixed, near, far = assemble_last(own, odd, mixed, some(got, cross), cross, planes)
    near, far = halo(near, far)

    taps = kernel_taps.T
    pad = pltpu.VMEM((planes + 2, height + 2, WW, ch), F32)

    def grad_shapes(g):
        return (
            jax.ShapeDtypeStruct((len(g), flat, ch), BF),
            jax.ShapeDtypeStruct((len(g), flat, ch), F32),
        )

    edge = jax.ShapeDtypeStruct((flat, ch), BF)
    grad_middle, silu_middle = call(
        functools.partial(forward_middle, middle, planes), grad_shapes(middle), [pad],
        mixed, taps, up_t, us=3.2,
    )
    grad_edges, silu_edges, to_near, to_far = call(
        functools.partial(forward_edges, planes), grad_shapes(edges) + (edge, edge), [pad],
        odd, mixed, near, far, taps, up_t, us=3.2, after=(grad_middle,),
    )
    grad_near, grad_far = halo(to_near, to_far)
    where = {p: (i, k) for i, g in enumerate(groups) for k, p in enumerate(g)}
    mg_middle = call(
        functools.partial(backward_middle, middle, where, planes),
        jax.ShapeDtypeStruct((len(middle), flat, ch), BF), [pad],
        grad_edges, grad_middle, taps, us=2.3,
    )
    steps = [0, 1] + cross
    whole, *send = call(
        functools.partial(backward_edges, where, planes, steps),
        [jax.ShapeDtypeStruct((total, ch), BF)] + [jax.ShapeDtypeStruct((blk, ch), BF)] * len(steps),
        [pad], own, odd, grad_edges, grad_middle, grad_near, grad_far, taps, mg_middle, us=2.8,
    )
    got = {s: swap(block, "filter", s) if s else block for s, block in zip(steps, send)}

    wide = ch % 128 == 0
    side = some(got, [0, 1])
    shapes = (jax.ShapeDtypeStruct((32, ch), F32), jax.ShapeDtypeStruct((ch, total), BF))
    shapes += (jax.ShapeDtypeStruct((blk, nf * ch), BF),) if wide else ()
    kernel = functools.partial(taps_kernel, where, planes, norm, [0, 1] if wide else [])
    taps_grad, output, *mg = call(
        kernel, shapes, [pad, pad],
        odd, mixed, near, far, grad_edges, grad_middle, silu_edges, silu_middle, vol,
        *(side if wide else []), us=5.8,
    )
    output = output.reshape(ch, planes, flat)
    send = blocks(own, whole, blk, near_steps, (taps_grad,))
    got.update((s, swap(block, "filter", s)) for s, block in zip(near_steps, send))
    base = mg[0] if wide else dict(zip([0, 1], side))
    rest = cross + near_steps
    mg_all, mine, theirs = weight_products(
        base, some(got, rest), rest, vol_t, taps_grad, ch, norm, ns
    )
    back = unmix(turn, mg_all, held, other, ch)
    got = exchange(back, "filter")
    volume_grad_1 = finish(own, up, None, some(got, [0, 1]), [0, 1])
    volume_grad_2 = finish(own, up, volume_grad_1, some(got, cross), cross)
    mixing_grad, taps_grad = scatter_rest(
        mine, theirs, taps_grad, ch, volume_grad_1, volume_grad_2
    )
    volume_grad = finish(own, up, volume_grad_2, some(got, near_steps), near_steps)
    volume_grad = volume_grad.reshape(ch, planes, flat)
    return (output, volume_grad, mixing_grad, taps_grad[:27].T)


def solution(mesh):
    in_specs = (
        P("filter", "space", None),
        P("filter", None),
        P("filter", None),
        P("filter", "space", None),
    )
    out_specs = (
        P("filter", "space", None),
        P("filter", "space", None),
        P("filter", "space"),
        P("filter", None),
    )
    return jax.shard_map(body, mesh=mesh, in_specs=in_specs, out_specs=out_specs, check_vma=False)
```

```python
import functools
import math

import jax
import jax.numpy as jnp
from jax import lax
from jax.experimental import pallas as pl
from jax.experimental.pallas import tpu as pltpu
from jax.sharding import PartitionSpec as P

WW = 64
BF = jnp.bfloat16
F32 = jnp.float32


def swap(block, axis, step):
    size = lax.axis_size(axis)
    return lax.ppermute(block, axis, [(i, i ^ step) for i in range(size)])


def exchange(pieces, axis):
    size = len(pieces)
    order = list(range(size // 2, size)) + list(range(1, size // 2))
    got = {0: pieces[0]}
    for s in order:
        got[s] = swap(pieces[s], axis, s)
    return [got[s] for s in range(size)]


def place(pieces, shift):
    out = jnp.zeros((len(pieces),) + pieces[0].shape, pieces[0].dtype)
    for s, piece in enumerate(pieces):
        out = lax.dynamic_update_index_in_dim(out, piece, shift ^ s, 0)
    return out


def pick(blocks, index):
    return lax.dynamic_index_in_dim(blocks, index, 0, keepdims=False)


def join(parts, after, us=0.4):
    def kernel(*refs):
        for k in range(len(parts)):
            refs[-1][k] = refs[k][...]

    shape = jax.ShapeDtypeStruct((len(parts),) + parts[0].shape, parts[0].dtype)
    return call(kernel, shape, [], *parts, us=us, after=after)


def gather_weights(mixing, me_space, send, arrived):
    rows, cols = mixing.shape
    nf, ns = lax.axis_size("filter"), lax.axis_size("space")
    share, pairs = cols // ns, ns // 2
    own = lax.dynamic_slice_in_dim(mixing, me_space * share, share, axis=1)
    even = join([own] + [swap(own, "filter", s) for s in range(2, nf, 2)], send[nf // 2 :])
    first = [even] + [swap(even, "space", s) for s in range(2, ns, 2)]
    odd = swap(even, "filter", 1)
    second = [odd] + [swap(odd, "space", s) for s in range(2, ns, 2)]

    def kernel(*refs):
        for k in range(pairs):
            for r in range(nf):
                source = refs[pairs * (r % 2) + k]
                refs[-1][k, r * rows : (r + 1) * rows, :] = source[r // 2]

    shape = jax.ShapeDtypeStruct((pairs, nf * rows, share), BF)
    held = call(kernel, shape, [], *first, *second, us=0.6, after=(arrived,))
    return held, swap(held, "space", 1)


def halved(ch, share, ns):
    return ns == 4 and share == 2 * ch and ch % 128 == 0


def halves_first(rows, nf, mine0, mine1, got, taps, a_keep, a_send, b_keep, b_next, b_send, sums):
    h, count = a_keep.shape[1], taps.shape[0]
    total = joined(*split(taps[...])) + joined(got[0, nf * rows :, :h], got[1, nf * rows :, :h])
    high, low = split(total)
    a_send[nf * rows : nf * rows + count, :] = high
    a_send[nf * rows + count :, :] = low
    sums[...] = joined(high, low)
    for r in range(nf):
        row = slice(r * rows, (r + 1) * rows)
        own = mine0[row, :] + got[0, row, :].astype(F32)
        step = mine1[row, :] + got[1, row, :].astype(F32)
        a_keep[row, :] = own[:, :h]
        a_send[row, :] = step[:, :h].astype(BF)
        if r % 2:
            b_send[0, r // 2] = own[:, h:].astype(BF)
            b_send[1, r // 2] = step[:, h:].astype(BF)
        else:
            b_keep[r // 2] = own[:, h:]
            b_next[r // 2] = step[:, h:]


def halves_second(rows, nf, a_keep, a_got, b_keep, b_next, b_got, sums, near, a_send, far, b_send, taps):
    count = taps.shape[0]
    high, low = a_got[nf * rows : nf * rows + count, :], a_got[nf * rows + count :, :]
    taps[...] = sums[...] + joined(high, low)
    for r in range(nf):
        row = slice(r * rows, (r + 1) * rows)
        own = a_keep[row, :] + a_got[row, :].astype(F32)
        if r % 2:
            a_send[r // 2] = own.astype(BF)
        else:
            near[r // 2] = own
    far[...] = b_keep[...] + b_got[0].astype(F32)
    b_send[...] = (b_next[...] + b_got[1].astype(F32)).astype(BF)


def halves_third(near, a_got, far, b_got, keep, *send):
    h = near.shape[2]
    for k in range(near.shape[0]):
        left = near[k] + a_got[k].astype(F32)
        right = far[k] + b_got[k].astype(F32)
        if k:
            send[k - 1][:, :h] = left.astype(BF)
            send[k - 1][:, h:] = right.astype(BF)
        else:
            keep[:, :h] = left
            keep[:, h:] = right


def scatter_rest(mine, theirs, taps, rows, first_in, second_in):
    nf, ns = lax.axis_size("filter"), lax.axis_size("space")
    pairs, share = ns // 2, theirs.shape[2]
    theirs = swap(theirs, "space", 1)
    if halved(rows, share, ns):
        h, n, count = share // 2, nf // 2, taps.shape[0]
        shapes = (
            jax.ShapeDtypeStruct((nf * rows, h), F32),
            jax.ShapeDtypeStruct((nf * rows + 2 * count, h), BF),
            jax.ShapeDtypeStruct((n, rows, h), F32), jax.ShapeDtypeStruct((n, rows, h), F32),
            jax.ShapeDtypeStruct((2, n, rows, h), BF), jax.ShapeDtypeStruct((count, h), F32),
        )
        kernel = functools.partial(halves_first, rows, nf)
        a_keep, a_send, b_keep, b_next, b_send, sums = call(
            kernel, shapes, [], *mine, theirs, taps, us=0.8
        )
        a_got = swap(a_send, "space", 2)
        b_got = swap(b_send, "filter", 1)
        shapes = (
            jax.ShapeDtypeStruct((n, rows, h), F32), jax.ShapeDtypeStruct((n, rows, h), BF),
            jax.ShapeDtypeStruct((n, rows, h), F32), jax.ShapeDtypeStruct((n, rows, h), BF),
            jax.ShapeDtypeStruct((count, h), F32),
        )
        kernel = functools.partial(halves_second, rows, nf)
        near, a_send, far, b_send, taps = call(
            kernel, shapes, [], a_keep, a_got, b_keep, b_next, b_got, sums,
            us=0.6, after=(first_in,),
        )
        a_got = swap(a_send, "filter", 1)
        b_got = swap(b_send, "space", 2)
        shapes = [jax.ShapeDtypeStruct((rows, share), F32)]
        shapes += [jax.ShapeDtypeStruct((rows, share), BF)] * (n - 1)
        keep, *rest = call(
            halves_third, shapes, [], near, a_got, far, b_got, us=0.5, after=(second_in,)
        )
    else:
        step = 1
        while step < ns:
            taps = taps + swap(taps, "space", step)
            step *= 2
        total = mine[0] + theirs[0].astype(F32)
        for k in range(1, pairs):
            send = (mine[k] + theirs[k].astype(F32)).astype(BF)
            total = total + swap(send, "space", 2 * k).astype(F32)
        total = total.reshape(nf // 2, 2, rows, share)
        near = total[:, 0] + swap(total[:, 1].astype(BF), "filter", 1).astype(F32)
        keep, rest = near[0], [near[k].astype(BF) for k in range(1, nf // 2)]
    for k, part in enumerate(rest):
        keep = keep + swap(part, "filter", 2 * (k + 1)).astype(F32)
    return keep, taps


def halo(near, far):
    size = lax.axis_size("space")
    inner = [(i, i ^ 1) for i in range(size)]
    outer = [(i, ((i + 1) ^ 1) - 1) for i in range(1, size - 1)]
    far = lax.ppermute(far, "space", outer)
    return lax.ppermute(near, "space", inner), far


def fill(pad_ref, plane, source):
    rows, width, ch = pad_ref.shape[1] - 2, pad_ref.shape[2], pad_ref.shape[3]
    pad_ref[plane, 1 : rows + 1] = source.astype(F32).reshape(rows, width, ch)
    pad_ref[plane, 0] = jnp.zeros((width, ch), F32)
    pad_ref[plane, rows + 1] = jnp.zeros((width, ch), F32)


def shifted(value, up):
    width = value.shape[0]
    index = lax.broadcasted_iota(jnp.int32, value.shape, 0)
    if up:
        return jnp.where(index == width - 1, 0.0, pltpu.roll(value, width - 1, 0))
    return jnp.where(index == 0, 0.0, pltpu.roll(value, 1, 0))


def conv_row(pad_ref, taps_ref, plane, row, flip):
    sums = [None, None, None]
    for a in range(3):
        for b in range(3):
            da, db = (1 - a, 1 - b) if flip else (a - 1, b - 1)
            line = pad_ref[plane + da, row + db]
            for e in range(3):
                term = taps_ref[pl.ds(a * 9 + b * 3 + e, 1), :] * line
                sums[e] = term if sums[e] is None else sums[e] + term
    lo, hi = (sums[2], sums[0]) if flip else (sums[0], sums[2])
    return sums[1] + shifted(lo, False) + shifted(hi, True)


def load_planes(pad_ref, refs, where, sides, wanted, planes):
    for p in sorted(wanted):
        if p < 0:
            fill(pad_ref, 0, jnp.where(sides[0][0] == 1, sides[1][...], sides[2][...]))
        elif p >= planes:
            fill(pad_ref, planes + 1, jnp.where(sides[0][0] == 1, sides[2][...], sides[1][...]))
        else:
            which, at = where[p]
            fill(pad_ref, p + 1, refs[which][at])


def forward_planes(group, planes, sides, m, taps, up, grad, silu, pad):
    wanted = {p + a for p in group for a in (-1, 0, 1)}
    where = {p: (0, p) for p in range(planes)}
    load_planes(pad, (m,), where, sides, wanted, planes)
    lanes, flat = 2 * WW, m.shape[1]
    for k, p in enumerate(group):

        def strip(f, carry, k=k, p=p):
            lines = [conv_row(pad, taps, p + 1, f * 2 + 1 + r, False) for r in range(2)]
            spatial = jnp.concatenate(lines, axis=0)
            sig = 1.0 / (1.0 + jnp.exp(-spatial))
            cells = pl.ds(pl.multiple_of(f * lanes, lanes), lanes)
            source = pl.ds(pl.multiple_of(p * flat + f * lanes, lanes), lanes)
            slope = sig * (1.0 + spatial * (1.0 - sig))
            grad[k, cells, :] = (up[source, :].astype(F32) * slope).astype(BF)
            silu[k, cells, :] = spatial * sig
            return carry

        lax.fori_loop(0, flat // lanes, strip, 0)


def forward_middle(group, planes, m, taps, up, grad, silu, pad):
    forward_planes(group, planes, (), m, taps, up, grad, silu, pad)


def forward_edges(planes, odd, m, near, far, taps, up, grad, silu, to_near, to_far, pad):
    sides = (odd, near, far)
    forward_planes((0, planes - 1), planes, sides, m, taps, up, grad, silu, pad)
    to_near[...] = jnp.where(odd[0] == 1, grad[0], grad[1])
    to_far[...] = jnp.where(odd[0] == 1, grad[1], grad[0])


def backward_planes(group, where, planes, sides, g0, g1, taps, put, pad):
    wanted = {p + a for p in group for a in (-1, 0, 1)}
    load_planes(pad, (g0, g1), where, sides, wanted, planes)
    lanes, flat = 2 * WW, g0.shape[1]
    for k, p in enumerate(group):

        def strip(f, carry, k=k, p=p):
            lines = [conv_row(pad, taps, p + 1, f * 2 + 1 + r, True) for r in range(2)]
            put(k, p, pl.multiple_of(f * lanes, lanes), jnp.concatenate(lines, axis=0).astype(BF))
            return carry

        lax.fori_loop(0, flat // lanes, strip, 0)


def backward_middle(group, where, planes, g0, g1, taps, out, pad):
    def put(k, p, cell, value):
        out[k, pl.ds(cell, value.shape[0]), :] = value

    backward_planes(group, where, planes, (), g0, g1, taps, put, pad)


def backward_edges(where, planes, steps, me, odd, g0, g1, near, far, taps, inner, whole, *refs):
    out, pad = refs[:-1], refs[-1]
    flat = g0.shape[1]

    def put(k, p, cell, value):
        whole[pl.ds(p * flat + cell, value.shape[0]), :] = value

    backward_planes((0, planes - 1), where, planes, (odd, near, far), g0, g1, taps, put, pad)
    for k in range(1, planes - 1):
        whole[k * flat : (k + 1) * flat, :] = inner[k - 1]
    blk = out[0].shape[0]
    for s, block in zip(steps, out):
        block[...] = whole[pl.ds(pl.multiple_of((me[0] ^ s) * blk, blk), blk), :]


def blocks(me, whole, blk, steps, after):
    def kernel(me, whole, *out):
        for s, block in zip(steps, out):
            block[...] = whole[pl.ds(pl.multiple_of((me[0] ^ s) * blk, blk), blk), :]

    shapes = [jax.ShapeDtypeStruct((blk, whole.shape[1]), BF)] * len(steps)
    return call(kernel, shapes, [], me, whole, us=0.3, after=after)


def taps_kernel(where_grad, planes, norm, steps, odd, m, near, far, g0, g1, s0, s1, vol, *refs):
    parts, refs = refs[: len(steps)], refs[len(steps) :]
    out, output, pad, gpad = refs[0], refs[1], refs[-2], refs[-1]
    for r, part in zip(steps, parts):
        refs[2][:, r * part.shape[1] : (r + 1) * part.shape[1]] = part[...]
    flat, lanes = m.shape[1], 2 * WW
    for p in range(planes):
        which, at = where_grad[p]
        silu = (s0, s1)[which]

        def strip(f, carry, p=p, at=at, silu=silu):
            cells = pl.ds(pl.multiple_of(f * lanes, lanes), lanes)
            lane = pl.ds(pl.multiple_of(p * flat + f * lanes, lanes), lanes)
            turned = jnp.transpose(silu[at, cells, :])
            output[:, lane] = (vol[:, lane].astype(F32) + turned).astype(BF)
            return carry

        lax.fori_loop(0, flat // lanes, strip, 0)
    where = {p: (0, p) for p in range(planes)}
    load_planes(pad, (m,), where, (odd, near, far), range(-1, planes + 1), planes)
    load_planes(gpad, (g0, g1), where_grad, (), range(planes), planes)
    rows, width, ch = pad.shape[1] - 2, pad.shape[2], pad.shape[3]
    sums = tuple(jnp.zeros((8, ch), F32) for _ in range(27))

    def line(at, sums):
        p, h = at // rows, at % rows
        sums = list(sums)
        own = gpad[p + 1, h + 1]
        turned = (shifted(own, True), own, shifted(own, False))
        for a in range(3):
            for b in range(3):
                field = pad[p + a, h + b]
                for e in range(3):
                    prod = (turned[e] * field).reshape(width // 8, 8, ch)
                    sums[a * 9 + b * 3 + e] = sums[a * 9 + b * 3 + e] + jnp.sum(prod, axis=0)
        return tuple(sums)

    sums = lax.fori_loop(0, planes * rows, line, sums)
    for k in range(27):
        out[k : k + 1, :] = jnp.sum(sums[k], axis=0, keepdims=True) * norm
    out[27:, :] = jnp.zeros((5, ch), F32)


def call(kernel, out_shape, scratch, *args, us=1.0, after=(), alias=None):
    specs = [
        pl.BlockSpec(memory_space=pltpu.SMEM if arg.dtype == jnp.int32 else pltpu.VMEM)
        for arg in args
    ]

    def wrapped(*refs):
        kernel(*refs[: len(args)], *refs[len(args) + len(after) :])

    return pl.pallas_call(
        wrapped,
        out_shape=out_shape,
        in_specs=specs + [pl.BlockSpec(memory_space=pl.ANY)] * len(after),
        out_specs=jax.tree.map(lambda _: pl.BlockSpec(memory_space=pltpu.VMEM), out_shape),
        scratch_shapes=scratch,
        input_output_aliases={} if alias is None else {alias: 0},
        compiler_params=pltpu.CompilerParams(vmem_limit_bytes=32 * 1024 * 1024),
        cost_estimate=pl.CostEstimate(
            flops=int(us * 1.15e9), bytes_accessed=1024 * 1024, transcendentals=0
        ),
    )(*args, *after)


def in_place(kernel, shape, leading, base, pieces, us):
    if base is None:
        return call(kernel, shape, [], *leading, *pieces, us=us)

    def wrapped(*refs):
        kernel(*refs[: len(leading)], *refs[len(leading) + 1 :])

    return call(wrapped, shape, [], *leading, base, *pieces, us=us, alias=len(leading))


def fold_volume(turn, base, pieces, steps):
    nf, (ch, blk) = lax.axis_size("filter"), pieces[0].shape
    if ch % 128:
        out = jnp.zeros((nf, ch, blk), BF) if base is None else base
        for t, piece in zip(steps, pieces):
            out = lax.dynamic_update_index_in_dim(out, piece, turn[0] ^ t, 0)
        return out

    def kernel(turn, *refs):
        for t, piece in zip(steps, refs[:-1]):
            lane = pl.ds(pl.multiple_of((turn[0] ^ t) * ch, 128), ch)
            refs[-1][:, lane] = jnp.transpose(piece[...])

    shape = jax.ShapeDtypeStruct((blk, nf * ch), BF)
    return in_place(kernel, shape, (turn,), base, pieces, 0.3 * len(pieces))


def mix_kernel(held, other, vol_t, *out):
    nf, ch, share = len(out), out[0].shape[1], held.shape[2]
    for s in range(0, nf, 2):
        total = None
        for v in range(2 * held.shape[0]):
            block = (other if v % 2 else held)[v // 2, s * ch : (s + 2) * ch, :]
            term = lax.dot_general(
                vol_t[:, v * share : (v + 1) * share], block, (((1,), (1,)), ((), ())),
                preferred_element_type=F32,
            )
            total = term if total is None else total + term
        out[s][...] = total[:, :ch].astype(BF)
        out[s + 1][...] = total[:, ch:].astype(BF)


def mix(vol, held, other, ch, after):
    pairs, rows, share = held.shape
    nf = rows // ch
    if ch % 128:
        vol_t = vol.reshape(rows, vol.shape[2]).T
        weights = jnp.stack([held, other], axis=1).reshape(2 * pairs, rows, share)
        out = jnp.einsum(
            "cvi,voi->co", vol_t.reshape(-1, 2 * pairs, share), weights, preferred_element_type=F32
        ).astype(BF)
        return vol_t, [out[:, s * ch : (s + 1) * ch] for s in range(nf)]
    shapes = [jax.ShapeDtypeStruct((vol.shape[0], ch), BF)] * nf
    return vol, call(mix_kernel, shapes, [], held, other, vol, us=2.6, after=after)


def turned(field):
    def kernel(field, out):
        step = 2 * WW

        def strip(f, carry):
            cells = pl.ds(pl.multiple_of(f * step, step), step)
            out[cells, :] = jnp.transpose(field[:, cells])
            return carry

        lax.fori_loop(0, field.shape[1] // step, strip, 0)

    return call(kernel, jax.ShapeDtypeStruct(field.shape[::-1], BF), [], field, us=1.2)


def unmix(turn, mg, held, other, ch):
    blk = mg.shape[0]
    pairs, rows, share = held.shape
    nf = rows // ch
    if ch % 128:
        weights = jnp.stack([held, other], axis=1).reshape(2 * pairs, rows, share)
        out = jnp.einsum("co,voi->vic", mg, weights, preferred_element_type=F32)
        out = out.astype(BF).reshape(nf, ch, blk)
        return [pick(out, turn[0] ^ s) for s in range(nf)]

    def kernel(turn, mg, held, other, *refs):
        out, back = refs[:-1], refs[-1]
        for v in range(2 * pairs):
            block = (other if v % 2 else held)[v // 2]
            total = lax.dot_general(
                mg[...], block, (((1,), (0,)), ((), ())), preferred_element_type=F32
            )
            turned = jnp.transpose(total).astype(BF)
            for k in range(share // ch):
                back[v * (share // ch) + k] = turned[k * ch : (k + 1) * ch, :]
        for s in range(nf):
            out[s][...] = back[turn[0] ^ s]

    shapes = [jax.ShapeDtypeStruct((ch, blk), BF)] * nf
    return call(
        kernel, shapes, [pltpu.VMEM((nf, ch, blk), BF)], turn, mg, held, other, us=2.2
    )


def split(value):
    high = value.astype(BF)
    return high, (value - high.astype(F32)).astype(BF)


def joined(high, low):
    return high.astype(F32) + low.astype(F32)


def weight_products(base, pieces, steps, vol_t, taps, ch, norm, ns):
    rows, pairs = vol_t.shape[1], ns // 2
    share = rows // ns
    if halved(ch, share, ns):
        count = taps.shape[0]

        def kernel(base, vol, taps, *refs):
            parts, mg, mine, theirs = refs[: len(steps)], refs[len(steps)], refs[-1 - pairs : -1], refs[-1]
            mg[...] = base[...]
            for r, part in zip(steps, parts):
                mg[:, r * ch : (r + 1) * ch] = part[...]
            for r in range(rows // ch):
                row = slice(r * ch, (r + 1) * ch)
                turned = jnp.transpose(mg[:, row])
                for v in range(ns):
                    total = norm * lax.dot_general(
                        turned, vol[:, v * share : (v + 1) * share], (((1,), (0,)), ((), ())),
                        preferred_element_type=F32,
                    )
                    if v % 2:
                        theirs[v // 2, row, :] = total.astype(BF)
                    else:
                        mine[v // 2][row, :] = total
            high, low = split(taps[...])
            theirs[0, rows:, :ch] = high
            theirs[1, rows:, :ch] = low

        shapes = [jax.ShapeDtypeStruct(vol_t.shape, BF)]
        shapes += [jax.ShapeDtypeStruct((rows, share), F32)] * pairs
        shapes.append(jax.ShapeDtypeStruct((pairs, rows + count, share), BF))
        got = call(kernel, shapes, [], base, vol_t, taps, *pieces, us=2.5)
        return got[0], got[1:-1], got[-1]
    if isinstance(base, dict):
        parts = {**base, **dict(zip(steps, pieces))}
        mg = jnp.concatenate([parts[r] for r in sorted(parts)], axis=1)
    else:
        mg = base
        for r, part in zip(steps, pieces):
            mg = lax.dynamic_update_slice_in_dim(mg, part, r * ch, axis=1)
    part = lax.dot_general(mg, vol_t, (((0,), (0,)), ((), ())), preferred_element_type=F32)
    part = (part * norm).reshape(rows, pairs, 2, share)
    theirs = part[:, :, 1].transpose(1, 0, 2).astype(BF)
    return mg, [part[:, k, 0] for k in range(pairs)], theirs


def assemble(me, base, pieces, steps):
    blk, ch = pieces[0].shape

    def kernel(me, *refs):
        for s, piece in zip(steps, refs[:-1]):
            refs[-1][me[0] ^ s] = piece[...]

    shape = jax.ShapeDtypeStruct((lax.axis_size("filter"), blk, ch), BF)
    return in_place(kernel, shape, (me,), base, pieces, 0.5)


def assemble_last(me, odd, base, pieces, steps, planes):
    nf, blk, ch = base.shape
    flat = nf * blk // planes

    def kernel(me, odd, base, *refs):
        out, near, far = refs[-3:]
        for s, piece in zip(steps, refs[:-3]):
            out[me[0] ^ s] = piece[...]
        for k in range(flat // blk):
            first, last = out[k], out[nf - flat // blk + k]
            near[k * blk : (k + 1) * blk, :] = jnp.where(odd[0] == 1, first, last)
            far[k * blk : (k + 1) * blk, :] = jnp.where(odd[0] == 1, last, first)

    edge = jax.ShapeDtypeStruct((flat, ch), BF)
    shapes = (jax.ShapeDtypeStruct((nf, blk, ch), BF), edge, edge)
    out, near, far = call(kernel, shapes, [], me, odd, base, *pieces, us=0.8, alias=2)
    return out.reshape(planes, flat, ch), near, far


def finish(me, up, base, pieces, steps):
    blk = pieces[0].shape[1]

    def kernel(me, up, *refs):
        for s, piece in zip(steps, refs[:-1]):
            lane = pl.ds(pl.multiple_of((me[0] ^ s) * blk, 128), blk)
            refs[-1][:, lane] = (up[:, lane].astype(F32) + piece[...].astype(F32)).astype(BF)

    shape = jax.ShapeDtypeStruct(up.shape, BF)
    return in_place(kernel, shape, (me, up), base, pieces, 0.25 * len(pieces))


def body(volume, mixing, kernel_taps, upstream):
    ch, planes, flat = volume.shape
    height = flat // WW
    nf, ns = lax.axis_size("filter"), lax.axis_size("space")
    me, me_space = lax.axis_index("filter"), lax.axis_index("space")
    total = planes * flat
    blk = total // nf
    norm = 1.0 / math.sqrt(ns * total)
    edges, middle = (0, planes - 1), tuple(range(1, planes - 1))
    groups = (edges, middle)
    turn = jnp.reshape(me ^ (me_space * (nf // ns)), (1,)).astype(jnp.int32)

    odd = jnp.reshape(me_space & 1, (1,)).astype(jnp.int32)
    own = jnp.reshape(me, (1,)).astype(jnp.int32)

    vol = volume.reshape(ch, total)
    mid = nf // 2
    early = [0, mid]
    later = [s for s in range(mid + 1, nf)]
    last = list(range(1, mid))

    def some(parts, steps):
        return [parts[s] for s in steps]

    send = [lax.dynamic_slice_in_dim(vol, (me ^ s) * blk, blk, axis=1) for s in range(nf)]
    pieces = exchange(send, "filter")
    steps = early + [mid + 1]
    vol_1 = fold_volume(turn, None, some(pieces, steps), steps)
    vol_2 = fold_volume(turn, vol_1, some(pieces, [mid + 2, 1, 2]), [mid + 2, 1, 2])
    rest = later[2:] + last[2:]
    vol_3 = fold_volume(turn, vol_2, some(pieces, rest), rest)
    held, other = gather_weights(mixing, me_space, send, vol_2)
    up = upstream.reshape(ch, total)
    up_t = turned(up)
    vol_t, prod = mix(vol_3, held, other, ch, (up_t,))

    got = exchange(prod, "filter")
    near_steps, cross = list(range(2, mid)), list(range(mid, nf))
    mixed = assemble(own, None, some(got, [0, 1]), [0, 1])
    mixed = assemble(own, mixed, some(got, near_steps), near_steps)
    mixed, near, far = assemble_last(own, odd, mixed, some(got, cross), cross, planes)
    near, far = halo(near, far)

    taps = kernel_taps.T
    pad = pltpu.VMEM((planes + 2, height + 2, WW, ch), F32)

    def grad_shapes(g):
        return (
            jax.ShapeDtypeStruct((len(g), flat, ch), BF),
            jax.ShapeDtypeStruct((len(g), flat, ch), F32),
        )

    edge = jax.ShapeDtypeStruct((flat, ch), BF)
    grad_middle, silu_middle = call(
        functools.partial(forward_middle, middle, planes), grad_shapes(middle), [pad],
        mixed, taps, up_t, us=3.2,
    )
    grad_edges, silu_edges, to_near, to_far = call(
        functools.partial(forward_edges, planes), grad_shapes(edges) + (edge, edge), [pad],
        odd, mixed, near, far, taps, up_t, us=3.2, after=(grad_middle,),
    )
    grad_near, grad_far = halo(to_near, to_far)
    where = {p: (i, k) for i, g in enumerate(groups) for k, p in enumerate(g)}
    mg_middle = call(
        functools.partial(backward_middle, middle, where, planes),
        jax.ShapeDtypeStruct((len(middle), flat, ch), BF), [pad],
        grad_edges, grad_middle, taps, us=2.3,
    )
    steps = [0, 1] + cross
    whole, *send = call(
        functools.partial(backward_edges, where, planes, steps),
        [jax.ShapeDtypeStruct((total, ch), BF)] + [jax.ShapeDtypeStruct((blk, ch), BF)] * len(steps),
        [pad], own, odd, grad_edges, grad_middle, grad_near, grad_far, taps, mg_middle, us=2.8,
    )
    got = {s: swap(block, "filter", s) if s else block for s, block in zip(steps, send)}

    wide = ch % 128 == 0
    side = some(got, [0, 1])
    shapes = (jax.ShapeDtypeStruct((32, ch), F32), jax.ShapeDtypeStruct((ch, total), BF))
    shapes += (jax.ShapeDtypeStruct((blk, nf * ch), BF),) if wide else ()
    kernel = functools.partial(taps_kernel, where, planes, norm, [0, 1] if wide else [])
    taps_grad, output, *mg = call(
        kernel, shapes, [pad, pad],
        odd, mixed, near, far, grad_edges, grad_middle, silu_edges, silu_middle, vol,
        *(side if wide else []), us=5.8,
    )
    output = output.reshape(ch, planes, flat)
    send = blocks(own, whole, blk, near_steps, (taps_grad,))
    got.update((s, swap(block, "filter", s)) for s, block in zip(near_steps, send))
    base = mg[0] if wide else dict(zip([0, 1], side))
    rest = cross + near_steps
    mg_all, mine, theirs = weight_products(
        base, some(got, rest), rest, vol_t, taps_grad, ch, norm, ns
    )
    back = unmix(turn, mg_all, held, other, ch)
    got = exchange(back, "filter")
    volume_grad_1 = finish(own, up, None, some(got, [0, 1]), [0, 1])
    volume_grad_2 = finish(own, up, volume_grad_1, some(got, cross), cross)
    mixing_grad, taps_grad = scatter_rest(
        mine, theirs, taps_grad, ch, volume_grad_1, volume_grad_2
    )
    volume_grad = finish(own, up, volume_grad_2, some(got, near_steps), near_steps)
    volume_grad = volume_grad.reshape(ch, planes, flat)
    return (output, volume_grad, mixing_grad, taps_grad[:27].T)


def solution(mesh):
    in_specs = (
        P("filter", "space", None),
        P("filter", None),
        P("filter", None),
        P("filter", "space", None),
    )
    out_specs = (
        P("filter", "space", None),
        P("filter", "space", None),
        P("filter", "space"),
        P("filter", None),
    )
    return jax.shard_map(body, mesh=mesh, in_specs=in_specs, out_specs=out_specs, check_vma=False)
```

```python
import functools
import math

import jax
import jax.numpy as jnp
from jax import lax
from jax.experimental import pallas as pl
from jax.experimental.pallas import tpu as pltpu
from jax.sharding import PartitionSpec as P

WW = 64
BF = jnp.bfloat16
F32 = jnp.float32


def swap(block, axis, step):
    size = lax.axis_size(axis)
    return lax.ppermute(block, axis, [(i, i ^ step) for i in range(size)])


def exchange(pieces, axis):
    size = len(pieces)
    order = list(range(size // 2, size)) + list(range(1, size // 2))
    got = {0: pieces[0]}
    for s in order:
        got[s] = swap(pieces[s], axis, s)
    return [got[s] for s in range(size)]


def place(pieces, shift):
    out = jnp.zeros((len(pieces),) + pieces[0].shape, pieces[0].dtype)
    for s, piece in enumerate(pieces):
        out = lax.dynamic_update_index_in_dim(out, piece, shift ^ s, 0)
    return out


def pick(blocks, index):
    return lax.dynamic_index_in_dim(blocks, index, 0, keepdims=False)


def join(parts, after, us=0.4):
    def kernel(*refs):
        for k in range(len(parts)):
            refs[-1][k] = refs[k][...]

    shape = jax.ShapeDtypeStruct((len(parts),) + parts[0].shape, parts[0].dtype)
    return call(kernel, shape, [], *parts, us=us, after=after)


def gather_weights(mixing, me_space, send, arrived):
    rows, cols = mixing.shape
    nf, ns = lax.axis_size("filter"), lax.axis_size("space")
    share, pairs = cols // ns, ns // 2
    own = lax.dynamic_slice_in_dim(mixing, me_space * share, share, axis=1)
    even = join([own] + [swap(own, "filter", s) for s in range(2, nf, 2)], send[nf // 2 :])
    first = [even] + [swap(even, "space", s) for s in range(2, ns, 2)]
    odd = swap(even, "filter", 1)
    second = [odd] + [swap(odd, "space", s) for s in range(2, ns, 2)]

    def kernel(*refs):
        for k in range(pairs):
            for r in range(nf):
                source = refs[pairs * (r % 2) + k]
                refs[-1][k, r * rows : (r + 1) * rows, :] = source[r // 2]

    shape = jax.ShapeDtypeStruct((pairs, nf * rows, share), BF)
    held = call(kernel, shape, [], *first, *second, us=0.6, after=(arrived,))
    return held, swap(held, "space", 1)


def halved(ch, share, ns):
    return ns == 4 and share == 2 * ch and ch % 128 == 0


def halves_first(rows, nf, mine0, mine1, got, taps, a_keep, a_send, b_keep, b_next, b_send, sums):
    h, count = a_keep.shape[1], taps.shape[0]
    total = joined(*split(taps[...])) + joined(got[0, nf * rows :, :h], got[1, nf * rows :, :h])
    high, low = split(total)
    a_send[nf * rows : nf * rows + count, :] = high
    a_send[nf * rows + count :, :] = low
    sums[...] = joined(high, low)
    for r in range(nf):
        row = slice(r * rows, (r + 1) * rows)
        own = mine0[row, :] + got[0, row, :].astype(F32)
        step = mine1[row, :] + got[1, row, :].astype(F32)
        a_keep[row, :] = own[:, :h]
        a_send[row, :] = step[:, :h].astype(BF)
        if r % 2:
            b_send[0, r // 2] = own[:, h:].astype(BF)
            b_send[1, r // 2] = step[:, h:].astype(BF)
        else:
            b_keep[r // 2] = own[:, h:]
            b_next[r // 2] = step[:, h:]


def halves_second(rows, nf, a_keep, a_got, b_keep, b_next, b_got, sums, near, a_send, far, b_send, taps):
    count = taps.shape[0]
    high, low = a_got[nf * rows : nf * rows + count, :], a_got[nf * rows + count :, :]
    taps[...] = sums[...] + joined(high, low)
    for r in range(nf):
        row = slice(r * rows, (r + 1) * rows)
        own = a_keep[row, :] + a_got[row, :].astype(F32)
        if r % 2:
            a_send[r // 2] = own.astype(BF)
        else:
            near[r // 2] = own
    far[...] = b_keep[...] + b_got[0].astype(F32)
    b_send[...] = (b_next[...] + b_got[1].astype(F32)).astype(BF)


def halves_third(near, a_got, far, b_got, keep, *send):
    h = near.shape[2]
    for k in range(near.shape[0]):
        left = near[k] + a_got[k].astype(F32)
        right = far[k] + b_got[k].astype(F32)
        if k:
            send[k - 1][:, :h] = left.astype(BF)
            send[k - 1][:, h:] = right.astype(BF)
        else:
            keep[:, :h] = left
            keep[:, h:] = right


def scatter_rest(mine, theirs, taps, rows, first_in, second_in):
    nf, ns = lax.axis_size("filter"), lax.axis_size("space")
    pairs, share = ns // 2, theirs.shape[2]
    theirs = swap(theirs, "space", 1)
    if halved(rows, share, ns):
        h, n, count = share // 2, nf // 2, taps.shape[0]
        shapes = (
            jax.ShapeDtypeStruct((nf * rows, h), F32),
            jax.ShapeDtypeStruct((nf * rows + 2 * count, h), BF),
            jax.ShapeDtypeStruct((n, rows, h), F32), jax.ShapeDtypeStruct((n, rows, h), F32),
            jax.ShapeDtypeStruct((2, n, rows, h), BF), jax.ShapeDtypeStruct((count, h), F32),
        )
        kernel = functools.partial(halves_first, rows, nf)
        a_keep, a_send, b_keep, b_next, b_send, sums = call(
            kernel, shapes, [], *mine, theirs, taps, us=0.8
        )
        a_got = swap(a_send, "space", 2)
        b_got = swap(b_send, "filter", 1)
        shapes = (
            jax.ShapeDtypeStruct((n, rows, h), F32), jax.ShapeDtypeStruct((n, rows, h), BF),
            jax.ShapeDtypeStruct((n, rows, h), F32), jax.ShapeDtypeStruct((n, rows, h), BF),
            jax.ShapeDtypeStruct((count, h), F32),
        )
        kernel = functools.partial(halves_second, rows, nf)
        near, a_send, far, b_send, taps = call(
            kernel, shapes, [], a_keep, a_got, b_keep, b_next, b_got, sums,
            us=0.6, after=(first_in,),
        )
        a_got = swap(a_send, "filter", 1)
        b_got = swap(b_send, "space", 2)
        shapes = [jax.ShapeDtypeStruct((rows, share), F32)]
        shapes += [jax.ShapeDtypeStruct((rows, share), BF)] * (n - 1)
        keep, *rest = call(
            halves_third, shapes, [], near, a_got, far, b_got, us=0.5, after=(second_in,)
        )
    else:
        step = 1
        while step < ns:
            taps = taps + swap(taps, "space", step)
            step *= 2
        total = mine[0] + theirs[0].astype(F32)
        for k in range(1, pairs):
            send = (mine[k] + theirs[k].astype(F32)).astype(BF)
            total = total + swap(send, "space", 2 * k).astype(F32)
        total = total.reshape(nf // 2, 2, rows, share)
        near = total[:, 0] + swap(total[:, 1].astype(BF), "filter", 1).astype(F32)
        keep, rest = near[0], [near[k].astype(BF) for k in range(1, nf // 2)]
    for k, part in enumerate(rest):
        keep = keep + swap(part, "filter", 2 * (k + 1)).astype(F32)
    return keep, taps


def halo(near, far):
    size = lax.axis_size("space")
    inner = [(i, i ^ 1) for i in range(size)]
    outer = [(i, ((i + 1) ^ 1) - 1) for i in range(1, size - 1)]
    far = lax.ppermute(far, "space", outer)
    return lax.ppermute(near, "space", inner), far


def fill(pad_ref, plane, source):
    rows, width, ch = pad_ref.shape[1] - 2, pad_ref.shape[2], pad_ref.shape[3]
    pad_ref[plane, 1 : rows + 1] = source.astype(F32).reshape(rows, width, ch)
    pad_ref[plane, 0] = jnp.zeros((width, ch), F32)
    pad_ref[plane, rows + 1] = jnp.zeros((width, ch), F32)


def shifted(value, up):
    width = value.shape[0]
    index = lax.broadcasted_iota(jnp.int32, value.shape, 0)
    if up:
        return jnp.where(index == width - 1, 0.0, pltpu.roll(value, width - 1, 0))
    return jnp.where(index == 0, 0.0, pltpu.roll(value, 1, 0))


def conv_row(pad_ref, taps_ref, plane, row, flip):
    sums = [None, None, None]
    for a in range(3):
        for b in range(3):
            da, db = (1 - a, 1 - b) if flip else (a - 1, b - 1)
            line = pad_ref[plane + da, row + db]
            for e in range(3):
                term = taps_ref[pl.ds(a * 9 + b * 3 + e, 1), :] * line
                sums[e] = term if sums[e] is None else sums[e] + term
    lo, hi = (sums[2], sums[0]) if flip else (sums[0], sums[2])
    return sums[1] + shifted(lo, False) + shifted(hi, True)


def load_planes(pad_ref, refs, where, sides, wanted, planes):
    for p in sorted(wanted):
        if p < 0:
            fill(pad_ref, 0, jnp.where(sides[0][0] == 1, sides[1][...], sides[2][...]))
        elif p >= planes:
            fill(pad_ref, planes + 1, jnp.where(sides[0][0] == 1, sides[2][...], sides[1][...]))
        else:
            which, at = where[p]
            fill(pad_ref, p + 1, refs[which][at])


def forward_planes(group, planes, sides, m, taps, up, grad, silu, pad):
    wanted = {p + a for p in group for a in (-1, 0, 1)}
    where = {p: (0, p) for p in range(planes)}
    load_planes(pad, (m,), where, sides, wanted, planes)
    lanes, flat = 2 * WW, m.shape[1]
    for k, p in enumerate(group):

        def strip(f, carry, k=k, p=p):
            lines = [conv_row(pad, taps, p + 1, f * 2 + 1 + r, False) for r in range(2)]
            spatial = jnp.concatenate(lines, axis=0)
            sig = 1.0 / (1.0 + jnp.exp(-spatial))
            cells = pl.ds(pl.multiple_of(f * lanes, lanes), lanes)
            source = pl.ds(pl.multiple_of(p * flat + f * lanes, lanes), lanes)
            slope = sig * (1.0 + spatial * (1.0 - sig))
            grad[k, cells, :] = (up[source, :].astype(F32) * slope).astype(BF)
            silu[k, cells, :] = spatial * sig
            return carry

        lax.fori_loop(0, flat // lanes, strip, 0, unroll=2)


def forward_middle(group, planes, m, taps, up, grad, silu, pad):
    forward_planes(group, planes, (), m, taps, up, grad, silu, pad)


def forward_edges(planes, odd, m, near, far, taps, up, grad, silu, to_near, to_far, pad):
    sides = (odd, near, far)
    forward_planes((0, planes - 1), planes, sides, m, taps, up, grad, silu, pad)
    to_near[...] = jnp.where(odd[0] == 1, grad[0], grad[1])
    to_far[...] = jnp.where(odd[0] == 1, grad[1], grad[0])


def backward_planes(group, where, planes, sides, g0, g1, taps, put, pad):
    wanted = {p + a for p in group for a in (-1, 0, 1)}
    load_planes(pad, (g0, g1), where, sides, wanted, planes)
    lanes, flat = 2 * WW, g0.shape[1]
    for k, p in enumerate(group):

        def strip(f, carry, k=k, p=p):
            lines = [conv_row(pad, taps, p + 1, f * 2 + 1 + r, True) for r in range(2)]
            put(k, p, pl.multiple_of(f * lanes, lanes), jnp.concatenate(lines, axis=0).astype(BF))
            return carry

        lax.fori_loop(0, flat // lanes, strip, 0, unroll=2)


def backward_middle(group, where, planes, g0, g1, taps, out, pad):
    def put(k, p, cell, value):
        out[k, pl.ds(cell, value.shape[0]), :] = value

    backward_planes(group, where, planes, (), g0, g1, taps, put, pad)


def backward_edges(where, planes, steps, me, odd, g0, g1, near, far, taps, inner, whole, *refs):
    out, pad = refs[:-1], refs[-1]
    flat = g0.shape[1]

    def put(k, p, cell, value):
        whole[pl.ds(p * flat + cell, value.shape[0]), :] = value

    backward_planes((0, planes - 1), where, planes, (odd, near, far), g0, g1, taps, put, pad)
    for k in range(1, planes - 1):
        whole[k * flat : (k + 1) * flat, :] = inner[k - 1]
    blk = out[0].shape[0]
    for s, block in zip(steps, out):
        block[...] = whole[pl.ds(pl.multiple_of((me[0] ^ s) * blk, blk), blk), :]


def blocks(me, whole, blk, steps, after):
    def kernel(me, whole, *out):
        for s, block in zip(steps, out):
            block[...] = whole[pl.ds(pl.multiple_of((me[0] ^ s) * blk, blk), blk), :]

    shapes = [jax.ShapeDtypeStruct((blk, whole.shape[1]), BF)] * len(steps)
    return call(kernel, shapes, [], me, whole, us=0.3, after=after)


def taps_kernel(where_grad, planes, norm, steps, odd, m, near, far, g0, g1, s0, s1, vol, *refs):
    parts, refs = refs[: len(steps)], refs[len(steps) :]
    out, output, pad, gpad = refs[0], refs[1], refs[-2], refs[-1]
    for r, part in zip(steps, parts):
        refs[2][:, r * part.shape[1] : (r + 1) * part.shape[1]] = part[...]
    flat, lanes = m.shape[1], 2 * WW
    for p in range(planes):
        which, at = where_grad[p]
        silu = (s0, s1)[which]

        def strip(f, carry, p=p, at=at, silu=silu):
            cells = pl.ds(pl.multiple_of(f * lanes, lanes), lanes)
            lane = pl.ds(pl.multiple_of(p * flat + f * lanes, lanes), lanes)
            turned = jnp.transpose(silu[at, cells, :])
            output[:, lane] = (vol[:, lane].astype(F32) + turned).astype(BF)
            return carry

        lax.fori_loop(0, flat // lanes, strip, 0, unroll=2)
    where = {p: (0, p) for p in range(planes)}
    load_planes(pad, (m,), where, (odd, near, far), range(-1, planes + 1), planes)
    load_planes(gpad, (g0, g1), where_grad, (), range(planes), planes)
    rows, width, ch = pad.shape[1] - 2, pad.shape[2], pad.shape[3]
    sums = tuple(jnp.zeros((8, ch), F32) for _ in range(27))

    def line(at, sums):
        p, h = at // rows, at % rows
        sums = list(sums)
        own = gpad[p + 1, h + 1]
        turned = (shifted(own, True), own, shifted(own, False))
        for a in range(3):
            for b in range(3):
                field = pad[p + a, h + b]
                for e in range(3):
                    prod = (turned[e] * field).reshape(width // 8, 8, ch)
                    sums[a * 9 + b * 3 + e] = sums[a * 9 + b * 3 + e] + jnp.sum(prod, axis=0)
        return tuple(sums)

    sums = lax.fori_loop(0, planes * rows, line, sums)
    for k in range(27):
        out[k : k + 1, :] = jnp.sum(sums[k], axis=0, keepdims=True) * norm
    out[27:, :] = jnp.zeros((5, ch), F32)


def call(kernel, out_shape, scratch, *args, us=1.0, after=(), alias=None):
    specs = [
        pl.BlockSpec(memory_space=pltpu.SMEM if arg.dtype == jnp.int32 else pltpu.VMEM)
        for arg in args
    ]

    def wrapped(*refs):
        kernel(*refs[: len(args)], *refs[len(args) + len(after) :])

    return pl.pallas_call(
        wrapped,
        out_shape=out_shape,
        in_specs=specs + [pl.BlockSpec(memory_space=pl.ANY)] * len(after),
        out_specs=jax.tree.map(lambda _: pl.BlockSpec(memory_space=pltpu.VMEM), out_shape),
        scratch_shapes=scratch,
        input_output_aliases={} if alias is None else {alias: 0},
        compiler_params=pltpu.CompilerParams(vmem_limit_bytes=32 * 1024 * 1024),
        cost_estimate=pl.CostEstimate(
            flops=int(us * 1.15e9), bytes_accessed=1024 * 1024, transcendentals=0
        ),
    )(*args, *after)


def in_place(kernel, shape, leading, base, pieces, us):
    if base is None:
        return call(kernel, shape, [], *leading, *pieces, us=us)

    def wrapped(*refs):
        kernel(*refs[: len(leading)], *refs[len(leading) + 1 :])

    return call(wrapped, shape, [], *leading, base, *pieces, us=us, alias=len(leading))


def fold_volume(turn, base, pieces, steps):
    nf, (ch, blk) = lax.axis_size("filter"), pieces[0].shape
    if ch % 128:
        out = jnp.zeros((nf, ch, blk), BF) if base is None else base
        for t, piece in zip(steps, pieces):
            out = lax.dynamic_update_index_in_dim(out, piece, turn[0] ^ t, 0)
        return out

    def kernel(turn, *refs):
        for t, piece in zip(steps, refs[:-1]):
            lane = pl.ds(pl.multiple_of((turn[0] ^ t) * ch, 128), ch)
            refs[-1][:, lane] = jnp.transpose(piece[...])

    shape = jax.ShapeDtypeStruct((blk, nf * ch), BF)
    return in_place(kernel, shape, (turn,), base, pieces, 0.3 * len(pieces))


def mix_kernel(held, other, vol_t, *out):
    nf, ch, share = len(out), out[0].shape[1], held.shape[2]
    for s in range(0, nf, 2):
        total = None
        for v in range(2 * held.shape[0]):
            block = (other if v % 2 else held)[v // 2, s * ch : (s + 2) * ch, :]
            term = lax.dot_general(
                vol_t[:, v * share : (v + 1) * share], block, (((1,), (1,)), ((), ())),
                preferred_element_type=F32,
            )
            total = term if total is None else total + term
        out[s][...] = total[:, :ch].astype(BF)
        out[s + 1][...] = total[:, ch:].astype(BF)


def mix(vol, held, other, ch, after):
    pairs, rows, share = held.shape
    nf = rows // ch
    if ch % 128:
        vol_t = vol.reshape(rows, vol.shape[2]).T
        weights = jnp.stack([held, other], axis=1).reshape(2 * pairs, rows, share)
        out = jnp.einsum(
            "cvi,voi->co", vol_t.reshape(-1, 2 * pairs, share), weights, preferred_element_type=F32
        ).astype(BF)
        return vol_t, [out[:, s * ch : (s + 1) * ch] for s in range(nf)]
    shapes = [jax.ShapeDtypeStruct((vol.shape[0], ch), BF)] * nf
    return vol, call(mix_kernel, shapes, [], held, other, vol, us=2.6, after=after)


def turned(field):
    def kernel(field, out):
        step = 2 * WW

        def strip(f, carry):
            cells = pl.ds(pl.multiple_of(f * step, step), step)
            out[cells, :] = jnp.transpose(field[:, cells])
            return carry

        lax.fori_loop(0, field.shape[1] // step, strip, 0)

    return call(kernel, jax.ShapeDtypeStruct(field.shape[::-1], BF), [], field, us=1.2)


def unmix(turn, mg, held, other, ch):
    blk = mg.shape[0]
    pairs, rows, share = held.shape
    nf = rows // ch
    if ch % 128:
        weights = jnp.stack([held, other], axis=1).reshape(2 * pairs, rows, share)
        out = jnp.einsum("co,voi->vic", mg, weights, preferred_element_type=F32)
        out = out.astype(BF).reshape(nf, ch, blk)
        return [pick(out, turn[0] ^ s) for s in range(nf)]

    def kernel(turn, mg, held, other, *refs):
        out, back = refs[:-1], refs[-1]
        for v in range(2 * pairs):
            block = (other if v % 2 else held)[v // 2]
            total = lax.dot_general(
                mg[...], block, (((1,), (0,)), ((), ())), preferred_element_type=F32
            )
            turned = jnp.transpose(total).astype(BF)
            for k in range(share // ch):
                back[v * (share // ch) + k] = turned[k * ch : (k + 1) * ch, :]
        for s in range(nf):
            out[s][...] = back[turn[0] ^ s]

    shapes = [jax.ShapeDtypeStruct((ch, blk), BF)] * nf
    return call(
        kernel, shapes, [pltpu.VMEM((nf, ch, blk), BF)], turn, mg, held, other, us=2.2
    )


def split(value):
    high = value.astype(BF)
    return high, (value - high.astype(F32)).astype(BF)


def joined(high, low):
    return high.astype(F32) + low.astype(F32)


def weight_products(base, pieces, steps, vol_t, taps, ch, norm, ns):
    rows, pairs = vol_t.shape[1], ns // 2
    share = rows // ns
    if halved(ch, share, ns):
        count = taps.shape[0]

        def kernel(base, vol, taps, *refs):
            parts, mg, mine, theirs = refs[: len(steps)], refs[len(steps)], refs[-1 - pairs : -1], refs[-1]
            mg[...] = base[...]
            for r, part in zip(steps, parts):
                mg[:, r * ch : (r + 1) * ch] = part[...]
            for r in range(rows // ch):
                row = slice(r * ch, (r + 1) * ch)
                turned = jnp.transpose(mg[:, row])
                for v in range(ns):
                    total = norm * lax.dot_general(
                        turned, vol[:, v * share : (v + 1) * share], (((1,), (0,)), ((), ())),
                        preferred_element_type=F32,
                    )
                    if v % 2:
                        theirs[v // 2, row, :] = total.astype(BF)
                    else:
                        mine[v // 2][row, :] = total
            high, low = split(taps[...])
            theirs[0, rows:, :ch] = high
            theirs[1, rows:, :ch] = low

        shapes = [jax.ShapeDtypeStruct(vol_t.shape, BF)]
        shapes += [jax.ShapeDtypeStruct((rows, share), F32)] * pairs
        shapes.append(jax.ShapeDtypeStruct((pairs, rows + count, share), BF))
        got = call(kernel, shapes, [], base, vol_t, taps, *pieces, us=2.5)
        return got[0], got[1:-1], got[-1]
    if isinstance(base, dict):
        parts = {**base, **dict(zip(steps, pieces))}
        mg = jnp.concatenate([parts[r] for r in sorted(parts)], axis=1)
    else:
        mg = base
        for r, part in zip(steps, pieces):
            mg = lax.dynamic_update_slice_in_dim(mg, part, r * ch, axis=1)
    part = lax.dot_general(mg, vol_t, (((0,), (0,)), ((), ())), preferred_element_type=F32)
    part = (part * norm).reshape(rows, pairs, 2, share)
    theirs = part[:, :, 1].transpose(1, 0, 2).astype(BF)
    return mg, [part[:, k, 0] for k in range(pairs)], theirs


def assemble(me, base, pieces, steps):
    blk, ch = pieces[0].shape

    def kernel(me, *refs):
        for s, piece in zip(steps, refs[:-1]):
            refs[-1][me[0] ^ s] = piece[...]

    shape = jax.ShapeDtypeStruct((lax.axis_size("filter"), blk, ch), BF)
    return in_place(kernel, shape, (me,), base, pieces, 0.5)


def assemble_last(me, odd, base, pieces, steps, planes):
    nf, blk, ch = base.shape
    flat = nf * blk // planes

    def kernel(me, odd, base, *refs):
        out, near, far = refs[-3:]
        for s, piece in zip(steps, refs[:-3]):
            out[me[0] ^ s] = piece[...]
        for k in range(flat // blk):
            first, last = out[k], out[nf - flat // blk + k]
            near[k * blk : (k + 1) * blk, :] = jnp.where(odd[0] == 1, first, last)
            far[k * blk : (k + 1) * blk, :] = jnp.where(odd[0] == 1, last, first)

    edge = jax.ShapeDtypeStruct((flat, ch), BF)
    shapes = (jax.ShapeDtypeStruct((nf, blk, ch), BF), edge, edge)
    out, near, far = call(kernel, shapes, [], me, odd, base, *pieces, us=0.8, alias=2)
    return out.reshape(planes, flat, ch), near, far


def finish(me, up, base, pieces, steps):
    blk = pieces[0].shape[1]

    def kernel(me, up, *refs):
        for s, piece in zip(steps, refs[:-1]):
            lane = pl.ds(pl.multiple_of((me[0] ^ s) * blk, 128), blk)
            refs[-1][:, lane] = (up[:, lane].astype(F32) + piece[...].astype(F32)).astype(BF)

    shape = jax.ShapeDtypeStruct(up.shape, BF)
    return in_place(kernel, shape, (me, up), base, pieces, 0.25 * len(pieces))


def body(volume, mixing, kernel_taps, upstream):
    ch, planes, flat = volume.shape
    height = flat // WW
    nf, ns = lax.axis_size("filter"), lax.axis_size("space")
    me, me_space = lax.axis_index("filter"), lax.axis_index("space")
    total = planes * flat
    blk = total // nf
    norm = 1.0 / math.sqrt(ns * total)
    edges, middle = (0, planes - 1), tuple(range(1, planes - 1))
    groups = (edges, middle)
    turn = jnp.reshape(me ^ (me_space * (nf // ns)), (1,)).astype(jnp.int32)

    odd = jnp.reshape(me_space & 1, (1,)).astype(jnp.int32)
    own = jnp.reshape(me, (1,)).astype(jnp.int32)

    vol = volume.reshape(ch, total)
    mid = nf // 2
    early = [0, mid]
    later = [s for s in range(mid + 1, nf)]
    last = list(range(1, mid))

    def some(parts, steps):
        return [parts[s] for s in steps]

    send = [lax.dynamic_slice_in_dim(vol, (me ^ s) * blk, blk, axis=1) for s in range(nf)]
    pieces = exchange(send, "filter")
    steps = early + [mid + 1]
    vol_1 = fold_volume(turn, None, some(pieces, steps), steps)
    vol_2 = fold_volume(turn, vol_1, some(pieces, [mid + 2, 1, 2]), [mid + 2, 1, 2])
    rest = later[2:] + last[2:]
    vol_3 = fold_volume(turn, vol_2, some(pieces, rest), rest)
    held, other = gather_weights(mixing, me_space, send, vol_2)
    up = upstream.reshape(ch, total)
    up_t = turned(up)
    vol_t, prod = mix(vol_3, held, other, ch, (up_t,))

    got = exchange(prod, "filter")
    near_steps, cross = list(range(2, mid)), list(range(mid, nf))
    mixed = assemble(own, None, some(got, [0, 1]), [0, 1])
    mixed = assemble(own, mixed, some(got, near_steps), near_steps)
    mixed, near, far = assemble_last(own, odd, mixed, some(got, cross), cross, planes)
    near, far = halo(near, far)

    taps = kernel_taps.T
    pad = pltpu.VMEM((planes + 2, height + 2, WW, ch), F32)

    def grad_shapes(g):
        return (
            jax.ShapeDtypeStruct((len(g), flat, ch), BF),
            jax.ShapeDtypeStruct((len(g), flat, ch), F32),
        )

    edge = jax.ShapeDtypeStruct((flat, ch), BF)
    grad_middle, silu_middle = call(
        functools.partial(forward_middle, middle, planes), grad_shapes(middle), [pad],
        mixed, taps, up_t, us=3.2,
    )
    grad_edges, silu_edges, to_near, to_far = call(
        functools.partial(forward_edges, planes), grad_shapes(edges) + (edge, edge), [pad],
        odd, mixed, near, far, taps, up_t, us=3.2, after=(grad_middle,),
    )
    grad_near, grad_far = halo(to_near, to_far)
    where = {p: (i, k) for i, g in enumerate(groups) for k, p in enumerate(g)}
    mg_middle = call(
        functools.partial(backward_middle, middle, where, planes),
        jax.ShapeDtypeStruct((len(middle), flat, ch), BF), [pad],
        grad_edges, grad_middle, taps, us=2.3,
    )
    steps = [0, 1] + cross
    whole, *send = call(
        functools.partial(backward_edges, where, planes, steps),
        [jax.ShapeDtypeStruct((total, ch), BF)] + [jax.ShapeDtypeStruct((blk, ch), BF)] * len(steps),
        [pad], own, odd, grad_edges, grad_middle, grad_near, grad_far, taps, mg_middle, us=2.8,
    )
    got = {s: swap(block, "filter", s) if s else block for s, block in zip(steps, send)}

    wide = ch % 128 == 0
    side = some(got, [0, 1])
    shapes = (jax.ShapeDtypeStruct((32, ch), F32), jax.ShapeDtypeStruct((ch, total), BF))
    shapes += (jax.ShapeDtypeStruct((blk, nf * ch), BF),) if wide else ()
    kernel = functools.partial(taps_kernel, where, planes, norm, [0, 1] if wide else [])
    taps_grad, output, *mg = call(
        kernel, shapes, [pad, pad],
        odd, mixed, near, far, grad_edges, grad_middle, silu_edges, silu_middle, vol,
        *(side if wide else []), us=5.8,
    )
    output = output.reshape(ch, planes, flat)
    send = blocks(own, whole, blk, near_steps, (taps_grad,))
    got.update((s, swap(block, "filter", s)) for s, block in zip(near_steps, send))
    base = mg[0] if wide else dict(zip([0, 1], side))
    rest = cross + near_steps
    mg_all, mine, theirs = weight_products(
        base, some(got, rest), rest, vol_t, taps_grad, ch, norm, ns
    )
    back = unmix(turn, mg_all, held, other, ch)
    got = exchange(back, "filter")
    volume_grad_1 = finish(own, up, None, some(got, [0, 1]), [0, 1])
    volume_grad_2 = finish(own, up, volume_grad_1, some(got, cross), cross)
    mixing_grad, taps_grad = scatter_rest(
        mine, theirs, taps_grad, ch, volume_grad_1, volume_grad_2
    )
    volume_grad = finish(own, up, volume_grad_2, some(got, near_steps), near_steps)
    volume_grad = volume_grad.reshape(ch, planes, flat)
    return (output, volume_grad, mixing_grad, taps_grad[:27].T)


def solution(mesh):
    in_specs = (
        P("filter", "space", None),
        P("filter", None),
        P("filter", None),
        P("filter", "space", None),
    )
    out_specs = (
        P("filter", "space", None),
        P("filter", "space", None),
        P("filter", "space"),
        P("filter", None),
    )
    return jax.shard_map(body, mesh=mesh, in_specs=in_specs, out_specs=out_specs, check_vma=False)
```

```python
import functools
import math

import jax
import jax.numpy as jnp
from jax import lax
from jax.experimental import pallas as pl
from jax.experimental.pallas import tpu as pltpu
from jax.sharding import PartitionSpec as P

WW = 64
BF = jnp.bfloat16
F32 = jnp.float32


def swap(block, axis, step):
    size = lax.axis_size(axis)
    return lax.ppermute(block, axis, [(i, i ^ step) for i in range(size)])


def exchange(pieces, axis):
    size = len(pieces)
    order = list(range(size // 2, size)) + list(range(1, size // 2))
    got = {0: pieces[0]}
    for s in order:
        got[s] = swap(pieces[s], axis, s)
    return [got[s] for s in range(size)]


def place(pieces, shift):
    out = jnp.zeros((len(pieces),) + pieces[0].shape, pieces[0].dtype)
    for s, piece in enumerate(pieces):
        out = lax.dynamic_update_index_in_dim(out, piece, shift ^ s, 0)
    return out


def pick(blocks, index):
    return lax.dynamic_index_in_dim(blocks, index, 0, keepdims=False)


def join(parts, after, us=0.4):
    def kernel(*refs):
        for k in range(len(parts)):
            refs[-1][k] = refs[k][...]

    shape = jax.ShapeDtypeStruct((len(parts),) + parts[0].shape, parts[0].dtype)
    return call(kernel, shape, [], *parts, us=us, after=after)


def gather_weights(mixing, me_space, send, arrived):
    rows, cols = mixing.shape
    nf, ns = lax.axis_size("filter"), lax.axis_size("space")
    share, pairs = cols // ns, ns // 2
    own = lax.dynamic_slice_in_dim(mixing, me_space * share, share, axis=1)
    even = join([own] + [swap(own, "filter", s) for s in range(2, nf, 2)], send[nf // 2 :])
    first = [even] + [swap(even, "space", s) for s in range(2, ns, 2)]
    odd = swap(even, "filter", 1)
    second = [odd] + [swap(odd, "space", s) for s in range(2, ns, 2)]

    def kernel(*refs):
        for k in range(pairs):
            for r in range(nf):
                source = refs[pairs * (r % 2) + k]
                refs[-1][k, r * rows : (r + 1) * rows, :] = source[r // 2]

    shape = jax.ShapeDtypeStruct((pairs, nf * rows, share), BF)
    held = call(kernel, shape, [], *first, *second, us=0.6, after=(arrived,))
    return held, swap(held, "space", 1)


def halved(ch, share, ns):
    return ns == 4 and share == 2 * ch and ch % 128 == 0


def halves_first(rows, nf, mine0, mine1, got, taps, a_keep, a_send, b_keep, b_next, b_send, sums):
    h, count = a_keep.shape[1], taps.shape[0]
    total = joined(*split(taps[...])) + joined(got[0, nf * rows :, :h], got[1, nf * rows :, :h])
    high, low = split(total)
    a_send[nf * rows : nf * rows + count, :] = high
    a_send[nf * rows + count :, :] = low
    sums[...] = joined(high, low)
    for r in range(nf):
        row = slice(r * rows, (r + 1) * rows)
        own = mine0[row, :] + got[0, row, :].astype(F32)
        step = mine1[row, :] + got[1, row, :].astype(F32)
        a_keep[row, :] = own[:, :h]
        a_send[row, :] = step[:, :h].astype(BF)
        if r % 2:
            b_send[0, r // 2] = own[:, h:].astype(BF)
            b_send[1, r // 2] = step[:, h:].astype(BF)
        else:
            b_keep[r // 2] = own[:, h:]
            b_next[r // 2] = step[:, h:]


def halves_second(rows, nf, a_keep, a_got, b_keep, b_next, b_got, sums, near, a_send, far, b_send, taps):
    count = taps.shape[0]
    high, low = a_got[nf * rows : nf * rows + count, :], a_got[nf * rows + count :, :]
    taps[...] = sums[...] + joined(high, low)
    for r in range(nf):
        row = slice(r * rows, (r + 1) * rows)
        own = a_keep[row, :] + a_got[row, :].astype(F32)
        if r % 2:
            a_send[r // 2] = own.astype(BF)
        else:
            near[r // 2] = own
    far[...] = b_keep[...] + b_got[0].astype(F32)
    b_send[...] = (b_next[...] + b_got[1].astype(F32)).astype(BF)


def halves_third(near, a_got, far, b_got, keep, *send):
    h = near.shape[2]
    for k in range(near.shape[0]):
        left = near[k] + a_got[k].astype(F32)
        right = far[k] + b_got[k].astype(F32)
        if k:
            send[k - 1][:, :h] = left.astype(BF)
            send[k - 1][:, h:] = right.astype(BF)
        else:
            keep[:, :h] = left
            keep[:, h:] = right


def scatter_rest(mine, theirs, taps, rows, first_in, second_in):
    nf, ns = lax.axis_size("filter"), lax.axis_size("space")
    pairs, share = ns // 2, theirs.shape[2]
    theirs = swap(theirs, "space", 1)
    if halved(rows, share, ns):
        h, n, count = share // 2, nf // 2, taps.shape[0]
        shapes = (
            jax.ShapeDtypeStruct((nf * rows, h), F32),
            jax.ShapeDtypeStruct((nf * rows + 2 * count, h), BF),
            jax.ShapeDtypeStruct((n, rows, h), F32), jax.ShapeDtypeStruct((n, rows, h), F32),
            jax.ShapeDtypeStruct((2, n, rows, h), BF), jax.ShapeDtypeStruct((count, h), F32),
        )
        kernel = functools.partial(halves_first, rows, nf)
        a_keep, a_send, b_keep, b_next, b_send, sums = call(
            kernel, shapes, [], *mine, theirs, taps, us=0.8
        )
        a_got = swap(a_send, "space", 2)
        b_got = swap(b_send, "filter", 1)
        shapes = (
            jax.ShapeDtypeStruct((n, rows, h), F32), jax.ShapeDtypeStruct((n, rows, h), BF),
            jax.ShapeDtypeStruct((n, rows, h), F32), jax.ShapeDtypeStruct((n, rows, h), BF),
            jax.ShapeDtypeStruct((count, h), F32),
        )
        kernel = functools.partial(halves_second, rows, nf)
        near, a_send, far, b_send, taps = call(
            kernel, shapes, [], a_keep, a_got, b_keep, b_next, b_got, sums,
            us=0.6, after=(first_in,),
        )
        a_got = swap(a_send, "filter", 1)
        b_got = swap(b_send, "space", 2)
        shapes = [jax.ShapeDtypeStruct((rows, share), F32)]
        shapes += [jax.ShapeDtypeStruct((rows, share), BF)] * (n - 1)
        keep, *rest = call(
            halves_third, shapes, [], near, a_got, far, b_got, us=0.5, after=(second_in,)
        )
    else:
        step = 1
        while step < ns:
            taps = taps + swap(taps, "space", step)
            step *= 2
        total = mine[0] + theirs[0].astype(F32)
        for k in range(1, pairs):
            send = (mine[k] + theirs[k].astype(F32)).astype(BF)
            total = total + swap(send, "space", 2 * k).astype(F32)
        total = total.reshape(nf // 2, 2, rows, share)
        near = total[:, 0] + swap(total[:, 1].astype(BF), "filter", 1).astype(F32)
        keep, rest = near[0], [near[k].astype(BF) for k in range(1, nf // 2)]
    for k, part in enumerate(rest):
        keep = keep + swap(part, "filter", 2 * (k + 1)).astype(F32)
    return keep, taps


def halo(near, far):
    size = lax.axis_size("space")
    inner = [(i, i ^ 1) for i in range(size)]
    outer = [(i, ((i + 1) ^ 1) - 1) for i in range(1, size - 1)]
    far = lax.ppermute(far, "space", outer)
    return lax.ppermute(near, "space", inner), far


def fill(pad_ref, plane, source):
    rows, width, ch = pad_ref.shape[1] - 2, pad_ref.shape[2], pad_ref.shape[3]
    pad_ref[plane, 1 : rows + 1] = source.astype(F32).reshape(rows, width, ch)
    pad_ref[plane, 0] = jnp.zeros((width, ch), F32)
    pad_ref[plane, rows + 1] = jnp.zeros((width, ch), F32)


def shifted(value, up):
    width = value.shape[0]
    index = lax.broadcasted_iota(jnp.int32, value.shape, 0)
    if up:
        return jnp.where(index == width - 1, 0.0, pltpu.roll(value, width - 1, 0))
    return jnp.where(index == 0, 0.0, pltpu.roll(value, 1, 0))


def conv_row(pad_ref, taps_ref, plane, row, flip):
    sums = [None, None, None]
    for a in range(3):
        for b in range(3):
            da, db = (1 - a, 1 - b) if flip else (a - 1, b - 1)
            line = pad_ref[plane + da, row + db]
            for e in range(3):
                term = taps_ref[pl.ds(a * 9 + b * 3 + e, 1), :] * line
                sums[e] = term if sums[e] is None else sums[e] + term
    lo, hi = (sums[2], sums[0]) if flip else (sums[0], sums[2])
    return sums[1] + shifted(lo, False) + shifted(hi, True)


def load_planes(pad_ref, refs, where, sides, wanted, planes):
    for p in sorted(wanted):
        if p < 0:
            fill(pad_ref, 0, jnp.where(sides[0][0] == 1, sides[1][...], sides[2][...]))
        elif p >= planes:
            fill(pad_ref, planes + 1, jnp.where(sides[0][0] == 1, sides[2][...], sides[1][...]))
        else:
            which, at = where[p]
            fill(pad_ref, p + 1, refs[which][at])


def forward_planes(group, planes, sides, m, taps, up, grad, silu, pad):
    wanted = {p + a for p in group for a in (-1, 0, 1)}
    where = {p: (0, p) for p in range(planes)}
    load_planes(pad, (m,), where, sides, wanted, planes)
    lanes, flat = 2 * WW, m.shape[1]
    for k, p in enumerate(group):

        def strip(f, carry, k=k, p=p):
            lines = [conv_row(pad, taps, p + 1, f * 2 + 1 + r, False) for r in range(2)]
            spatial = jnp.concatenate(lines, axis=0)
            sig = 1.0 / (1.0 + jnp.exp(-spatial))
            cells = pl.ds(pl.multiple_of(f * lanes, lanes), lanes)
            source = pl.ds(pl.multiple_of(p * flat + f * lanes, lanes), lanes)
            slope = sig * (1.0 + spatial * (1.0 - sig))
            grad[k, cells, :] = (up[source, :].astype(F32) * slope).astype(BF)
            silu[k, cells, :] = spatial * sig
            return carry

        lax.fori_loop(0, flat // lanes, strip, 0, unroll=2)


def forward_middle(group, planes, m, taps, up, grad, silu, pad):
    forward_planes(group, planes, (), m, taps, up, grad, silu, pad)


def forward_edges(planes, odd, m, near, far, taps, up, grad, silu, to_near, to_far, pad):
    sides = (odd, near, far)
    forward_planes((0, planes - 1), planes, sides, m, taps, up, grad, silu, pad)
    to_near[...] = jnp.where(odd[0] == 1, grad[0], grad[1])
    to_far[...] = jnp.where(odd[0] == 1, grad[1], grad[0])


def backward_planes(group, where, planes, sides, g0, g1, taps, put, pad):
    wanted = {p + a for p in group for a in (-1, 0, 1)}
    load_planes(pad, (g0, g1), where, sides, wanted, planes)
    lanes, flat = 2 * WW, g0.shape[1]
    for k, p in enumerate(group):

        def strip(f, carry, k=k, p=p):
            lines = [conv_row(pad, taps, p + 1, f * 2 + 1 + r, True) for r in range(2)]
            put(k, p, pl.multiple_of(f * lanes, lanes), jnp.concatenate(lines, axis=0).astype(BF))
            return carry

        lax.fori_loop(0, flat // lanes, strip, 0, unroll=2)


def backward_middle(group, where, planes, g0, g1, taps, out, pad):
    def put(k, p, cell, value):
        out[k, pl.ds(cell, value.shape[0]), :] = value

    backward_planes(group, where, planes, (), g0, g1, taps, put, pad)


def backward_edges(where, planes, steps, me, odd, g0, g1, near, far, taps, inner, whole, *refs):
    out, pad = refs[:-1], refs[-1]
    flat = g0.shape[1]

    def put(k, p, cell, value):
        whole[pl.ds(p * flat + cell, value.shape[0]), :] = value

    backward_planes((0, planes - 1), where, planes, (odd, near, far), g0, g1, taps, put, pad)
    for k in range(1, planes - 1):
        whole[k * flat : (k + 1) * flat, :] = inner[k - 1]
    blk = out[0].shape[0]
    for s, block in zip(steps, out):
        block[...] = whole[pl.ds(pl.multiple_of((me[0] ^ s) * blk, blk), blk), :]


def blocks(me, whole, blk, steps, after):
    def kernel(me, whole, *out):
        for s, block in zip(steps, out):
            block[...] = whole[pl.ds(pl.multiple_of((me[0] ^ s) * blk, blk), blk), :]

    shapes = [jax.ShapeDtypeStruct((blk, whole.shape[1]), BF)] * len(steps)
    return call(kernel, shapes, [], me, whole, us=0.3, after=after)


def taps_kernel(where_grad, planes, norm, steps, odd, m, near, far, g0, g1, s0, s1, vol, *refs):
    parts, refs = refs[: len(steps)], refs[len(steps) :]
    out, output, pad, gpad = refs[0], refs[1], refs[-2], refs[-1]
    for r, part in zip(steps, parts):
        refs[2][:, r * part.shape[1] : (r + 1) * part.shape[1]] = part[...]
    flat, lanes = m.shape[1], 2 * WW
    for p in range(planes):
        which, at = where_grad[p]
        silu = (s0, s1)[which]

        def strip(f, carry, p=p, at=at, silu=silu):
            cells = pl.ds(pl.multiple_of(f * lanes, lanes), lanes)
            lane = pl.ds(pl.multiple_of(p * flat + f * lanes, lanes), lanes)
            turned = jnp.transpose(silu[at, cells, :])
            output[:, lane] = (vol[:, lane].astype(F32) + turned).astype(BF)
            return carry

        lax.fori_loop(0, flat // lanes, strip, 0, unroll=2)
    where = {p: (0, p) for p in range(planes)}
    load_planes(pad, (m,), where, (odd, near, far), range(-1, planes + 1), planes)
    load_planes(gpad, (g0, g1), where_grad, (), range(planes), planes)
    rows, width, ch = pad.shape[1] - 2, pad.shape[2], pad.shape[3]
    sums = tuple(jnp.zeros((8, ch), F32) for _ in range(27))

    def line(at, sums):
        p, h = at // rows, at % rows
        sums = list(sums)
        own = gpad[p + 1, h + 1]
        turned = (shifted(own, True), own, shifted(own, False))
        for a in range(3):
            for b in range(3):
                field = pad[p + a, h + b]
                for e in range(3):
                    prod = (turned[e] * field).reshape(width // 8, 8, ch)
                    sums[a * 9 + b * 3 + e] = sums[a * 9 + b * 3 + e] + jnp.sum(prod, axis=0)
        return tuple(sums)

    sums = lax.fori_loop(0, planes * rows, line, sums)
    for k in range(27):
        out[k : k + 1, :] = jnp.sum(sums[k], axis=0, keepdims=True) * norm
    out[27:, :] = jnp.zeros((5, ch), F32)


def call(kernel, out_shape, scratch, *args, us=1.0, after=(), alias=None):
    specs = [
        pl.BlockSpec(memory_space=pltpu.SMEM if arg.dtype == jnp.int32 else pltpu.VMEM)
        for arg in args
    ]

    def wrapped(*refs):
        kernel(*refs[: len(args)], *refs[len(args) + len(after) :])

    return pl.pallas_call(
        wrapped,
        out_shape=out_shape,
        in_specs=specs + [pl.BlockSpec(memory_space=pl.ANY)] * len(after),
        out_specs=jax.tree.map(lambda _: pl.BlockSpec(memory_space=pltpu.VMEM), out_shape),
        scratch_shapes=scratch,
        input_output_aliases={} if alias is None else {alias: 0},
        compiler_params=pltpu.CompilerParams(vmem_limit_bytes=32 * 1024 * 1024),
        cost_estimate=pl.CostEstimate(
            flops=int(us * 1.15e9), bytes_accessed=1024 * 1024, transcendentals=0
        ),
    )(*args, *after)


def in_place(kernel, shape, leading, base, pieces, us):
    if base is None:
        return call(kernel, shape, [], *leading, *pieces, us=us)

    def wrapped(*refs):
        kernel(*refs[: len(leading)], *refs[len(leading) + 1 :])

    return call(wrapped, shape, [], *leading, base, *pieces, us=us, alias=len(leading))


def fold_volume(turn, base, pieces, steps):
    nf, (ch, blk) = lax.axis_size("filter"), pieces[0].shape
    if ch % 128:
        out = jnp.zeros((nf, ch, blk), BF) if base is None else base
        for t, piece in zip(steps, pieces):
            out = lax.dynamic_update_index_in_dim(out, piece, turn[0] ^ t, 0)
        return out

    def kernel(turn, *refs):
        for t, piece in zip(steps, refs[:-1]):
            lane = pl.ds(pl.multiple_of((turn[0] ^ t) * ch, 128), ch)
            refs[-1][:, lane] = jnp.transpose(piece[...])

    shape = jax.ShapeDtypeStruct((blk, nf * ch), BF)
    return in_place(kernel, shape, (turn,), base, pieces, 0.3 * len(pieces))


def mix_kernel(held, other, vol_t, *out):
    nf, ch, share = len(out), out[0].shape[1], held.shape[2]
    for s in range(0, nf, 2):
        total = None
        for v in range(2 * held.shape[0]):
            block = (other if v % 2 else held)[v // 2, s * ch : (s + 2) * ch, :]
            term = lax.dot_general(
                vol_t[:, v * share : (v + 1) * share], block, (((1,), (1,)), ((), ())),
                preferred_element_type=F32,
            )
            total = term if total is None else total + term
        out[s][...] = total[:, :ch].astype(BF)
        out[s + 1][...] = total[:, ch:].astype(BF)


def mix(vol, held, other, ch, after):
    pairs, rows, share = held.shape
    nf = rows // ch
    if ch % 128:
        vol_t = vol.reshape(rows, vol.shape[2]).T
        weights = jnp.stack([held, other], axis=1).reshape(2 * pairs, rows, share)
        out = jnp.einsum(
            "cvi,voi->co", vol_t.reshape(-1, 2 * pairs, share), weights, preferred_element_type=F32
        ).astype(BF)
        return vol_t, [out[:, s * ch : (s + 1) * ch] for s in range(nf)]
    shapes = [jax.ShapeDtypeStruct((vol.shape[0], ch), BF)] * nf
    return vol, call(mix_kernel, shapes, [], held, other, vol, us=2.6, after=after)


def turned(field):
    def kernel(field, out):
        step = 2 * WW

        def strip(f, carry):
            cells = pl.ds(pl.multiple_of(f * step, step), step)
            out[cells, :] = jnp.transpose(field[:, cells])
            return carry

        lax.fori_loop(0, field.shape[1] // step, strip, 0)

    return call(kernel, jax.ShapeDtypeStruct(field.shape[::-1], BF), [], field, us=1.2)


def unmix(turn, mg, held, other, ch):
    blk = mg.shape[0]
    pairs, rows, share = held.shape
    nf = rows // ch
    if ch % 128:
        weights = jnp.stack([held, other], axis=1).reshape(2 * pairs, rows, share)
        out = jnp.einsum("co,voi->vic", mg, weights, preferred_element_type=F32)
        out = out.astype(BF).reshape(nf, ch, blk)
        return [pick(out, turn[0] ^ s) for s in range(nf)]

    def kernel(turn, mg, held, other, *refs):
        out, back = refs[:-1], refs[-1]
        for v in range(2 * pairs):
            block = (other if v % 2 else held)[v // 2]
            total = lax.dot_general(
                mg[...], block, (((1,), (0,)), ((), ())), preferred_element_type=F32
            )
            turned = jnp.transpose(total).astype(BF)
            for k in range(share // ch):
                back[v * (share // ch) + k] = turned[k * ch : (k + 1) * ch, :]
        for s in range(nf):
            out[s][...] = back[turn[0] ^ s]

    shapes = [jax.ShapeDtypeStruct((ch, blk), BF)] * nf
    return call(
        kernel, shapes, [pltpu.VMEM((nf, ch, blk), BF)], turn, mg, held, other, us=2.2
    )


def split(value):
    high = value.astype(BF)
    return high, (value - high.astype(F32)).astype(BF)


def joined(high, low):
    return high.astype(F32) + low.astype(F32)


def weight_products(base, pieces, steps, vol_t, taps, ch, norm, ns):
    rows, pairs = vol_t.shape[1], ns // 2
    share = rows // ns
    if halved(ch, share, ns):
        count = taps.shape[0]

        def kernel(base, vol, taps, *refs):
            parts, mg, mine, theirs = refs[: len(steps)], refs[len(steps)], refs[-1 - pairs : -1], refs[-1]
            mg[...] = base[...]
            for r, part in zip(steps, parts):
                mg[:, r * ch : (r + 1) * ch] = part[...]
            for r in range(rows // ch):
                row = slice(r * ch, (r + 1) * ch)
                turned = jnp.transpose(mg[:, row])
                for v in range(ns):
                    total = norm * lax.dot_general(
                        turned, vol[:, v * share : (v + 1) * share], (((1,), (0,)), ((), ())),
                        preferred_element_type=F32,
                    )
                    if v % 2:
                        theirs[v // 2, row, :] = total.astype(BF)
                    else:
                        mine[v // 2][row, :] = total
            high, low = split(taps[...])
            theirs[0, rows:, :ch] = high
            theirs[1, rows:, :ch] = low

        shapes = [jax.ShapeDtypeStruct(vol_t.shape, BF)]
        shapes += [jax.ShapeDtypeStruct((rows, share), F32)] * pairs
        shapes.append(jax.ShapeDtypeStruct((pairs, rows + count, share), BF))
        got = call(kernel, shapes, [], base, vol_t, taps, *pieces, us=2.5)
        return got[0], got[1:-1], got[-1]
    if isinstance(base, dict):
        parts = {**base, **dict(zip(steps, pieces))}
        mg = jnp.concatenate([parts[r] for r in sorted(parts)], axis=1)
    else:
        mg = base
        for r, part in zip(steps, pieces):
            mg = lax.dynamic_update_slice_in_dim(mg, part, r * ch, axis=1)
    part = lax.dot_general(mg, vol_t, (((0,), (0,)), ((), ())), preferred_element_type=F32)
    part = (part * norm).reshape(rows, pairs, 2, share)
    theirs = part[:, :, 1].transpose(1, 0, 2).astype(BF)
    return mg, [part[:, k, 0] for k in range(pairs)], theirs


def assemble(me, base, pieces, steps):
    blk, ch = pieces[0].shape

    def kernel(me, *refs):
        for s, piece in zip(steps, refs[:-1]):
            refs[-1][me[0] ^ s] = piece[...]

    shape = jax.ShapeDtypeStruct((lax.axis_size("filter"), blk, ch), BF)
    return in_place(kernel, shape, (me,), base, pieces, 0.5)


def assemble_last(me, odd, base, pieces, steps, planes):
    nf, blk, ch = base.shape
    flat = nf * blk // planes

    def kernel(me, odd, base, *refs):
        out, near, far = refs[-3:]
        for s, piece in zip(steps, refs[:-3]):
            out[me[0] ^ s] = piece[...]
        for k in range(flat // blk):
            first, last = out[k], out[nf - flat // blk + k]
            near[k * blk : (k + 1) * blk, :] = jnp.where(odd[0] == 1, first, last)
            far[k * blk : (k + 1) * blk, :] = jnp.where(odd[0] == 1, last, first)

    edge = jax.ShapeDtypeStruct((flat, ch), BF)
    shapes = (jax.ShapeDtypeStruct((nf, blk, ch), BF), edge, edge)
    out, near, far = call(kernel, shapes, [], me, odd, base, *pieces, us=0.8, alias=2)
    return out.reshape(planes, flat, ch), near, far


def finish(me, up, base, pieces, steps):
    blk = pieces[0].shape[1]

    def kernel(me, up, *refs):
        for s, piece in zip(steps, refs[:-1]):
            lane = pl.ds(pl.multiple_of((me[0] ^ s) * blk, 128), blk)
            refs[-1][:, lane] = (up[:, lane].astype(F32) + piece[...].astype(F32)).astype(BF)

    shape = jax.ShapeDtypeStruct(up.shape, BF)
    return in_place(kernel, shape, (me, up), base, pieces, 0.1)


def body(volume, mixing, kernel_taps, upstream):
    ch, planes, flat = volume.shape
    height = flat // WW
    nf, ns = lax.axis_size("filter"), lax.axis_size("space")
    me, me_space = lax.axis_index("filter"), lax.axis_index("space")
    total = planes * flat
    blk = total // nf
    norm = 1.0 / math.sqrt(ns * total)
    edges, middle = (0, planes - 1), tuple(range(1, planes - 1))
    groups = (edges, middle)
    turn = jnp.reshape(me ^ (me_space * (nf // ns)), (1,)).astype(jnp.int32)

    odd = jnp.reshape(me_space & 1, (1,)).astype(jnp.int32)
    own = jnp.reshape(me, (1,)).astype(jnp.int32)

    vol = volume.reshape(ch, total)
    mid = nf // 2
    early = [0, mid]
    later = [s for s in range(mid + 1, nf)]
    last = list(range(1, mid))

    def some(parts, steps):
        return [parts[s] for s in steps]

    send = [lax.dynamic_slice_in_dim(vol, (me ^ s) * blk, blk, axis=1) for s in range(nf)]
    pieces = exchange(send, "filter")
    steps = early + [mid + 1]
    vol_1 = fold_volume(turn, None, some(pieces, steps), steps)
    vol_2 = fold_volume(turn, vol_1, some(pieces, [mid + 2, 1, 2]), [mid + 2, 1, 2])
    rest = later[2:] + last[2:]
    vol_3 = fold_volume(turn, vol_2, some(pieces, rest), rest)
    held, other = gather_weights(mixing, me_space, send, vol_2)
    up = upstream.reshape(ch, total)
    up_t = turned(up)
    vol_t, prod = mix(vol_3, held, other, ch, (up_t,))

    got = exchange(prod, "filter")
    near_steps, cross = list(range(2, mid)), list(range(mid, nf))
    mixed = assemble(own, None, some(got, [0, 1]), [0, 1])
    mixed = assemble(own, mixed, some(got, near_steps), near_steps)
    mixed, near, far = assemble_last(own, odd, mixed, some(got, cross), cross, planes)
    near, far = halo(near, far)

    taps = kernel_taps.T
    pad = pltpu.VMEM((planes + 2, height + 2, WW, ch), F32)

    def grad_shapes(g):
        return (
            jax.ShapeDtypeStruct((len(g), flat, ch), BF),
            jax.ShapeDtypeStruct((len(g), flat, ch), F32),
        )

    edge = jax.ShapeDtypeStruct((flat, ch), BF)
    grad_middle, silu_middle = call(
        functools.partial(forward_middle, middle, planes), grad_shapes(middle), [pad],
        mixed, taps, up_t, us=3.2,
    )
    grad_edges, silu_edges, to_near, to_far = call(
        functools.partial(forward_edges, planes), grad_shapes(edges) + (edge, edge), [pad],
        odd, mixed, near, far, taps, up_t, us=3.2, after=(grad_middle,),
    )
    grad_near, grad_far = halo(to_near, to_far)
    where = {p: (i, k) for i, g in enumerate(groups) for k, p in enumerate(g)}
    mg_middle = call(
        functools.partial(backward_middle, middle, where, planes),
        jax.ShapeDtypeStruct((len(middle), flat, ch), BF), [pad],
        grad_edges, grad_middle, taps, us=2.3,
    )
    steps = [0, 1] + cross
    whole, *send = call(
        functools.partial(backward_edges, where, planes, steps),
        [jax.ShapeDtypeStruct((total, ch), BF)] + [jax.ShapeDtypeStruct((blk, ch), BF)] * len(steps),
        [pad], own, odd, grad_edges, grad_middle, grad_near, grad_far, taps, mg_middle, us=2.8,
    )
    got = {s: swap(block, "filter", s) if s else block for s, block in zip(steps, send)}

    wide = ch % 128 == 0
    side = some(got, [0, 1])
    shapes = (jax.ShapeDtypeStruct((32, ch), F32), jax.ShapeDtypeStruct((ch, total), BF))
    shapes += (jax.ShapeDtypeStruct((blk, nf * ch), BF),) if wide else ()
    kernel = functools.partial(taps_kernel, where, planes, norm, [0, 1] if wide else [])
    taps_grad, output, *mg = call(
        kernel, shapes, [pad, pad],
        odd, mixed, near, far, grad_edges, grad_middle, silu_edges, silu_middle, vol,
        *(side if wide else []), us=5.8,
    )
    output = output.reshape(ch, planes, flat)
    send = blocks(own, whole, blk, near_steps, (taps_grad,))
    got.update((s, swap(block, "filter", s)) for s, block in zip(near_steps, send))
    base = mg[0] if wide else dict(zip([0, 1], side))
    rest = cross + near_steps
    mg_all, mine, theirs = weight_products(
        base, some(got, rest), rest, vol_t, taps_grad, ch, norm, ns
    )
    back = unmix(turn, mg_all, held, other, ch)
    got = exchange(back, "filter")
    volume_grad_1 = finish(own, up, None, some(got, [0, 1]), [0, 1])
    volume_grad_2 = finish(own, up, volume_grad_1, some(got, cross), cross)
    mixing_grad, taps_grad = scatter_rest(
        mine, theirs, taps_grad, ch, volume_grad_1, volume_grad_2
    )
    volume_grad = finish(own, up, volume_grad_2, some(got, near_steps), near_steps)
    volume_grad = volume_grad.reshape(ch, planes, flat)
    return (output, volume_grad, mixing_grad, taps_grad[:27].T)


def solution(mesh):
    in_specs = (
        P("filter", "space", None),
        P("filter", None),
        P("filter", None),
        P("filter", "space", None),
    )
    out_specs = (
        P("filter", "space", None),
        P("filter", "space", None),
        P("filter", "space"),
        P("filter", None),
    )
    return jax.shard_map(body, mesh=mesh, in_specs=in_specs, out_specs=out_specs, check_vma=False)
```

```python
import functools
import math

import jax
import jax.numpy as jnp
from jax import lax
from jax.experimental import pallas as pl
from jax.experimental.pallas import tpu as pltpu
from jax.sharding import PartitionSpec as P

WW = 64
BF = jnp.bfloat16
F32 = jnp.float32


def swap(block, axis, step):
    size = lax.axis_size(axis)
    return lax.ppermute(block, axis, [(i, i ^ step) for i in range(size)])


def exchange(pieces, axis):
    size = len(pieces)
    order = list(range(size // 2, size)) + list(range(1, size // 2))
    got = {0: pieces[0]}
    for s in order:
        got[s] = swap(pieces[s], axis, s)
    return [got[s] for s in range(size)]


def place(pieces, shift):
    out = jnp.zeros((len(pieces),) + pieces[0].shape, pieces[0].dtype)
    for s, piece in enumerate(pieces):
        out = lax.dynamic_update_index_in_dim(out, piece, shift ^ s, 0)
    return out


def pick(blocks, index):
    return lax.dynamic_index_in_dim(blocks, index, 0, keepdims=False)


def join(parts, after, us=0.4):
    def kernel(*refs):
        for k in range(len(parts)):
            refs[-1][k] = refs[k][...]

    shape = jax.ShapeDtypeStruct((len(parts),) + parts[0].shape, parts[0].dtype)
    return call(kernel, shape, [], *parts, us=us, after=after)


def gather_weights(mixing, me_space, send, arrived):
    rows, cols = mixing.shape
    nf, ns = lax.axis_size("filter"), lax.axis_size("space")
    share, pairs = cols // ns, ns // 2
    own = lax.dynamic_slice_in_dim(mixing, me_space * share, share, axis=1)
    even = join([own] + [swap(own, "filter", s) for s in range(2, nf, 2)], send[nf // 2 :])
    first = [even] + [swap(even, "space", s) for s in range(2, ns, 2)]
    odd = swap(even, "filter", 1)
    second = [odd] + [swap(odd, "space", s) for s in range(2, ns, 2)]

    def kernel(*refs):
        for k in range(pairs):
            for r in range(nf):
                source = refs[pairs * (r % 2) + k]
                refs[-1][k, r * rows : (r + 1) * rows, :] = source[r // 2]

    shape = jax.ShapeDtypeStruct((pairs, nf * rows, share), BF)
    held = call(kernel, shape, [], *first, *second, us=0.6, after=(arrived,))
    return held, swap(held, "space", 1)


def halved(ch, share, ns):
    return ns == 4 and share == 2 * ch and ch % 128 == 0


def halves_first(rows, nf, mine0, mine1, got, taps, a_keep, a_send, b_keep, b_next, b_send, sums):
    h, count = a_keep.shape[1], taps.shape[0]
    total = joined(*split(taps[...])) + joined(got[0, nf * rows :, :h], got[1, nf * rows :, :h])
    high, low = split(total)
    a_send[nf * rows : nf * rows + count, :] = high
    a_send[nf * rows + count :, :] = low
    sums[...] = joined(high, low)
    for r in range(nf):
        row = slice(r * rows, (r + 1) * rows)
        own = mine0[row, :] + got[0, row, :].astype(F32)
        step = mine1[row, :] + got[1, row, :].astype(F32)
        a_keep[row, :] = own[:, :h]
        a_send[row, :] = step[:, :h].astype(BF)
        if r % 2:
            b_send[0, r // 2] = own[:, h:].astype(BF)
            b_send[1, r // 2] = step[:, h:].astype(BF)
        else:
            b_keep[r // 2] = own[:, h:]
            b_next[r // 2] = step[:, h:]


def halves_second(rows, nf, a_keep, a_got, b_keep, b_next, b_got, sums, near, a_send, far, b_send, taps):
    count = taps.shape[0]
    high, low = a_got[nf * rows : nf * rows + count, :], a_got[nf * rows + count :, :]
    taps[...] = sums[...] + joined(high, low)
    for r in range(nf):
        row = slice(r * rows, (r + 1) * rows)
        own = a_keep[row, :] + a_got[row, :].astype(F32)
        if r % 2:
            a_send[r // 2] = own.astype(BF)
        else:
            near[r // 2] = own
    far[...] = b_keep[...] + b_got[0].astype(F32)
    b_send[...] = (b_next[...] + b_got[1].astype(F32)).astype(BF)


def halves_third(near, a_got, far, b_got, keep, *send):
    h = near.shape[2]
    for k in range(near.shape[0]):
        left = near[k] + a_got[k].astype(F32)
        right = far[k] + b_got[k].astype(F32)
        if k:
            send[k - 1][:, :h] = left.astype(BF)
            send[k - 1][:, h:] = right.astype(BF)
        else:
            keep[:, :h] = left
            keep[:, h:] = right


def scatter_rest(mine, theirs, taps, rows, first_in, second_in):
    nf, ns = lax.axis_size("filter"), lax.axis_size("space")
    pairs, share = ns // 2, theirs.shape[2]
    theirs = swap(theirs, "space", 1)
    if halved(rows, share, ns):
        h, n, count = share // 2, nf // 2, taps.shape[0]
        shapes = (
            jax.ShapeDtypeStruct((nf * rows, h), F32),
            jax.ShapeDtypeStruct((nf * rows + 2 * count, h), BF),
            jax.ShapeDtypeStruct((n, rows, h), F32), jax.ShapeDtypeStruct((n, rows, h), F32),
            jax.ShapeDtypeStruct((2, n, rows, h), BF), jax.ShapeDtypeStruct((count, h), F32),
        )
        kernel = functools.partial(halves_first, rows, nf)
        a_keep, a_send, b_keep, b_next, b_send, sums = call(
            kernel, shapes, [], *mine, theirs, taps, us=0.1
        )
        a_got = swap(a_send, "space", 2)
        b_got = swap(b_send, "filter", 1)
        shapes = (
            jax.ShapeDtypeStruct((n, rows, h), F32), jax.ShapeDtypeStruct((n, rows, h), BF),
            jax.ShapeDtypeStruct((n, rows, h), F32), jax.ShapeDtypeStruct((n, rows, h), BF),
            jax.ShapeDtypeStruct((count, h), F32),
        )
        kernel = functools.partial(halves_second, rows, nf)
        near, a_send, far, b_send, taps = call(
            kernel, shapes, [], a_keep, a_got, b_keep, b_next, b_got, sums,
            us=0.1, after=(first_in,),
        )
        a_got = swap(a_send, "filter", 1)
        b_got = swap(b_send, "space", 2)
        shapes = [jax.ShapeDtypeStruct((rows, share), F32)]
        shapes += [jax.ShapeDtypeStruct((rows, share), BF)] * (n - 1)
        keep, *rest = call(
            halves_third, shapes, [], near, a_got, far, b_got, us=0.1, after=(second_in,)
        )
    else:
        step = 1
        while step < ns:
            taps = taps + swap(taps, "space", step)
            step *= 2
        total = mine[0] + theirs[0].astype(F32)
        for k in range(1, pairs):
            send = (mine[k] + theirs[k].astype(F32)).astype(BF)
            total = total + swap(send, "space", 2 * k).astype(F32)
        total = total.reshape(nf // 2, 2, rows, share)
        near = total[:, 0] + swap(total[:, 1].astype(BF), "filter", 1).astype(F32)
        keep, rest = near[0], [near[k].astype(BF) for k in range(1, nf // 2)]
    for k, part in enumerate(rest):
        keep = keep + swap(part, "filter", 2 * (k + 1)).astype(F32)
    return keep, taps


def halo(near, far):
    size = lax.axis_size("space")
    inner = [(i, i ^ 1) for i in range(size)]
    outer = [(i, ((i + 1) ^ 1) - 1) for i in range(1, size - 1)]
    far = lax.ppermute(far, "space", outer)
    return lax.ppermute(near, "space", inner), far


def fill(pad_ref, plane, source):
    rows, width, ch = pad_ref.shape[1] - 2, pad_ref.shape[2], pad_ref.shape[3]
    pad_ref[plane, 1 : rows + 1] = source.astype(F32).reshape(rows, width, ch)
    pad_ref[plane, 0] = jnp.zeros((width, ch), F32)
    pad_ref[plane, rows + 1] = jnp.zeros((width, ch), F32)


def shifted(value, up):
    width = value.shape[0]
    index = lax.broadcasted_iota(jnp.int32, value.shape, 0)
    if up:
        return jnp.where(index == width - 1, 0.0, pltpu.roll(value, width - 1, 0))
    return jnp.where(index == 0, 0.0, pltpu.roll(value, 1, 0))


def conv_row(pad_ref, taps_ref, plane, row, flip):
    sums = [None, None, None]
    for a in range(3):
        for b in range(3):
            da, db = (1 - a, 1 - b) if flip else (a - 1, b - 1)
            line = pad_ref[plane + da, row + db]
            for e in range(3):
                term = taps_ref[pl.ds(a * 9 + b * 3 + e, 1), :] * line
                sums[e] = term if sums[e] is None else sums[e] + term
    lo, hi = (sums[2], sums[0]) if flip else (sums[0], sums[2])
    return sums[1] + shifted(lo, False) + shifted(hi, True)


def load_planes(pad_ref, refs, where, sides, wanted, planes):
    for p in sorted(wanted):
        if p < 0:
            fill(pad_ref, 0, jnp.where(sides[0][0] == 1, sides[1][...], sides[2][...]))
        elif p >= planes:
            fill(pad_ref, planes + 1, jnp.where(sides[0][0] == 1, sides[2][...], sides[1][...]))
        else:
            which, at = where[p]
            fill(pad_ref, p + 1, refs[which][at])


def forward_planes(group, planes, sides, m, taps, up, grad, silu, pad):
    wanted = {p + a for p in group for a in (-1, 0, 1)}
    where = {p: (0, p) for p in range(planes)}
    load_planes(pad, (m,), where, sides, wanted, planes)
    lanes, flat = 2 * WW, m.shape[1]
    for k, p in enumerate(group):

        def strip(f, carry, k=k, p=p):
            lines = [conv_row(pad, taps, p + 1, f * 2 + 1 + r, False) for r in range(2)]
            spatial = jnp.concatenate(lines, axis=0)
            sig = 1.0 / (1.0 + jnp.exp(-spatial))
            cells = pl.ds(pl.multiple_of(f * lanes, lanes), lanes)
            source = pl.ds(pl.multiple_of(p * flat + f * lanes, lanes), lanes)
            slope = sig * (1.0 + spatial * (1.0 - sig))
            grad[k, cells, :] = (up[source, :].astype(F32) * slope).astype(BF)
            silu[k, cells, :] = spatial * sig
            return carry

        lax.fori_loop(0, flat // lanes, strip, 0, unroll=2)


def forward_middle(group, planes, m, taps, up, grad, silu, pad):
    forward_planes(group, planes, (), m, taps, up, grad, silu, pad)


def forward_edges(planes, odd, m, near, far, taps, up, grad, silu, to_near, to_far, pad):
    sides = (odd, near, far)
    forward_planes((0, planes - 1), planes, sides, m, taps, up, grad, silu, pad)
    to_near[...] = jnp.where(odd[0] == 1, grad[0], grad[1])
    to_far[...] = jnp.where(odd[0] == 1, grad[1], grad[0])


def backward_planes(group, where, planes, sides, g0, g1, taps, put, pad):
    wanted = {p + a for p in group for a in (-1, 0, 1)}
    load_planes(pad, (g0, g1), where, sides, wanted, planes)
    lanes, flat = 2 * WW, g0.shape[1]
    for k, p in enumerate(group):

        def strip(f, carry, k=k, p=p):
            lines = [conv_row(pad, taps, p + 1, f * 2 + 1 + r, True) for r in range(2)]
            put(k, p, pl.multiple_of(f * lanes, lanes), jnp.concatenate(lines, axis=0).astype(BF))
            return carry

        lax.fori_loop(0, flat // lanes, strip, 0, unroll=2)


def backward_middle(group, where, planes, g0, g1, taps, out, pad):
    def put(k, p, cell, value):
        out[k, pl.ds(cell, value.shape[0]), :] = value

    backward_planes(group, where, planes, (), g0, g1, taps, put, pad)


def backward_edges(where, planes, steps, me, odd, g0, g1, near, far, taps, inner, whole, *refs):
    out, pad = refs[:-1], refs[-1]
    flat = g0.shape[1]

    def put(k, p, cell, value):
        whole[pl.ds(p * flat + cell, value.shape[0]), :] = value

    backward_planes((0, planes - 1), where, planes, (odd, near, far), g0, g1, taps, put, pad)
    for k in range(1, planes - 1):
        whole[k * flat : (k + 1) * flat, :] = inner[k - 1]
    blk = out[0].shape[0]
    for s, block in zip(steps, out):
        block[...] = whole[pl.ds(pl.multiple_of((me[0] ^ s) * blk, blk), blk), :]


def blocks(me, whole, blk, steps, after):
    def kernel(me, whole, *out):
        for s, block in zip(steps, out):
            block[...] = whole[pl.ds(pl.multiple_of((me[0] ^ s) * blk, blk), blk), :]

    shapes = [jax.ShapeDtypeStruct((blk, whole.shape[1]), BF)] * len(steps)
    return call(kernel, shapes, [], me, whole, us=0.3, after=after)


def taps_kernel(where_grad, planes, norm, steps, odd, m, near, far, g0, g1, s0, s1, vol, *refs):
    parts, refs = refs[: len(steps)], refs[len(steps) :]
    out, output, pad, gpad = refs[0], refs[1], refs[-2], refs[-1]
    for r, part in zip(steps, parts):
        refs[2][:, r * part.shape[1] : (r + 1) * part.shape[1]] = part[...]
    flat, lanes = m.shape[1], 2 * WW
    for p in range(planes):
        which, at = where_grad[p]
        silu = (s0, s1)[which]

        def strip(f, carry, p=p, at=at, silu=silu):
            cells = pl.ds(pl.multiple_of(f * lanes, lanes), lanes)
            lane = pl.ds(pl.multiple_of(p * flat + f * lanes, lanes), lanes)
            turned = jnp.transpose(silu[at, cells, :])
            output[:, lane] = (vol[:, lane].astype(F32) + turned).astype(BF)
            return carry

        lax.fori_loop(0, flat // lanes, strip, 0, unroll=2)
    where = {p: (0, p) for p in range(planes)}
    load_planes(pad, (m,), where, (odd, near, far), range(-1, planes + 1), planes)
    load_planes(gpad, (g0, g1), where_grad, (), range(planes), planes)
    rows, width, ch = pad.shape[1] - 2, pad.shape[2], pad.shape[3]
    sums = tuple(jnp.zeros((8, ch), F32) for _ in range(27))

    def line(at, sums):
        p, h = at // rows, at % rows
        sums = list(sums)
        own = gpad[p + 1, h + 1]
        turned = (shifted(own, True), own, shifted(own, False))
        for a in range(3):
            for b in range(3):
                field = pad[p + a, h + b]
                for e in range(3):
                    prod = (turned[e] * field).reshape(width // 8, 8, ch)
                    sums[a * 9 + b * 3 + e] = sums[a * 9 + b * 3 + e] + jnp.sum(prod, axis=0)
        return tuple(sums)

    sums = lax.fori_loop(0, planes * rows, line, sums)
    for k in range(27):
        out[k : k + 1, :] = jnp.sum(sums[k], axis=0, keepdims=True) * norm
    out[27:, :] = jnp.zeros((5, ch), F32)


def call(kernel, out_shape, scratch, *args, us=1.0, after=(), alias=None):
    specs = [
        pl.BlockSpec(memory_space=pltpu.SMEM if arg.dtype == jnp.int32 else pltpu.VMEM)
        for arg in args
    ]

    def wrapped(*refs):
        kernel(*refs[: len(args)], *refs[len(args) + len(after) :])

    return pl.pallas_call(
        wrapped,
        out_shape=out_shape,
        in_specs=specs + [pl.BlockSpec(memory_space=pl.ANY)] * len(after),
        out_specs=jax.tree.map(lambda _: pl.BlockSpec(memory_space=pltpu.VMEM), out_shape),
        scratch_shapes=scratch,
        input_output_aliases={} if alias is None else {alias: 0},
        compiler_params=pltpu.CompilerParams(vmem_limit_bytes=32 * 1024 * 1024),
        cost_estimate=pl.CostEstimate(
            flops=int(us * 1.15e9), bytes_accessed=1024 * 1024, transcendentals=0
        ),
    )(*args, *after)


def in_place(kernel, shape, leading, base, pieces, us):
    if base is None:
        return call(kernel, shape, [], *leading, *pieces, us=us)

    def wrapped(*refs):
        kernel(*refs[: len(leading)], *refs[len(leading) + 1 :])

    return call(wrapped, shape, [], *leading, base, *pieces, us=us, alias=len(leading))


def fold_volume(turn, base, pieces, steps):
    nf, (ch, blk) = lax.axis_size("filter"), pieces[0].shape
    if ch % 128:
        out = jnp.zeros((nf, ch, blk), BF) if base is None else base
        for t, piece in zip(steps, pieces):
            out = lax.dynamic_update_index_in_dim(out, piece, turn[0] ^ t, 0)
        return out

    def kernel(turn, *refs):
        for t, piece in zip(steps, refs[:-1]):
            lane = pl.ds(pl.multiple_of((turn[0] ^ t) * ch, 128), ch)
            refs[-1][:, lane] = jnp.transpose(piece[...])

    shape = jax.ShapeDtypeStruct((blk, nf * ch), BF)
    return in_place(kernel, shape, (turn,), base, pieces, 0.3 * len(pieces))


def mix_kernel(held, other, vol_t, *out):
    nf, ch, share = len(out), out[0].shape[1], held.shape[2]
    for s in range(0, nf, 2):
        total = None
        for v in range(2 * held.shape[0]):
            block = (other if v % 2 else held)[v // 2, s * ch : (s + 2) * ch, :]
            term = lax.dot_general(
                vol_t[:, v * share : (v + 1) * share], block, (((1,), (1,)), ((), ())),
                preferred_element_type=F32,
            )
            total = term if total is None else total + term
        out[s][...] = total[:, :ch].astype(BF)
        out[s + 1][...] = total[:, ch:].astype(BF)


def mix(vol, held, other, ch, after):
    pairs, rows, share = held.shape
    nf = rows // ch
    if ch % 128:
        vol_t = vol.reshape(rows, vol.shape[2]).T
        weights = jnp.stack([held, other], axis=1).reshape(2 * pairs, rows, share)
        out = jnp.einsum(
            "cvi,voi->co", vol_t.reshape(-1, 2 * pairs, share), weights, preferred_element_type=F32
        ).astype(BF)
        return vol_t, [out[:, s * ch : (s + 1) * ch] for s in range(nf)]
    shapes = [jax.ShapeDtypeStruct((vol.shape[0], ch), BF)] * nf
    return vol, call(mix_kernel, shapes, [], held, other, vol, us=2.6, after=after)


def turned(field):
    def kernel(field, out):
        step = 2 * WW

        def strip(f, carry):
            cells = pl.ds(pl.multiple_of(f * step, step), step)
            out[cells, :] = jnp.transpose(field[:, cells])
            return carry

        lax.fori_loop(0, field.shape[1] // step, strip, 0)

    return call(kernel, jax.ShapeDtypeStruct(field.shape[::-1], BF), [], field, us=1.2)


def unmix(turn, mg, held, other, ch):
    blk = mg.shape[0]
    pairs, rows, share = held.shape
    nf = rows // ch
    if ch % 128:
        weights = jnp.stack([held, other], axis=1).reshape(2 * pairs, rows, share)
        out = jnp.einsum("co,voi->vic", mg, weights, preferred_element_type=F32)
        out = out.astype(BF).reshape(nf, ch, blk)
        return [pick(out, turn[0] ^ s) for s in range(nf)]

    def kernel(turn, mg, held, other, *refs):
        out, back = refs[:-1], refs[-1]
        for v in range(2 * pairs):
            block = (other if v % 2 else held)[v // 2]
            total = lax.dot_general(
                mg[...], block, (((1,), (0,)), ((), ())), preferred_element_type=F32
            )
            turned = jnp.transpose(total).astype(BF)
            for k in range(share // ch):
                back[v * (share // ch) + k] = turned[k * ch : (k + 1) * ch, :]
        for s in range(nf):
            out[s][...] = back[turn[0] ^ s]

    shapes = [jax.ShapeDtypeStruct((ch, blk), BF)] * nf
    return call(
        kernel, shapes, [pltpu.VMEM((nf, ch, blk), BF)], turn, mg, held, other, us=2.2
    )


def split(value):
    high = value.astype(BF)
    return high, (value - high.astype(F32)).astype(BF)


def joined(high, low):
    return high.astype(F32) + low.astype(F32)


def weight_products(base, pieces, steps, vol_t, taps, ch, norm, ns):
    rows, pairs = vol_t.shape[1], ns // 2
    share = rows // ns
    if halved(ch, share, ns):
        count = taps.shape[0]

        def kernel(base, vol, taps, *refs):
            parts, mg, mine, theirs = refs[: len(steps)], refs[len(steps)], refs[-1 - pairs : -1], refs[-1]
            mg[...] = base[...]
            for r, part in zip(steps, parts):
                mg[:, r * ch : (r + 1) * ch] = part[...]
            for r in range(rows // ch):
                row = slice(r * ch, (r + 1) * ch)
                turned = jnp.transpose(mg[:, row])
                for v in range(ns):
                    total = norm * lax.dot_general(
                        turned, vol[:, v * share : (v + 1) * share], (((1,), (0,)), ((), ())),
                        preferred_element_type=F32,
                    )
                    if v % 2:
                        theirs[v // 2, row, :] = total.astype(BF)
                    else:
                        mine[v // 2][row, :] = total
            high, low = split(taps[...])
            theirs[0, rows:, :ch] = high
            theirs[1, rows:, :ch] = low

        shapes = [jax.ShapeDtypeStruct(vol_t.shape, BF)]
        shapes += [jax.ShapeDtypeStruct((rows, share), F32)] * pairs
        shapes.append(jax.ShapeDtypeStruct((pairs, rows + count, share), BF))
        got = call(kernel, shapes, [], base, vol_t, taps, *pieces, us=2.5)
        return got[0], got[1:-1], got[-1]
    if isinstance(base, dict):
        parts = {**base, **dict(zip(steps, pieces))}
        mg = jnp.concatenate([parts[r] for r in sorted(parts)], axis=1)
    else:
        mg = base
        for r, part in zip(steps, pieces):
            mg = lax.dynamic_update_slice_in_dim(mg, part, r * ch, axis=1)
    part = lax.dot_general(mg, vol_t, (((0,), (0,)), ((), ())), preferred_element_type=F32)
    part = (part * norm).reshape(rows, pairs, 2, share)
    theirs = part[:, :, 1].transpose(1, 0, 2).astype(BF)
    return mg, [part[:, k, 0] for k in range(pairs)], theirs


def assemble(me, base, pieces, steps):
    blk, ch = pieces[0].shape

    def kernel(me, *refs):
        for s, piece in zip(steps, refs[:-1]):
            refs[-1][me[0] ^ s] = piece[...]

    shape = jax.ShapeDtypeStruct((lax.axis_size("filter"), blk, ch), BF)
    return in_place(kernel, shape, (me,), base, pieces, 0.5)


def assemble_last(me, odd, base, pieces, steps, planes):
    nf, blk, ch = base.shape
    flat = nf * blk // planes

    def kernel(me, odd, base, *refs):
        out, near, far = refs[-3:]
        for s, piece in zip(steps, refs[:-3]):
            out[me[0] ^ s] = piece[...]
        for k in range(flat // blk):
            first, last = out[k], out[nf - flat // blk + k]
            near[k * blk : (k + 1) * blk, :] = jnp.where(odd[0] == 1, first, last)
            far[k * blk : (k + 1) * blk, :] = jnp.where(odd[0] == 1, last, first)

    edge = jax.ShapeDtypeStruct((flat, ch), BF)
    shapes = (jax.ShapeDtypeStruct((nf, blk, ch), BF), edge, edge)
    out, near, far = call(kernel, shapes, [], me, odd, base, *pieces, us=0.8, alias=2)
    return out.reshape(planes, flat, ch), near, far


def finish(me, up, base, pieces, steps):
    blk = pieces[0].shape[1]

    def kernel(me, up, *refs):
        for s, piece in zip(steps, refs[:-1]):
            lane = pl.ds(pl.multiple_of((me[0] ^ s) * blk, 128), blk)
            refs[-1][:, lane] = (up[:, lane].astype(F32) + piece[...].astype(F32)).astype(BF)

    shape = jax.ShapeDtypeStruct(up.shape, BF)
    return in_place(kernel, shape, (me, up), base, pieces, 0.1)


def body(volume, mixing, kernel_taps, upstream):
    ch, planes, flat = volume.shape
    height = flat // WW
    nf, ns = lax.axis_size("filter"), lax.axis_size("space")
    me, me_space = lax.axis_index("filter"), lax.axis_index("space")
    total = planes * flat
    blk = total // nf
    norm = 1.0 / math.sqrt(ns * total)
    edges, middle = (0, planes - 1), tuple(range(1, planes - 1))
    groups = (edges, middle)
    turn = jnp.reshape(me ^ (me_space * (nf // ns)), (1,)).astype(jnp.int32)

    odd = jnp.reshape(me_space & 1, (1,)).astype(jnp.int32)
    own = jnp.reshape(me, (1,)).astype(jnp.int32)

    vol = volume.reshape(ch, total)
    mid = nf // 2
    early = [0, mid]
    later = [s for s in range(mid + 1, nf)]
    last = list(range(1, mid))

    def some(parts, steps):
        return [parts[s] for s in steps]

    send = [lax.dynamic_slice_in_dim(vol, (me ^ s) * blk, blk, axis=1) for s in range(nf)]
    pieces = exchange(send, "filter")
    steps = early + [mid + 1]
    vol_1 = fold_volume(turn, None, some(pieces, steps), steps)
    vol_2 = fold_volume(turn, vol_1, some(pieces, [mid + 2, 1, 2]), [mid + 2, 1, 2])
    rest = later[2:] + last[2:]
    vol_3 = fold_volume(turn, vol_2, some(pieces, rest), rest)
    held, other = gather_weights(mixing, me_space, send, vol_2)
    up = upstream.reshape(ch, total)
    up_t = turned(up)
    vol_t, prod = mix(vol_3, held, other, ch, (up_t,))

    got = exchange(prod, "filter")
    near_steps, cross = list(range(2, mid)), list(range(mid, nf))
    mixed = assemble(own, None, some(got, [0, 1]), [0, 1])
    mixed = assemble(own, mixed, some(got, near_steps), near_steps)
    mixed, near, far = assemble_last(own, odd, mixed, some(got, cross), cross, planes)
    near, far = halo(near, far)

    taps = kernel_taps.T
    pad = pltpu.VMEM((planes + 2, height + 2, WW, ch), F32)

    def grad_shapes(g):
        return (
            jax.ShapeDtypeStruct((len(g), flat, ch), BF),
            jax.ShapeDtypeStruct((len(g), flat, ch), F32),
        )

    edge = jax.ShapeDtypeStruct((flat, ch), BF)
    grad_middle, silu_middle = call(
        functools.partial(forward_middle, middle, planes), grad_shapes(middle), [pad],
        mixed, taps, up_t, us=3.2,
    )
    grad_edges, silu_edges, to_near, to_far = call(
        functools.partial(forward_edges, planes), grad_shapes(edges) + (edge, edge), [pad],
        odd, mixed, near, far, taps, up_t, us=3.2, after=(grad_middle,),
    )
    grad_near, grad_far = halo(to_near, to_far)
    where = {p: (i, k) for i, g in enumerate(groups) for k, p in enumerate(g)}
    mg_middle = call(
        functools.partial(backward_middle, middle, where, planes),
        jax.ShapeDtypeStruct((len(middle), flat, ch), BF), [pad],
        grad_edges, grad_middle, taps, us=2.3,
    )
    steps = [0, 1] + cross
    whole, *send = call(
        functools.partial(backward_edges, where, planes, steps),
        [jax.ShapeDtypeStruct((total, ch), BF)] + [jax.ShapeDtypeStruct((blk, ch), BF)] * len(steps),
        [pad], own, odd, grad_edges, grad_middle, grad_near, grad_far, taps, mg_middle, us=2.8,
    )
    got = {s: swap(block, "filter", s) if s else block for s, block in zip(steps, send)}

    wide = ch % 128 == 0
    side = some(got, [0, 1])
    shapes = (jax.ShapeDtypeStruct((32, ch), F32), jax.ShapeDtypeStruct((ch, total), BF))
    shapes += (jax.ShapeDtypeStruct((blk, nf * ch), BF),) if wide else ()
    kernel = functools.partial(taps_kernel, where, planes, norm, [0, 1] if wide else [])
    taps_grad, output, *mg = call(
        kernel, shapes, [pad, pad],
        odd, mixed, near, far, grad_edges, grad_middle, silu_edges, silu_middle, vol,
        *(side if wide else []), us=5.8,
    )
    output = output.reshape(ch, planes, flat)
    send = blocks(own, whole, blk, near_steps, (taps_grad,))
    got.update((s, swap(block, "filter", s)) for s, block in zip(near_steps, send))
    base = mg[0] if wide else dict(zip([0, 1], side))
    rest = cross + near_steps
    mg_all, mine, theirs = weight_products(
        base, some(got, rest), rest, vol_t, taps_grad, ch, norm, ns
    )
    back = unmix(turn, mg_all, held, other, ch)
    got = exchange(back, "filter")
    volume_grad_1 = finish(own, up, None, some(got, [0, 1]), [0, 1])
    volume_grad_2 = finish(own, up, volume_grad_1, some(got, cross), cross)
    mixing_grad, taps_grad = scatter_rest(
        mine, theirs, taps_grad, ch, volume_grad_1, volume_grad_2
    )
    volume_grad = finish(own, up, volume_grad_2, some(got, near_steps), near_steps)
    volume_grad = volume_grad.reshape(ch, planes, flat)
    return (output, volume_grad, mixing_grad, taps_grad[:27].T)


def solution(mesh):
    in_specs = (
        P("filter", "space", None),
        P("filter", None),
        P("filter", None),
        P("filter", "space", None),
    )
    out_specs = (
        P("filter", "space", None),
        P("filter", "space", None),
        P("filter", "space"),
        P("filter", None),
    )
    return jax.shard_map(body, mesh=mesh, in_specs=in_specs, out_specs=out_specs, check_vma=False)
```
